32 devices in a mesh: seq: 8 (over z, y), ch: 4 (over x, core).
Axes of the slice: x: 2, y: 2, z: 4, core: 2. Of those that a mesh axis runs over, the one named last changes fastest.
Arguments:
- inputs: bfloat16 [256, 2048], P('ch', 'seq'), may hold values from -6 to 6
- gate_values: bfloat16 [256, 2048], P('ch', 'seq'), may hold values from -6 to 6
- probe_values: bfloat16 [256, 2048], P('ch', 'seq'), may hold values from -6 to 6
- filter_taps: float32 [256, 2048], P('ch', 'seq'), may hold values from -0.125 to 0.125
- member_blocks: int32 [64], P('seq'), may hold values from 0 to 31, as said below
- member_nodes: int32 [64], P('seq'), may hold values from 0 to 8191
- node_place: int32 [8192], replicated, may hold values from 0 to 8191, each once
Outputs:
- position_saliency: float32 [2048], P('seq')
- node_rows: float32 [256, 8192], P('ch', 'seq')
The draws below stay inside these ranges and needn't reach their ends.
Inputs may be any that keep to these rules, and one draw needn't show every extreme that they name: `member_blocks`: in the g-th aligned group of 8 entries every value lies in g * 4 to (g + 1) * 4 - 1, and each of these values appears in that group at least once. `node_place`: each node appears exactly once.
All inputs are finite; a program needn't handle non-finite values.
Results may differ from the reference program's by a relative error of at most 0.0003.
Values may be sent and summed in bfloat16 or wider, within the bound.
No kernel may reach another device: no remote copies, remote signals or barrier semaphores. Data moves between devices by JAX's collectives and lax.ppermute only.
A program may use at most 64 MiB of HBM per device.

```python
import math
import jax
import jax.numpy as jnp
import numpy as np
from jax import lax

BLOCK = 64
NODES = 8192
SEQ = 2048
CH = 256
BLK_DEV = 4
BLOCKS = 32
MEMB_DEV = 8
MEMBERS = 64


def draw_member_blocks(key, part):
    devices = MEMBERS // MEMB_DEV

    def one_device(device_key, device):
        shuffled = jax.random.permutation(jax.random.fold_in(device_key, 1), BLK_DEV).astype(jnp.int32)
        extra_ids = jax.random.randint(jax.random.fold_in(device_key, 2), (MEMB_DEV - BLK_DEV,), 0, BLK_DEV, dtype=jnp.int32)
        return jnp.concatenate([shuffled, extra_ids]) + device * BLK_DEV
    device_keys = jax.random.split(jax.random.fold_in(key, 7), devices)
    result = jax.vmap(one_device)(device_keys, jnp.arange(devices, dtype=jnp.int32))
    return result.reshape(MEMBERS).astype(jnp.int32)


def place_ends(values, own_key, low, largest):
    place = [jax.random.randint(jax.random.fold_in(own_key, axis), (), 0, length) for axis, length in enumerate(values.shape)]
    longest = values.shape.index(max(values.shape))
    neighbour = place[:longest] + [(place[longest] + 1) % values.shape[longest]] + place[longest + 1:]
    return values.at[tuple(place)].set(low).at[tuple(neighbour)].set(largest)


def steps_of(rng, extent, pieces, smallest, largest):
    def one(position, shards_of):
        draws = jax.random.uniform(jax.random.fold_in(jax.random.fold_in(rng, 6), position), (shards_of,), jnp.float32, smallest / len(pieces), largest / len(pieces))
        return jnp.repeat(jnp.exp(draws), extent[position] // shards_of).reshape((-1,) + (1,) * (len(extent) - position - 1))

    level = one(*pieces[0])
    for cut in pieces[1:]:
        level = level * one(*cut)
    return level


def cumulative_ranks(amount, skew):
    loads = [(1 << 20) // math.isqrt(standing ** skew) + 1 for standing in range(1, amount + 1)]
    scale = 1 + sum(loads) // (1 << 30)
    return np.cumsum(np.array([max(1, weight // scale) for weight in loads]))


def ranked(own_key, extent, number_of, lean):
    listing = cumulative_ranks(number_of, lean)
    ticket = jax.random.randint(jax.random.fold_in(own_key, 1), extent, 0, int(listing[number_of - 1]))
    rank = jnp.searchsorted(jnp.asarray(listing, jnp.int32), ticket, side="right")
    return jax.random.permutation(jax.random.fold_in(own_key, 2), number_of)[rank].astype(jnp.int32)


def noise(stream_key, shape, scale, limit, cuts=(), kind=jnp.bfloat16):
    array = scale * jax.random.normal(stream_key, shape, jnp.float32)
    if cuts:
        array = array * steps_of(stream_key, shape, cuts, -0.22, 0.18)
    return jnp.clip(array, -limit, limit).astype(kind)


def setup_inputs(seed: int = 0) -> dict:
    keys = jax.random.split(jax.random.key(seed), 8)
    inputs = noise(keys[0], (CH, SEQ), 1.0, 6.0, ((0, 4), (1, 8)))
    gate_values = noise(keys[1], (CH, SEQ), 1.0, 6.0, ((0, 4), (1, 8)))
    probe_values = noise(keys[2], (CH, SEQ), 1.0, 6.0, ((0, 4), (1, 8)))
    filter_taps = noise(keys[3], (CH, SEQ), SEQ ** -0.5, 0.125, ((0, 4), (1, 8)), jnp.float32)
    member_blocks = draw_member_blocks(jax.random.fold_in(keys[7], 71), 0)
    member_nodes = place_ends(ranked(keys[5], (MEMBERS,), NODES, 1), jax.random.fold_in(keys[5], 3), 0, NODES - 1).astype(jnp.int32)
    node_place = jax.random.permutation(keys[6], NODES).astype(jnp.int32)
    return {"inputs": inputs, "gate_values": gate_values, "probe_values": probe_values, "filter_taps": filter_taps, "member_blocks": member_blocks, "member_nodes": member_nodes, "node_place": node_place}


def causal_block(stacked):
    signal_rows, taps_rows, gating, probing = stacked
    length = signal_rows.shape[1]
    padded = 2 * length
    taps_spec = jnp.fft.rfft(taps_rows, n=padded, axis=1)
    conv = jnp.fft.irfft(jnp.fft.rfft(signal_rows, n=padded, axis=1) * taps_spec, n=padded, axis=1)[:, :length]
    mixed = gating * conv
    sigmoid_val = jax.nn.sigmoid(mixed)
    back = gating * probing * sigmoid_val * (1.0 + mixed * (1.0 - sigmoid_val))
    grad = jnp.fft.irfft(jnp.fft.rfft(back, n=padded, axis=1) * jnp.conj(taps_spec), n=padded, axis=1)[:, :length]
    return grad * signal_rows


def reference(inputs, gate_values, probe_values, filter_taps, member_blocks, member_nodes, node_place):
    channels = inputs.shape[0]
    group_size = 4

    def regroup(values):
        return values.astype(jnp.float32).reshape(channels // group_size, group_size, SEQ)

    saliency = lax.map(causal_block, (regroup(inputs), regroup(filter_taps), regroup(gate_values), regroup(probe_values)))
    saliency = saliency.reshape(channels, SEQ)
    position_saliency = jnp.sum(saliency, axis=0) / channels
    block_rows = jnp.sum(saliency.reshape(channels, BLOCKS, BLOCK), axis=2)
    targets = node_place[member_nodes]
    member_rows = jnp.take(block_rows, member_blocks, axis=1)
    node_sums = jax.ops.segment_sum(member_rows.T, targets, num_segments=NODES).T
    node_counts = jax.ops.segment_sum(jnp.ones(member_blocks.shape, jnp.float32), targets, num_segments=NODES)
    node_rows = node_sums / jnp.maximum(node_counts, 1.0)[None, :]
    return position_saliency, node_rows
```

```python
import functools
import math

import jax
import jax.numpy as jnp
from jax import lax
from jax.experimental import pallas as pl
from jax.experimental.pallas import tpu as pltpu
from jax.sharding import PartitionSpec as P

BLOCK = 64
NODES = 8192
LANES = 128
SUBS = 8
HALF = LANES // 2
FIELD_ROWS = 16
FIELDS = 5
MEMBER_ROW = FIELDS * FIELD_ROWS
PACK_ROWS = MEMBER_ROW + FIELD_ROWS


HIGHEST = lax.Precision.HIGHEST


def iota(shape, dim):
    return lax.broadcasted_iota(jnp.int32, shape, dim)


def halves(vals):
    high = vals.astype(jnp.bfloat16)
    return high, (vals - high.astype(jnp.float32)).astype(jnp.bfloat16)


def pack_kernel(
    blocks_dev, inputs_ref, gate_ref, probe_ref, taps_ref, blocks_ref, nodes_ref, packed_ref
):
    devices = packed_ref.shape[0]

    def put(pair, field, tiles):
        for side in range(2):
            rows = slice(side * SUBS, (side + 1) * SUBS)
            both = jnp.concatenate([tile[rows] for tile in tiles], axis=0)
            place = slice(field * FIELD_ROWS, (field + 1) * FIELD_ROWS)
            packed_ref[2 * pair + side, place, :] = both.astype(jnp.bfloat16)

    for pair in range(devices // 2):
        rows = slice(pair * 2 * SUBS, (pair + 1) * 2 * SUBS)
        columns = [slice(0, LANES), slice(LANES, 2 * LANES)]
        for field, ref in enumerate((inputs_ref, gate_ref, probe_ref)):
            put(pair, field, [ref[rows, cols].astype(jnp.float32) for cols in columns])
        split = [halves(taps_ref[rows, cols]) for cols in columns]
        for term in range(2):
            put(pair, 3 + term, [terms[term].astype(jnp.float32) for terms in split])

    def as_column(row):
        members = row.shape[1]
        same = iota((members, members), 0) == iota((members, members), 1)
        return jnp.sum(jnp.where(same, row, 0).astype(jnp.float32), axis=1, keepdims=True)

    nodes = nodes_ref[...]
    low_lanes = iota((SUBS, LANES), 1) < HALF
    digits = jnp.where(low_lanes, as_column(nodes // LANES), as_column(nodes % LANES))
    places = jnp.broadcast_to(as_column(blocks_ref[...] % blocks_dev), (SUBS, LANES))
    member_rows = jnp.concatenate([digits, places], axis=0).astype(jnp.bfloat16)
    for device in range(devices):
        packed_ref[device, MEMBER_ROW:, :] = member_rows


def half_turn(vals):
    return pltpu.roll(vals, HALF, axis=1)


def saliency_kernel(packed_ref, sums_ref, fields, taps, padded, products):
    devices = packed_ref.shape[0]
    blocks = 2 * devices
    copies = sums_ref.shape[0] // devices
    low_lanes = iota((SUBS, LANES), 1) < HALF
    row_ids = iota((SUBS, LANES), 0)
    below = iota((HALF, LANES), 1) < iota((HALF, LANES), 0)
    for source in range(devices):
        rows = slice(source * SUBS, (source + 1) * SUBS)
        for field in range(3):
            place = slice(field * FIELD_ROWS, (field + 1) * FIELD_ROWS)
            both = packed_ref[source, place, :].astype(jnp.float32)
            fields[field, 0, rows, :] = both[:SUBS]
            fields[field, 1, rows, :] = both[SUBS:]
        high, low = (
            packed_ref[source, (3 + term) * FIELD_ROWS : (4 + term) * FIELD_ROWS, :].astype(
                jnp.float32
            )
            for term in range(2)
        )
        taps[source * FIELD_ROWS : (source + 1) * FIELD_ROWS, :] = high + low
    zeros = jnp.zeros((SUBS, LANES), jnp.float32)
    for channel in range(SUBS):
        for kind in range(4):
            padded[channel, kind, :SUBS, :] = zeros
            padded[channel, 4 + kind, SUBS:, :] = zeros
    position_sums = [zeros, zeros]
    for channel in range(SUBS):
        strided = pl.ds(channel, devices, stride=SUBS)
        signal, gating, probing = (
            [fields[field, side, strided, :] for side in range(2)] for field in range(3)
        )
        windows_high, windows_low = [], []
        earlier = jnp.zeros((HALF, LANES), jnp.float32)
        for block in range(blocks):
            row = taps[pl.ds(block * SUBS + channel, 1), :]
            turned = pltpu.roll(
                jnp.broadcast_to(row, (HALF, LANES)), 0, axis=1, stride=1, stride_axis=0
            )
            high, low = halves(jnp.where(below, earlier, turned))
            windows_high.append(high)
            windows_low.append(low)
            earlier = turned
        turned = [half_turn(vals) for vals in signal]
        later = pltpu.roll(signal[1], 1, axis=0)
        later_turned = pltpu.roll(turned[1], 1, axis=0)
        later = jnp.where(row_ids == 0, 0.0, later)
        later_turned = jnp.where(row_ids == 0, 0.0, later_turned)
        kinds = (
            jnp.where(low_lanes, signal[0], later_turned),
            jnp.where(low_lanes, signal[1], turned[0]),
            jnp.where(low_lanes, turned[0], later),
            jnp.where(low_lanes, turned[1], signal[0]),
        )
        for kind in range(4):
            padded[channel, kind, SUBS:, :] = kinds[kind]
        left = jnp.concatenate(
            [
                jnp.concatenate(
                    [padded[channel, kind, SUBS - step : 2 * SUBS - step, :] for kind in range(4)],
                    axis=0,
                )
                for step in range(devices)
            ],
            axis=1,
        ).astype(jnp.bfloat16)
        right = jnp.concatenate(
            [
                jnp.concatenate([high, low], axis=1)
                for high, low in zip(windows_high, windows_low)
            ],
            axis=0,
        )
        parts = jnp.dot(left, right, preferred_element_type=jnp.float32)
        parts = parts[:, :LANES] + parts[:, LANES:]
        even, odd = (
            [parts[(2 * which + side) * SUBS : (2 * which + side + 1) * SUBS] for side in range(2)]
            for which in range(2)
        )
        odd_before = jnp.where(row_ids == 0, 0.0, pltpu.roll(odd[1], 1, axis=0))
        conv = (
            even[0] + half_turn(jnp.where(low_lanes, odd[0], odd_before)),
            even[1] + half_turn(jnp.where(low_lanes, odd[1], odd[0])),
        )
        back = []
        for side in range(2):
            mixed = gating[side] * conv[side]
            sigmoid_val = jax.nn.sigmoid(mixed)
            back.append(
                gating[side] * probing[side] * sigmoid_val * (1.0 + mixed * (1.0 - sigmoid_val))
            )
        next_row = jnp.where(row_ids == SUBS - 1, 0.0, pltpu.roll(back[0], SUBS - 1, axis=0))
        shifted = (
            half_turn(jnp.where(low_lanes, back[1], back[0])),
            half_turn(jnp.where(low_lanes, next_row, back[1])),
        )
        for kind, vals in enumerate((*back, *shifted)):
            padded[channel, 4 + kind, :SUBS, :] = vals

        def reach(kind, step):
            return padded[channel, 4 + kind, step : SUBS + step, :]

        pieces = []
        for block in range(blocks):
            step, odd_block = divmod(block, 2)
            if odd_block:
                group = (reach(1, step), reach(0, step + 1), reach(3, step), reach(2, step + 1))
            else:
                group = (reach(0, step), reach(1, step), reach(2, step), reach(3, step))
            pieces.append(jnp.concatenate(halves(jnp.concatenate(group, axis=0)), axis=0))
        left = jnp.concatenate(pieces, axis=1)
        right = jnp.concatenate(
            [jnp.concatenate(windows_high, axis=1), jnp.concatenate(windows_low, axis=1)], axis=0
        )
        parts = lax.dot_general(
            left, right, (((1,), (1,)), ((), ())), preferred_element_type=jnp.float32
        )
        parts = parts[: 4 * SUBS] + parts[4 * SUBS :]
        parts = parts + half_turn(parts)
        for side in range(2):
            grad = jnp.where(
                low_lanes,
                parts[side * SUBS : (side + 1) * SUBS],
                parts[(2 + side) * SUBS : (3 + side) * SUBS],
            )
            saliency = grad * signal[side]
            position_sums[side] += saliency
            place = (channel * 2 + side) * SUBS
            products[place : place + SUBS, :] = saliency
    pick = (iota((SUBS, LANES), 1) // BLOCK == iota((SUBS, LANES), 0)).astype(jnp.bfloat16)
    block_sums = sum(
        lax.dot_general(
            pick, term, (((1,), (1,)), ((), ())), preferred_element_type=jnp.float32
        )
        for term in halves(products[...])
    )
    for device in range(devices):
        rows = [vals[device : device + 1] for vals in position_sums] + [block_sums[:2]]
        message = jnp.concatenate(rows, axis=0)
        for copy in range(copies):
            sums_ref[device * copies + copy, :, :] = message


def weight_kernel(packed_ref, place_ref, weight_ref, scale_ref):
    devices = packed_ref.shape[0]
    members = devices * SUBS
    columns = weight_ref.shape[1]
    blocks_dev = 2 * LANES // BLOCK
    digits, offsets = [], []
    for source in range(devices):
        both = packed_ref[source, MEMBER_ROW:, :].astype(jnp.float32)
        digits.append(both[:SUBS])
        offsets.append(both[SUBS:] + float(source * blocks_dev))
    digits = jnp.concatenate(digits, axis=0)
    offsets = jnp.concatenate(offsets, axis=0)
    place = place_ref[...]
    place_rows = place.shape[0]
    row_pick = iota((members, place_rows), 1).astype(jnp.float32) == digits[:, :1]
    row_pick = row_pick.astype(jnp.bfloat16)
    lane_ids = iota((members, LANES), 1).astype(jnp.float32)
    low_digit = jnp.broadcast_to(digits[:, HALF : HALF + 1], (members, LANES))

    def looked_up(table):
        found = jnp.dot(
            row_pick, table.astype(jnp.float32).astype(jnp.bfloat16),
            preferred_element_type=jnp.float32,
        )
        return jnp.sum(jnp.where(lane_ids == low_digit, found, 0.0), axis=1, keepdims=True)

    targets = looked_up(place // LANES) * LANES + looked_up(place % LANES)
    targets = targets - (lax.axis_index("seq") * columns).astype(jnp.float32)
    node_pick = iota((members, columns), 1).astype(jnp.float32) == targets
    node_pick = node_pick.astype(jnp.float32)
    counts = jnp.sum(node_pick, axis=0, keepdims=True)
    scale_ref[...] = 1.0 / jnp.maximum(counts, 1.0)
    slot = iota((members, 2 * LANES), 1)
    inner = slot % LANES % (2 * SUBS)
    slot_block = (inner % SUBS) * 4 + (inner // SUBS) * 2 + slot // LANES
    own_block = jnp.broadcast_to(offsets[:, :1], (members, 2 * LANES))
    block_pick = (slot_block.astype(jnp.float32) == own_block).astype(jnp.float32)
    weight_ref[...] = lax.dot_general(
        block_pick.T.astype(jnp.bfloat16),
        node_pick.astype(jnp.bfloat16),
        (((1,), (0,)), ((), ())),
        preferred_element_type=jnp.float32,
    ).astype(jnp.bfloat16)


def finish_kernel(channel_count, sums_ref, weight_ref, scale_ref, position_ref, nodes_ref):
    copies = lax.axis_size("ch")
    devices = sums_ref.shape[0] // copies
    own = lax.axis_index("ch")
    total = sums_ref[0]
    for source in range(1, devices * copies):
        total = total + sums_ref[source]
    position_ref[...] = total[:2] / channel_count
    own_lanes = iota((SUBS, LANES), 1) // (2 * SUBS) == iota((SUBS, LANES), 0)
    rows = []
    for source in range(devices):
        message = sums_ref[source * copies + own]
        rows.append(
            jnp.concatenate(
                [jnp.where(own_lanes, message[2 + side : 3 + side], 0.0) for side in range(2)],
                axis=1,
            )
        )
    high, low = halves(jnp.concatenate(rows, axis=0))
    both = jnp.dot(
        jnp.concatenate([high, low], axis=0), weight_ref[...], preferred_element_type=jnp.float32
    )
    count = high.shape[0]
    nodes_ref[...] = (both[:count] + both[count:]) * scale_ref[...]


def whole_channels(
    inputs, gate_values, probe_values, filter_taps, member_blocks, member_nodes, node_place
):
    devices = lax.axis_size("seq")
    copies = lax.axis_size("ch")
    channels, length = inputs.shape
    columns = node_place.shape[0] // devices
    packed = pl.pallas_call(
        functools.partial(pack_kernel, length // BLOCK),
        out_shape=jax.ShapeDtypeStruct((devices, PACK_ROWS, LANES), jnp.bfloat16),
        name="pack",
    )(
        inputs,
        gate_values,
        probe_values,
        filter_taps,
        member_blocks.reshape(1, -1),
        member_nodes.reshape(1, -1),
    )
    packed = lax.all_to_all(packed, "seq", split_axis=0, concat_axis=0, tiled=True)
    sums = pl.pallas_call(
        saliency_kernel,
        out_shape=jax.ShapeDtypeStruct((devices * copies, 4, LANES), jnp.float32),
        scratch_shapes=[
            pltpu.VMEM((3, 2, devices * SUBS, LANES), jnp.float32),
            pltpu.VMEM((devices * FIELD_ROWS, LANES), jnp.float32),
            pltpu.VMEM((SUBS, 8, 2 * SUBS, LANES), jnp.float32),
            pltpu.VMEM((2 * SUBS * SUBS, LANES), jnp.float32),
        ],
        name="saliency",
    )(packed)
    sums = lax.all_to_all(sums, ("seq", "ch"), split_axis=0, concat_axis=0, tiled=True)
    weight, scale = pl.pallas_call(
        weight_kernel,
        out_shape=(
            jax.ShapeDtypeStruct((2 * LANES, columns), jnp.bfloat16),
            jax.ShapeDtypeStruct((1, columns), jnp.float32),
        ),
        name="weights",
    )(packed, node_place.reshape(-1, LANES))
    position, node_rows = pl.pallas_call(
        functools.partial(finish_kernel, channels * copies),
        out_shape=(
            jax.ShapeDtypeStruct((2, LANES), jnp.float32),
            jax.ShapeDtypeStruct((channels, columns), jnp.float32),
        ),
        name="finish",
    )(sums, weight, scale)
    return position.reshape(length), node_rows


def phase_table(rows_count, cols_count, modulus, sine_sign, row_start, col_start):
    row_ids = lax.broadcasted_iota(jnp.int32, (rows_count, cols_count), 0) + row_start
    col_ids = lax.broadcasted_iota(jnp.int32, (rows_count, cols_count), 1) + col_start
    angles = (row_ids * col_ids % modulus).astype(jnp.float32) * (2.0 * math.pi / modulus)
    return (jnp.cos(angles), sine_sign * jnp.sin(angles))


def complex_times(first_pair, second_pair):
    first_real, first_imag = first_pair
    second_real, second_imag = second_pair
    return (
        first_real * second_real - first_imag * second_imag,
        first_real * second_imag + first_imag * second_real,
    )


def complex_product(formula, first_pair, second_pair):
    first_real, first_imag = first_pair
    second_real, second_imag = second_pair
    real_part = jnp.einsum(formula, first_real, second_real, precision=HIGHEST) - jnp.einsum(
        formula, first_imag, second_imag, precision=HIGHEST
    )
    imag_part = jnp.einsum(formula, first_real, second_imag, precision=HIGHEST) + jnp.einsum(
        formula, first_imag, second_real, precision=HIGHEST
    )
    return (real_part, imag_part)


def split_sizes(length):
    return (length // 128, 128)


def local_forward(real_part, imag_part):
    stacks, rows_count, channels, length = real_part.shape
    outer_size, inner_size = split_sizes(length)
    data_pair = (
        real_part.reshape(-1, outer_size, inner_size),
        imag_part.reshape(-1, outer_size, inner_size),
    )
    part_pair = complex_product(
        "jn,rnm->rjm", phase_table(outer_size, outer_size, outer_size, -1.0, 0, 0), data_pair
    )
    part_pair = complex_times(part_pair, phase_table(outer_size, inner_size, length, -1.0, 0, 0))
    spec_real, spec_imag = complex_product(
        "rjn,nm->rjm", part_pair, phase_table(inner_size, inner_size, inner_size, -1.0, 0, 0)
    )
    new_shape = (stacks, rows_count * channels, outer_size, inner_size)
    return (spec_real.reshape(new_shape), spec_imag.reshape(new_shape))


def local_inverse(spec_real, spec_imag):
    stacks, rows_count, outer_size, inner_size = spec_real.shape
    length = outer_size * inner_size
    data_pair = (
        spec_real.reshape(-1, outer_size, inner_size),
        spec_imag.reshape(-1, outer_size, inner_size),
    )
    part_pair = complex_product(
        "rjn,nm->rjm", data_pair, phase_table(inner_size, inner_size, inner_size, 1.0, 0, 0)
    )
    part_pair = complex_times(part_pair, phase_table(outer_size, inner_size, length, 1.0, 0, 0))
    out_real, out_imag = complex_product(
        "jn,rnm->rjm", phase_table(outer_size, outer_size, outer_size, 1.0, 0, 0), part_pair
    )
    return (
        out_real.reshape(stacks, rows_count, length),
        out_imag.reshape(stacks, rows_count, length),
    )


def spectrum_full(columns, seq_index, send):
    stacks, devices, channels, col_width = columns.shape
    modulus = 2 * devices * devices * col_width
    flattened = columns.reshape(stacks, devices, channels * col_width)
    row_cos, row_sin = phase_table(2 * devices, devices, 2 * devices, -1.0, 0, 0)
    grid_shape = (stacks, 2 * devices, channels, col_width)
    real_part = jnp.einsum("kn,snm->skm", row_cos, flattened, precision=HIGHEST).reshape(grid_shape)
    imag_part = jnp.einsum("kn,snm->skm", row_sin, flattened, precision=HIGHEST).reshape(grid_shape)
    turn_cos, turn_sin = phase_table(
        2 * devices, col_width, modulus, -1.0, 0, seq_index * col_width
    )
    real_part, imag_part = complex_times(
        (real_part, imag_part), (turn_cos[:, None, :], turn_sin[:, None, :])
    )
    real_part, imag_part = send(real_part, imag_part)
    return local_forward(real_part, imag_part)


def signal_full(spec_real, spec_imag, seq_index, devices, send):
    real_part, imag_part = local_inverse(spec_real, spec_imag)
    stacks, rows_count, length = real_part.shape
    channels = rows_count // 2
    modulus = 2 * devices * length
    real_part = real_part.reshape(stacks, 2, channels, length)
    imag_part = imag_part.reshape(stacks, 2, channels, length)
    turn_cos, turn_sin = phase_table(2, length, modulus, 1.0, 2 * seq_index, 0)
    real_part, imag_part = complex_times(
        (real_part, imag_part), (turn_cos[:, None, :], turn_sin[:, None, :])
    )
    real_part, imag_part = send(real_part, imag_part)
    col_width = length // devices
    back_cos, back_sin = phase_table(devices, 2 * devices, 2 * devices, 1.0, 0, 0)
    flat_real = real_part.reshape(stacks, 2 * devices, channels * col_width)
    flat_imag = imag_part.reshape(stacks, 2 * devices, channels * col_width)
    signal_vals = (
        jnp.einsum("ak,skm->sam", back_cos, flat_real, precision=HIGHEST)
        - jnp.einsum("ak,skm->sam", back_sin, flat_imag, precision=HIGHEST)
    ) / modulus
    return signal_vals.reshape(stacks, devices, channels, col_width)


def cotangent(conv_vals, gating, probing):
    gate_wide = gating.astype(jnp.float32)
    mixed = gate_wide * conv_vals
    sigmoid_val = jax.nn.sigmoid(mixed)
    return (
        gate_wide * probing.astype(jnp.float32) * sigmoid_val * (1.0 + mixed * (1.0 - sigmoid_val))
    )


def spread_channels(
    inputs, gate_values, probe_values, filter_taps, member_blocks, member_nodes, node_place
):
    seq_index = lax.axis_index("seq")
    devices = lax.axis_size("seq")
    channels, length = inputs.shape
    inputs_wide = inputs.astype(jnp.float32)
    stacked = jnp.stack([inputs_wide, filter_taps]).reshape(2, 1, channels, length)
    columns_pair = lax.all_to_all(stacked, "seq", split_axis=3, concat_axis=1, tiled=True)

    def send_input(real_part, imag_part):
        return (
            lax.all_to_all(real_part, "seq", split_axis=1, concat_axis=3, tiled=True),
            lax.all_to_all(imag_part, "seq", split_axis=1, concat_axis=3, tiled=True),
        )

    def send_output(real_part, imag_part):
        return (
            lax.all_to_all(real_part, "seq", split_axis=3, concat_axis=1, tiled=True),
            lax.all_to_all(imag_part, "seq", split_axis=3, concat_axis=1, tiled=True),
        )

    def send_cotangent(real_part, imag_part):
        return (
            lax.all_to_all(real_part, "seq", split_axis=1, concat_axis=3, tiled=True),
            lax.all_to_all(imag_part, "seq", split_axis=1, concat_axis=3, tiled=True),
        )

    def send_gradient(real_part, imag_part):
        return (
            lax.all_to_all(real_part, "seq", split_axis=3, concat_axis=1, tiled=True),
            lax.all_to_all(imag_part, "seq", split_axis=3, concat_axis=1, tiled=True),
        )

    forward_section, inverse_section = (spectrum_full, signal_full)
    spec_real, spec_imag = forward_section(columns_pair, seq_index, send_input)
    filter_pair = (spec_real[1], spec_imag[1])
    conv_real, conv_imag = complex_times((spec_real[0], spec_imag[0]), filter_pair)
    conv_cols = inverse_section(conv_real[None], conv_imag[None], seq_index, devices, send_output)
    conv_rows = lax.all_to_all(conv_cols, "seq", split_axis=1, concat_axis=3, tiled=True).reshape(
        channels, length
    )
    back_rows = cotangent(conv_rows, gate_values, probe_values)
    back_cols = lax.all_to_all(
        back_rows.reshape(1, 1, channels, length), "seq", split_axis=3, concat_axis=1, tiled=True
    )
    back_real, back_imag = forward_section(back_cols, seq_index, send_cotangent)
    grad_real = back_real[0] * filter_pair[0] + back_imag[0] * filter_pair[1]
    grad_imag = back_imag[0] * filter_pair[0] - back_real[0] * filter_pair[1]
    grad_cols = inverse_section(grad_real[None], grad_imag[None], seq_index, devices, send_gradient)
    returned = lax.all_to_all(grad_cols, "seq", split_axis=1, concat_axis=3, tiled=True).reshape(
        channels, length
    )
    saliency = returned * inputs_wide
    channel_count = channels * lax.axis_size("ch")
    position_saliency = lax.psum(jnp.sum(saliency, axis=0), "ch") / channel_count
    blocks_dev = length // BLOCK
    block_rows = jnp.sum(saliency.reshape(channels, blocks_dev, BLOCK), axis=2)
    local_blocks = member_blocks - seq_index * blocks_dev
    targets = node_place[member_nodes]
    member_rows = jnp.take(block_rows, local_blocks, axis=1)
    nodes_dev = NODES // devices
    gathered_rows, gathered_targets = (
        lax.all_gather(member_rows, "seq", axis=1, tiled=True),
        lax.all_gather(targets.astype(jnp.float32), "seq", axis=0, tiled=True),
    )
    owned_ids = gathered_targets.astype(jnp.int32) - seq_index * nodes_dev
    slot_ids = jnp.where((owned_ids >= 0) & (owned_ids < nodes_dev), owned_ids, nodes_dev)
    node_sums = jax.ops.segment_sum(gathered_rows.T, slot_ids, num_segments=nodes_dev + 1)[
        :nodes_dev
    ].T
    node_counts = jax.ops.segment_sum(
        jnp.ones(slot_ids.shape, jnp.float32), slot_ids, num_segments=nodes_dev + 1
    )[:nodes_dev]
    node_rows = node_sums / jnp.maximum(node_counts, 1.0)[None, :]
    return (position_saliency, node_rows)


def per_device(*args):
    channels, length = args[0].shape
    devices = lax.axis_size("seq")
    members = args[4].shape[0]
    fits = channels == SUBS * devices and devices == SUBS and length == 2 * LANES
    if fits and members == SUBS and NODES % (devices * LANES) == 0:
        return whole_channels(*args)
    return spread_channels(*args)


def solution(mesh):
    placed = (
        P("ch", "seq"),
        P("ch", "seq"),
        P("ch", "seq"),
        P("ch", "seq"),
        P("seq"),
        P("seq"),
        P(),
    )
    return jax.shard_map(
        per_device,
        mesh=mesh,
        in_specs=placed,
        out_specs=(P("seq"), P("ch", "seq")),
        check_vma=False,
    )
```

```python
import functools
import math

import jax
import jax.numpy as jnp
from jax import lax
from jax.experimental import pallas as pl
from jax.experimental.pallas import tpu as pltpu
from jax.sharding import PartitionSpec as P

BLOCK = 64
NODES = 8192
LANES = 128
SUBS = 8
HALF = LANES // 2
FIELD_ROWS = 16
FIELDS = 5
MEMBER_ROW = FIELDS * FIELD_ROWS
PACK_ROWS = MEMBER_ROW + FIELD_ROWS


HIGHEST = lax.Precision.HIGHEST
LEAN = pltpu.CompilerParams(vmem_limit_bytes=16 * 1024 * 1024)


def iota(shape, dim):
    return lax.broadcasted_iota(jnp.int32, shape, dim)


def halves(vals):
    high = vals.astype(jnp.bfloat16)
    return high, (vals - high.astype(jnp.float32)).astype(jnp.bfloat16)


def pack_kernel(blocks_dev, *refs):
    sources, packed_ref, arrived, landed = refs[:6], refs[6], refs[7:13], refs[13]
    inputs_ref, gate_ref, probe_ref, taps_ref, blocks_ref, nodes_ref = arrived
    devices = packed_ref.shape[0]
    loads = [
        pltpu.make_async_copy(source, target, landed.at[place])
        for place, (source, target) in enumerate(zip(sources, arrived))
    ]
    for load in loads:
        load.start()
    for load in loads:
        load.wait()

    def put(pair, field, tiles):
        for side in range(2):
            rows = slice(side * SUBS, (side + 1) * SUBS)
            both = jnp.concatenate([tile[rows] for tile in tiles], axis=0)
            place = slice(field * FIELD_ROWS, (field + 1) * FIELD_ROWS)
            packed_ref[2 * pair + side, place, :] = both.astype(jnp.bfloat16)

    for pair in range(devices // 2):
        rows = slice(pair * 2 * SUBS, (pair + 1) * 2 * SUBS)
        columns = [slice(0, LANES), slice(LANES, 2 * LANES)]
        for field, ref in enumerate((inputs_ref, gate_ref, probe_ref)):
            put(pair, field, [ref[rows, cols].astype(jnp.float32) for cols in columns])
        split = [halves(taps_ref[rows, cols]) for cols in columns]
        for term in range(2):
            put(pair, 3 + term, [terms[term].astype(jnp.float32) for terms in split])

    def as_column(row):
        members = row.shape[1]
        same = iota((members, members), 0) == iota((members, members), 1)
        return jnp.sum(jnp.where(same, row, 0).astype(jnp.float32), axis=1, keepdims=True)

    nodes = nodes_ref[...]
    low_lanes = iota((SUBS, LANES), 1) < HALF
    digits = jnp.where(low_lanes, as_column(nodes // LANES), as_column(nodes % LANES))
    places = jnp.broadcast_to(as_column(blocks_ref[...] % blocks_dev), (SUBS, LANES))
    member_rows = jnp.concatenate([digits, places], axis=0).astype(jnp.bfloat16)
    for device in range(devices):
        packed_ref[device, MEMBER_ROW:, :] = member_rows


def half_turn(vals):
    return pltpu.roll(vals, HALF, axis=1)


def fill_weights(packed_ref, place_ref, weight_ref, scale_ref):
    devices = packed_ref.shape[0]
    members = devices * SUBS
    columns = weight_ref.shape[1]
    blocks_dev = 2 * LANES // BLOCK
    digits, offsets = [], []
    for source in range(devices):
        both = packed_ref[source, MEMBER_ROW:, :].astype(jnp.float32)
        digits.append(both[:SUBS])
        offsets.append(both[SUBS:] + float(source * blocks_dev))
    digits = jnp.concatenate(digits, axis=0)
    offsets = jnp.concatenate(offsets, axis=0)
    place = place_ref[...]
    place_rows = place.shape[0]
    row_pick = iota((members, place_rows), 1).astype(jnp.float32) == digits[:, :1]
    row_pick = row_pick.astype(jnp.bfloat16)
    lane_ids = iota((members, LANES), 1).astype(jnp.float32)
    low_digit = jnp.broadcast_to(digits[:, HALF : HALF + 1], (members, LANES))

    def looked_up(table):
        found = jnp.dot(
            row_pick, table.astype(jnp.float32).astype(jnp.bfloat16),
            preferred_element_type=jnp.float32,
        )
        return jnp.sum(jnp.where(lane_ids == low_digit, found, 0.0), axis=1, keepdims=True)

    targets = looked_up(place // LANES) * LANES + looked_up(place % LANES)
    targets = targets - (lax.axis_index("seq") * columns).astype(jnp.float32)
    node_pick = iota((members, columns), 1).astype(jnp.float32) == targets
    node_pick = node_pick.astype(jnp.float32)
    counts = jnp.sum(node_pick, axis=0, keepdims=True)
    scale_ref[...] = 1.0 / jnp.maximum(counts, 1.0)
    slot = iota((members, 2 * LANES), 1)
    inner = slot % LANES % (2 * SUBS)
    slot_block = (inner % SUBS) * 4 + (inner // SUBS) * 2 + slot // LANES
    own_block = jnp.broadcast_to(offsets[:, :1], (members, 2 * LANES))
    block_pick = (slot_block.astype(jnp.float32) == own_block).astype(jnp.float32)
    weight_ref[...] = lax.dot_general(
        block_pick.T.astype(jnp.bfloat16),
        node_pick.astype(jnp.bfloat16),
        (((1,), (0,)), ((), ())),
        preferred_element_type=jnp.float32,
    ).astype(jnp.bfloat16)


def saliency_kernel(
    packed_ref, place_ref, sums_ref, weight_ref, scale_ref, fields, taps, padded, products
):
    devices = packed_ref.shape[0]
    blocks = 2 * devices
    copies = sums_ref.shape[0] // devices
    low_lanes = iota((SUBS, LANES), 1) < HALF
    row_ids = iota((SUBS, LANES), 0)
    below = iota((HALF, LANES), 1) < iota((HALF, LANES), 0)
    fill_weights(packed_ref, place_ref, weight_ref, scale_ref)
    for source in range(devices):
        rows = slice(source * SUBS, (source + 1) * SUBS)
        for field in range(3):
            place = slice(field * FIELD_ROWS, (field + 1) * FIELD_ROWS)
            both = packed_ref[source, place, :].astype(jnp.float32)
            fields[field, 0, rows, :] = both[:SUBS]
            fields[field, 1, rows, :] = both[SUBS:]
        high, low = (
            packed_ref[source, (3 + term) * FIELD_ROWS : (4 + term) * FIELD_ROWS, :].astype(
                jnp.float32
            )
            for term in range(2)
        )
        taps[source * FIELD_ROWS : (source + 1) * FIELD_ROWS, :] = high + low
    zeros = jnp.zeros((SUBS, LANES), jnp.float32)
    for channel in range(SUBS):
        for kind in range(4):
            padded[channel, kind, :SUBS, :] = zeros
            padded[channel, 4 + kind, SUBS:, :] = zeros
    position_sums = [zeros, zeros]
    for channel in range(SUBS):
        strided = pl.ds(channel, devices, stride=SUBS)
        signal, gating, probing = (
            [fields[field, side, strided, :] for side in range(2)] for field in range(3)
        )
        windows_high, windows_low = [], []
        earlier = jnp.zeros((HALF, LANES), jnp.float32)
        for block in range(blocks):
            row = taps[pl.ds(block * SUBS + channel, 1), :]
            turned = pltpu.roll(
                jnp.broadcast_to(row, (HALF, LANES)), 0, axis=1, stride=1, stride_axis=0
            )
            high, low = halves(jnp.where(below, earlier, turned))
            windows_high.append(high)
            windows_low.append(low)
            earlier = turned
        turned = [half_turn(vals) for vals in signal]
        later = pltpu.roll(signal[1], 1, axis=0)
        later_turned = pltpu.roll(turned[1], 1, axis=0)
        later = jnp.where(row_ids == 0, 0.0, later)
        later_turned = jnp.where(row_ids == 0, 0.0, later_turned)
        kinds = (
            jnp.where(low_lanes, signal[0], later_turned),
            jnp.where(low_lanes, signal[1], turned[0]),
            jnp.where(low_lanes, turned[0], later),
            jnp.where(low_lanes, turned[1], signal[0]),
        )
        for kind in range(4):
            padded[channel, kind, SUBS:, :] = kinds[kind]
        left = jnp.concatenate(
            [
                jnp.concatenate(
                    [padded[channel, kind, SUBS - step : 2 * SUBS - step, :] for kind in range(4)],
                    axis=0,
                )
                for step in range(devices)
            ],
            axis=1,
        ).astype(jnp.bfloat16)
        right = jnp.concatenate(
            [
                jnp.concatenate([high, low], axis=1)
                for high, low in zip(windows_high, windows_low)
            ],
            axis=0,
        )
        parts = jnp.dot(left, right, preferred_element_type=jnp.float32)
        parts = parts[:, :LANES] + parts[:, LANES:]
        even, odd = (
            [parts[(2 * which + side) * SUBS : (2 * which + side + 1) * SUBS] for side in range(2)]
            for which in range(2)
        )
        odd_before = jnp.where(row_ids == 0, 0.0, pltpu.roll(odd[1], 1, axis=0))
        conv = (
            even[0] + half_turn(jnp.where(low_lanes, odd[0], odd_before)),
            even[1] + half_turn(jnp.where(low_lanes, odd[1], odd[0])),
        )
        back = []
        for side in range(2):
            mixed = gating[side] * conv[side]
            sigmoid_val = jax.nn.sigmoid(mixed)
            back.append(
                gating[side] * probing[side] * sigmoid_val * (1.0 + mixed * (1.0 - sigmoid_val))
            )
        next_row = jnp.where(row_ids == SUBS - 1, 0.0, pltpu.roll(back[0], SUBS - 1, axis=0))
        shifted = (
            half_turn(jnp.where(low_lanes, back[1], back[0])),
            half_turn(jnp.where(low_lanes, next_row, back[1])),
        )
        for kind, vals in enumerate((*back, *shifted)):
            padded[channel, 4 + kind, :SUBS, :] = vals

        def reach(kind, step):
            return padded[channel, 4 + kind, step : SUBS + step, :]

        pieces = []
        for block in range(blocks):
            step, odd_block = divmod(block, 2)
            if odd_block:
                group = (reach(1, step), reach(0, step + 1), reach(3, step), reach(2, step + 1))
            else:
                group = (reach(0, step), reach(1, step), reach(2, step), reach(3, step))
            pieces.append(jnp.concatenate(halves(jnp.concatenate(group, axis=0)), axis=0))
        left = jnp.concatenate(pieces, axis=1)
        right = jnp.concatenate(
            [jnp.concatenate(windows_high, axis=1), jnp.concatenate(windows_low, axis=1)], axis=0
        )
        parts = lax.dot_general(
            left, right, (((1,), (1,)), ((), ())), preferred_element_type=jnp.float32
        )
        parts = parts[: 4 * SUBS] + parts[4 * SUBS :]
        parts = parts + half_turn(parts)
        for side in range(2):
            grad = jnp.where(
                low_lanes,
                parts[side * SUBS : (side + 1) * SUBS],
                parts[(2 + side) * SUBS : (3 + side) * SUBS],
            )
            saliency = grad * signal[side]
            position_sums[side] += saliency
            place = (channel * 2 + side) * SUBS
            products[place : place + SUBS, :] = saliency
    pick = (iota((SUBS, LANES), 1) // BLOCK == iota((SUBS, LANES), 0)).astype(jnp.bfloat16)
    block_sums = sum(
        lax.dot_general(
            pick, term, (((1,), (1,)), ((), ())), preferred_element_type=jnp.float32
        )
        for term in halves(products[...])
    )
    for device in range(devices):
        rows = [vals[device : device + 1] for vals in position_sums] + [block_sums[:2]]
        message = jnp.concatenate(rows, axis=0)
        for copy in range(copies):
            sums_ref[device * copies + copy, :, :] = message


def finish_kernel(channel_count, sums_ref, weight_ref, scale_ref, position_ref, nodes_ref):
    copies = lax.axis_size("ch")
    devices = sums_ref.shape[0] // copies
    own = lax.axis_index("ch")
    total = sums_ref[0]
    for source in range(1, devices * copies):
        total = total + sums_ref[source]
    position_ref[...] = total[:2] / channel_count
    own_lanes = iota((SUBS, LANES), 1) // (2 * SUBS) == iota((SUBS, LANES), 0)
    rows = []
    for source in range(devices):
        message = sums_ref[source * copies + own]
        rows.append(
            jnp.concatenate(
                [jnp.where(own_lanes, message[2 + side : 3 + side], 0.0) for side in range(2)],
                axis=1,
            )
        )
    high, low = halves(jnp.concatenate(rows, axis=0))
    both = jnp.dot(
        jnp.concatenate([high, low], axis=0), weight_ref[...], preferred_element_type=jnp.float32
    )
    count = high.shape[0]
    nodes_ref[...] = (both[:count] + both[count:]) * scale_ref[...]


def whole_channels(
    inputs, gate_values, probe_values, filter_taps, member_blocks, member_nodes, node_place
):
    devices = lax.axis_size("seq")
    copies = lax.axis_size("ch")
    channels, length = inputs.shape
    columns = node_place.shape[0] // devices
    local = (
        inputs,
        gate_values,
        probe_values,
        filter_taps,
        member_blocks.reshape(1, -1),
        member_nodes.reshape(1, -1),
    )
    packed = pl.pallas_call(
        functools.partial(pack_kernel, length // BLOCK),
        out_shape=jax.ShapeDtypeStruct((devices, PACK_ROWS, LANES), jnp.bfloat16),
        in_specs=[pl.BlockSpec(memory_space=pltpu.HBM)] * len(local),
        scratch_shapes=[pltpu.VMEM(part.shape, part.dtype) for part in local]
        + [pltpu.SemaphoreType.DMA((len(local),))],
        compiler_params=LEAN,
        name="pack",
    )(*(pltpu.with_memory_space_constraint(part, pltpu.HBM) for part in local))
    packed = lax.all_to_all(packed, "seq", split_axis=0, concat_axis=0, tiled=True)
    sums, weight, scale = pl.pallas_call(
        saliency_kernel,
        out_shape=(
            jax.ShapeDtypeStruct((devices * copies, 4, LANES), jnp.float32),
            jax.ShapeDtypeStruct((2 * LANES, columns), jnp.bfloat16),
            jax.ShapeDtypeStruct((1, columns), jnp.float32),
        ),
        scratch_shapes=[
            pltpu.VMEM((3, 2, devices * SUBS, LANES), jnp.float32),
            pltpu.VMEM((devices * FIELD_ROWS, LANES), jnp.float32),
            pltpu.VMEM((SUBS, 8, 2 * SUBS, LANES), jnp.float32),
            pltpu.VMEM((2 * SUBS * SUBS, LANES), jnp.float32),
        ],
        compiler_params=LEAN,
        name="saliency",
    )(packed, node_place.reshape(-1, LANES))
    sums = lax.all_to_all(sums, ("seq", "ch"), split_axis=0, concat_axis=0, tiled=True)
    position, node_rows = pl.pallas_call(
        functools.partial(finish_kernel, channels * copies),
        out_shape=(
            jax.ShapeDtypeStruct((2, LANES), jnp.float32),
            jax.ShapeDtypeStruct((channels, columns), jnp.float32),
        ),
        compiler_params=LEAN,
        name="finish",
    )(sums, weight, scale)
    return position.reshape(length), node_rows


def phase_table(rows_count, cols_count, modulus, sine_sign, row_start, col_start):
    row_ids = lax.broadcasted_iota(jnp.int32, (rows_count, cols_count), 0) + row_start
    col_ids = lax.broadcasted_iota(jnp.int32, (rows_count, cols_count), 1) + col_start
    angles = (row_ids * col_ids % modulus).astype(jnp.float32) * (2.0 * math.pi / modulus)
    return (jnp.cos(angles), sine_sign * jnp.sin(angles))


def complex_times(first_pair, second_pair):
    first_real, first_imag = first_pair
    second_real, second_imag = second_pair
    return (
        first_real * second_real - first_imag * second_imag,
        first_real * second_imag + first_imag * second_real,
    )


def complex_product(formula, first_pair, second_pair):
    first_real, first_imag = first_pair
    second_real, second_imag = second_pair
    real_part = jnp.einsum(formula, first_real, second_real, precision=HIGHEST) - jnp.einsum(
        formula, first_imag, second_imag, precision=HIGHEST
    )
    imag_part = jnp.einsum(formula, first_real, second_imag, precision=HIGHEST) + jnp.einsum(
        formula, first_imag, second_real, precision=HIGHEST
    )
    return (real_part, imag_part)


def split_sizes(length):
    return (length // 128, 128)


def local_forward(real_part, imag_part):
    stacks, rows_count, channels, length = real_part.shape
    outer_size, inner_size = split_sizes(length)
    data_pair = (
        real_part.reshape(-1, outer_size, inner_size),
        imag_part.reshape(-1, outer_size, inner_size),
    )
    part_pair = complex_product(
        "jn,rnm->rjm", phase_table(outer_size, outer_size, outer_size, -1.0, 0, 0), data_pair
    )
    part_pair = complex_times(part_pair, phase_table(outer_size, inner_size, length, -1.0, 0, 0))
    spec_real, spec_imag = complex_product(
        "rjn,nm->rjm", part_pair, phase_table(inner_size, inner_size, inner_size, -1.0, 0, 0)
    )
    new_shape = (stacks, rows_count * channels, outer_size, inner_size)
    return (spec_real.reshape(new_shape), spec_imag.reshape(new_shape))


def local_inverse(spec_real, spec_imag):
    stacks, rows_count, outer_size, inner_size = spec_real.shape
    length = outer_size * inner_size
    data_pair = (
        spec_real.reshape(-1, outer_size, inner_size),
        spec_imag.reshape(-1, outer_size, inner_size),
    )
    part_pair = complex_product(
        "rjn,nm->rjm", data_pair, phase_table(inner_size, inner_size, inner_size, 1.0, 0, 0)
    )
    part_pair = complex_times(part_pair, phase_table(outer_size, inner_size, length, 1.0, 0, 0))
    out_real, out_imag = complex_product(
        "jn,rnm->rjm", phase_table(outer_size, outer_size, outer_size, 1.0, 0, 0), part_pair
    )
    return (
        out_real.reshape(stacks, rows_count, length),
        out_imag.reshape(stacks, rows_count, length),
    )


def spectrum_full(columns, seq_index, send):
    stacks, devices, channels, col_width = columns.shape
    modulus = 2 * devices * devices * col_width
    flattened = columns.reshape(stacks, devices, channels * col_width)
    row_cos, row_sin = phase_table(2 * devices, devices, 2 * devices, -1.0, 0, 0)
    grid_shape = (stacks, 2 * devices, channels, col_width)
    real_part = jnp.einsum("kn,snm->skm", row_cos, flattened, precision=HIGHEST).reshape(grid_shape)
    imag_part = jnp.einsum("kn,snm->skm", row_sin, flattened, precision=HIGHEST).reshape(grid_shape)
    turn_cos, turn_sin = phase_table(
        2 * devices, col_width, modulus, -1.0, 0, seq_index * col_width
    )
    real_part, imag_part = complex_times(
        (real_part, imag_part), (turn_cos[:, None, :], turn_sin[:, None, :])
    )
    real_part, imag_part = send(real_part, imag_part)
    return local_forward(real_part, imag_part)


def signal_full(spec_real, spec_imag, seq_index, devices, send):
    real_part, imag_part = local_inverse(spec_real, spec_imag)
    stacks, rows_count, length = real_part.shape
    channels = rows_count // 2
    modulus = 2 * devices * length
    real_part = real_part.reshape(stacks, 2, channels, length)
    imag_part = imag_part.reshape(stacks, 2, channels, length)
    turn_cos, turn_sin = phase_table(2, length, modulus, 1.0, 2 * seq_index, 0)
    real_part, imag_part = complex_times(
        (real_part, imag_part), (turn_cos[:, None, :], turn_sin[:, None, :])
    )
    real_part, imag_part = send(real_part, imag_part)
    col_width = length // devices
    back_cos, back_sin = phase_table(devices, 2 * devices, 2 * devices, 1.0, 0, 0)
    flat_real = real_part.reshape(stacks, 2 * devices, channels * col_width)
    flat_imag = imag_part.reshape(stacks, 2 * devices, channels * col_width)
    signal_vals = (
        jnp.einsum("ak,skm->sam", back_cos, flat_real, precision=HIGHEST)
        - jnp.einsum("ak,skm->sam", back_sin, flat_imag, precision=HIGHEST)
    ) / modulus
    return signal_vals.reshape(stacks, devices, channels, col_width)


def cotangent(conv_vals, gating, probing):
    gate_wide = gating.astype(jnp.float32)
    mixed = gate_wide * conv_vals
    sigmoid_val = jax.nn.sigmoid(mixed)
    return (
        gate_wide * probing.astype(jnp.float32) * sigmoid_val * (1.0 + mixed * (1.0 - sigmoid_val))
    )


def spread_channels(
    inputs, gate_values, probe_values, filter_taps, member_blocks, member_nodes, node_place
):
    seq_index = lax.axis_index("seq")
    devices = lax.axis_size("seq")
    channels, length = inputs.shape
    inputs_wide = inputs.astype(jnp.float32)
    stacked = jnp.stack([inputs_wide, filter_taps]).reshape(2, 1, channels, length)
    columns_pair = lax.all_to_all(stacked, "seq", split_axis=3, concat_axis=1, tiled=True)

    def send_input(real_part, imag_part):
        return (
            lax.all_to_all(real_part, "seq", split_axis=1, concat_axis=3, tiled=True),
            lax.all_to_all(imag_part, "seq", split_axis=1, concat_axis=3, tiled=True),
        )

    def send_output(real_part, imag_part):
        return (
            lax.all_to_all(real_part, "seq", split_axis=3, concat_axis=1, tiled=True),
            lax.all_to_all(imag_part, "seq", split_axis=3, concat_axis=1, tiled=True),
        )

    def send_cotangent(real_part, imag_part):
        return (
            lax.all_to_all(real_part, "seq", split_axis=1, concat_axis=3, tiled=True),
            lax.all_to_all(imag_part, "seq", split_axis=1, concat_axis=3, tiled=True),
        )

    def send_gradient(real_part, imag_part):
        return (
            lax.all_to_all(real_part, "seq", split_axis=3, concat_axis=1, tiled=True),
            lax.all_to_all(imag_part, "seq", split_axis=3, concat_axis=1, tiled=True),
        )

    forward_section, inverse_section = (spectrum_full, signal_full)
    spec_real, spec_imag = forward_section(columns_pair, seq_index, send_input)
    filter_pair = (spec_real[1], spec_imag[1])
    conv_real, conv_imag = complex_times((spec_real[0], spec_imag[0]), filter_pair)
    conv_cols = inverse_section(conv_real[None], conv_imag[None], seq_index, devices, send_output)
    conv_rows = lax.all_to_all(conv_cols, "seq", split_axis=1, concat_axis=3, tiled=True).reshape(
        channels, length
    )
    back_rows = cotangent(conv_rows, gate_values, probe_values)
    back_cols = lax.all_to_all(
        back_rows.reshape(1, 1, channels, length), "seq", split_axis=3, concat_axis=1, tiled=True
    )
    back_real, back_imag = forward_section(back_cols, seq_index, send_cotangent)
    grad_real = back_real[0] * filter_pair[0] + back_imag[0] * filter_pair[1]
    grad_imag = back_imag[0] * filter_pair[0] - back_real[0] * filter_pair[1]
    grad_cols = inverse_section(grad_real[None], grad_imag[None], seq_index, devices, send_gradient)
    returned = lax.all_to_all(grad_cols, "seq", split_axis=1, concat_axis=3, tiled=True).reshape(
        channels, length
    )
    saliency = returned * inputs_wide
    channel_count = channels * lax.axis_size("ch")
    position_saliency = lax.psum(jnp.sum(saliency, axis=0), "ch") / channel_count
    blocks_dev = length // BLOCK
    block_rows = jnp.sum(saliency.reshape(channels, blocks_dev, BLOCK), axis=2)
    local_blocks = member_blocks - seq_index * blocks_dev
    targets = node_place[member_nodes]
    member_rows = jnp.take(block_rows, local_blocks, axis=1)
    nodes_dev = NODES // devices
    gathered_rows, gathered_targets = (
        lax.all_gather(member_rows, "seq", axis=1, tiled=True),
        lax.all_gather(targets.astype(jnp.float32), "seq", axis=0, tiled=True),
    )
    owned_ids = gathered_targets.astype(jnp.int32) - seq_index * nodes_dev
    slot_ids = jnp.where((owned_ids >= 0) & (owned_ids < nodes_dev), owned_ids, nodes_dev)
    node_sums = jax.ops.segment_sum(gathered_rows.T, slot_ids, num_segments=nodes_dev + 1)[
        :nodes_dev
    ].T
    node_counts = jax.ops.segment_sum(
        jnp.ones(slot_ids.shape, jnp.float32), slot_ids, num_segments=nodes_dev + 1
    )[:nodes_dev]
    node_rows = node_sums / jnp.maximum(node_counts, 1.0)[None, :]
    return (position_saliency, node_rows)


def per_device(*args):
    channels, length = args[0].shape
    devices = lax.axis_size("seq")
    members = args[4].shape[0]
    fits = channels == SUBS * devices and devices == SUBS and length == 2 * LANES
    if fits and members == SUBS and NODES % (devices * LANES) == 0:
        return whole_channels(*args)
    return spread_channels(*args)


def solution(mesh):
    placed = (
        P("ch", "seq"),
        P("ch", "seq"),
        P("ch", "seq"),
        P("ch", "seq"),
        P("seq"),
        P("seq"),
        P(),
    )
    return jax.shard_map(
        per_device,
        mesh=mesh,
        in_specs=placed,
        out_specs=(P("seq"), P("ch", "seq")),
        check_vma=False,
    )
```

```python
import functools
import math

import jax
import jax.numpy as jnp
from jax import lax
from jax.experimental import pallas as pl
from jax.experimental.pallas import tpu as pltpu
from jax.sharding import PartitionSpec as P

BLOCK = 64
NODES = 8192
LANES = 128
SUBS = 8
HALF = LANES // 2
PART = 32
PARTS = LANES // PART
FIELD_ROWS = 16
FIELDS = 5
MEMBER_ROW = FIELDS * FIELD_ROWS
PACK_ROWS = MEMBER_ROW + FIELD_ROWS


HIGHEST = lax.Precision.HIGHEST
LEAN = pltpu.CompilerParams(vmem_limit_bytes=16 * 1024 * 1024)


def iota(shape, dim):
    return lax.broadcasted_iota(jnp.int32, shape, dim)


def halves(vals):
    high = vals.astype(jnp.bfloat16)
    return high, (vals - high.astype(jnp.float32)).astype(jnp.bfloat16)


def pack_kernel(blocks_dev, *refs):
    sources, packed_ref, arrived, landed = refs[:6], refs[6], refs[7:13], refs[13]
    inputs_ref, gate_ref, probe_ref, taps_ref, blocks_ref, nodes_ref = arrived
    devices = packed_ref.shape[0]
    loads = [
        pltpu.make_async_copy(source, target, landed.at[place])
        for place, (source, target) in enumerate(zip(sources, arrived))
    ]
    for load in loads:
        load.start()
    for load in loads:
        load.wait()

    def put(pair, field, tiles):
        for side in range(2):
            rows = slice(side * SUBS, (side + 1) * SUBS)
            both = jnp.concatenate([tile[rows] for tile in tiles], axis=0)
            place = slice(field * FIELD_ROWS, (field + 1) * FIELD_ROWS)
            packed_ref[2 * pair + side, place, :] = both.astype(jnp.bfloat16)

    for pair in range(devices // 2):
        rows = slice(pair * 2 * SUBS, (pair + 1) * 2 * SUBS)
        columns = [slice(0, LANES), slice(LANES, 2 * LANES)]
        for field, ref in enumerate((inputs_ref, gate_ref, probe_ref)):
            put(pair, field, [ref[rows, cols].astype(jnp.float32) for cols in columns])
        split = [halves(taps_ref[rows, cols]) for cols in columns]
        for term in range(2):
            put(pair, 3 + term, [terms[term].astype(jnp.float32) for terms in split])

    def as_column(row):
        members = row.shape[1]
        same = iota((members, members), 0) == iota((members, members), 1)
        return jnp.sum(jnp.where(same, row, 0).astype(jnp.float32), axis=1, keepdims=True)

    nodes = nodes_ref[...]
    low_lanes = iota((SUBS, LANES), 1) < HALF
    digits = jnp.where(low_lanes, as_column(nodes // LANES), as_column(nodes % LANES))
    places = jnp.broadcast_to(as_column(blocks_ref[...] % blocks_dev), (SUBS, LANES))
    member_rows = jnp.concatenate([digits, places], axis=0).astype(jnp.bfloat16)
    for device in range(devices):
        packed_ref[device, MEMBER_ROW:, :] = member_rows


def fill_weights(packed_ref, place_ref, weight_ref, scale_ref):
    devices = packed_ref.shape[0]
    members = devices * SUBS
    columns = weight_ref.shape[1]
    blocks_dev = 2 * LANES // BLOCK
    digits, offsets = [], []
    for source in range(devices):
        both = packed_ref[source, MEMBER_ROW:, :].astype(jnp.float32)
        digits.append(both[:SUBS])
        offsets.append(both[SUBS:] + float(source * blocks_dev))
    digits = jnp.concatenate(digits, axis=0)
    offsets = jnp.concatenate(offsets, axis=0)
    place = place_ref[...]
    place_rows = place.shape[0]
    row_pick = iota((members, place_rows), 1).astype(jnp.float32) == digits[:, :1]
    row_pick = row_pick.astype(jnp.bfloat16)
    lane_ids = iota((members, LANES), 1).astype(jnp.float32)
    low_digit = jnp.broadcast_to(digits[:, HALF : HALF + 1], (members, LANES))

    def looked_up(table):
        found = jnp.dot(
            row_pick, table.astype(jnp.float32).astype(jnp.bfloat16),
            preferred_element_type=jnp.float32,
        )
        return jnp.sum(jnp.where(lane_ids == low_digit, found, 0.0), axis=1, keepdims=True)

    targets = looked_up(place // LANES) * LANES + looked_up(place % LANES)
    targets = targets - (lax.axis_index("seq") * columns).astype(jnp.float32)
    node_pick = iota((members, columns), 1).astype(jnp.float32) == targets
    node_pick = node_pick.astype(jnp.float32)
    counts = jnp.sum(node_pick, axis=0, keepdims=True)
    scale_ref[...] = 1.0 / jnp.maximum(counts, 1.0)
    slot = iota((members, 2 * LANES), 1)
    slot_block = slot % (2 * SUBS) * 2 + slot // LANES
    own_block = jnp.broadcast_to(offsets[:, :1], (members, 2 * LANES))
    block_pick = (slot_block.astype(jnp.float32) == own_block).astype(jnp.float32)
    weight_ref[...] = lax.dot_general(
        block_pick.T.astype(jnp.bfloat16),
        node_pick.astype(jnp.bfloat16),
        (((1,), (0,)), ((), ())),
        preferred_element_type=jnp.float32,
    ).astype(jnp.bfloat16)


def windows(taps, channel, first_turn, from_earlier):
    rows = []
    earlier = jnp.zeros((PART, LANES), jnp.float32)
    for block in range(taps.shape[0] // SUBS):
        row = jnp.broadcast_to(taps[pl.ds(block * SUBS + channel, 1), :], (PART, LANES))
        turned = pltpu.roll(row, first_turn, axis=1, stride=1, stride_axis=0)
        rows.append(jnp.concatenate(halves(jnp.where(from_earlier, earlier, turned)), axis=1))
        earlier = turned
    return jnp.concatenate(rows, axis=0)


def by_part(pieces):
    blocks = pieces[0].shape[0]
    lanes = iota((blocks, LANES), 1)
    result = pieces[-1]
    for part in range(len(pieces) - 2, -1, -1):
        result = jnp.where(lanes < (part + 1) * PART, pieces[part], result)
    return result


def turn(vals, parts):
    shift = parts * PART % LANES
    return pltpu.roll(vals, shift, axis=1) if shift else vals


def spread(rows, padded, single, sign):
    blocks = rows.shape[0]
    start = blocks if sign < 0 else 0
    zeros = jnp.zeros((blocks, LANES), jnp.float32)
    single[start : start + blocks, :] = rows
    single[blocks - start : 2 * blocks - start, :] = zeros
    moved = [single[start + sign * step : start + sign * step + blocks, :] for step in range(PARTS)]
    for part in range(PARTS):
        joined = by_part([turn(moved[step], step - part) for step in range(PARTS)])
        padded[part, start : start + blocks, :] = joined
        padded[part, blocks - start : 2 * blocks - start, :] = zeros
    columns = []
    for step in range(0, blocks, PARTS):
        offset = start + sign * step
        columns.append(
            jnp.concatenate(
                [padded[part, offset : offset + blocks, :] for part in range(PARTS)], axis=0
            )
        )
    return jnp.concatenate(columns, axis=1)


def next_block(vals, sign):
    blocks = vals.shape[0]
    row_ids = iota((blocks, LANES), 0)
    if sign < 0:
        return jnp.where(row_ids == 0, 0.0, pltpu.roll(vals, 1, axis=0))
    return jnp.where(row_ids == blocks - 1, 0.0, pltpu.roll(vals, blocks - 1, axis=0))


def saliency_kernel(
    packed_ref,
    place_ref,
    sums_ref,
    weight_ref,
    scale_ref,
    fields,
    taps,
    taps_turned,
    single,
    padded,
    products,
):
    devices = packed_ref.shape[0]
    blocks = 2 * devices
    copies = sums_ref.shape[0] // devices
    row_ids, lane_ids = iota((PART, LANES), 0), iota((PART, LANES), 1)
    lanes = iota((blocks, LANES), 1)
    terms = []
    for term in range(2):
        place = slice((3 + term) * FIELD_ROWS, (4 + term) * FIELD_ROWS)
        terms.append(
            jnp.concatenate([packed_ref[source, place, :] for source in range(devices)], axis=0)
        )
    taps[...] = terms[0].astype(jnp.float32) + terms[1].astype(jnp.float32)
    flip = iota((LANES, LANES), 0) + iota((LANES, LANES), 1) == LANES - 1
    flip = flip.astype(jnp.float32).astype(jnp.bfloat16)
    taps_turned[...] = sum(
        jnp.dot(term, flip, preferred_element_type=jnp.float32) for term in terms
    )
    for source in range(devices):
        for field in range(3):
            place = slice(field * FIELD_ROWS, (field + 1) * FIELD_ROWS)
            both = packed_ref[source, place, :].astype(jnp.float32)
            for side in range(2):
                rows = pl.ds(2 * source + side, SUBS, stride=blocks)
                fields[field, rows, :] = both[side * SUBS : (side + 1) * SUBS]
    fill_weights(packed_ref, place_ref, weight_ref, scale_ref)
    position_sums = jnp.zeros((blocks, LANES), jnp.float32)
    for channel in range(SUBS):
        place = slice(channel * blocks, (channel + 1) * blocks)
        signal, gating, probing = (fields[field, place, :] for field in range(3))
        left = spread(signal, padded.at[channel, 0], single.at[channel, 0], -1)
        right = windows(taps, channel, 0, lane_ids < row_ids)
        sums = jnp.dot(left.astype(jnp.bfloat16), right, preferred_element_type=jnp.float32)
        sums = sums[:, :LANES] + sums[:, LANES:]
        conv = sums[:blocks]
        for part in range(1, PARTS):
            own = sums[part * blocks : (part + 1) * blocks]
            wrapped = lanes >= LANES - part * PART
            conv = conv + turn(jnp.where(wrapped, next_block(own, -1), own), part)
        mixed = gating * conv
        sigmoid_val = jax.nn.sigmoid(mixed)
        back = gating * probing * sigmoid_val * (1.0 + mixed * (1.0 - sigmoid_val))
        left = spread(back, padded.at[channel, 1], single.at[channel, 1], 1)
        left = jnp.concatenate(halves(left), axis=0)
        right = windows(
            taps_turned, channel, LANES + 1 - PART, lane_ids + PART - 1 - row_ids >= LANES
        )
        sums = jnp.dot(left, right, preferred_element_type=jnp.float32)
        sums = sums[:, :LANES] + sums[:, LANES:]
        sums = sums[: PARTS * blocks] + sums[PARTS * blocks :]
        grad = sums[(PARTS - 1) * blocks :]
        for part in range(PARTS - 1):
            own = sums[part * blocks : (part + 1) * blocks]
            kept = lanes >= LANES - (part + 1) * PART
            grad = grad + turn(jnp.where(kept, own, next_block(own, 1)), part + 1)
        saliency = grad * signal
        position_sums += saliency
        products[place, :] = saliency
    pick = iota((SUBS, LANES), 1) // BLOCK == iota((SUBS, LANES), 0)
    pick = pick.astype(jnp.float32).astype(jnp.bfloat16)
    block_sums = sum(
        lax.dot_general(
            pick, term, (((1,), (1,)), ((), ())), preferred_element_type=jnp.float32
        )
        for term in halves(products[...])
    )
    for device in range(devices):
        message = jnp.concatenate(
            [position_sums[2 * device : 2 * device + 2], block_sums[:2]], axis=0
        )
        for copy in range(copies):
            sums_ref[device * copies + copy, :, :] = message


def finish_kernel(channel_count, sums_ref, weight_ref, scale_ref, position_ref, nodes_ref):
    copies = lax.axis_size("ch")
    devices = sums_ref.shape[0] // copies
    own = lax.axis_index("ch")
    total = sums_ref[0]
    for source in range(1, devices * copies):
        total = total + sums_ref[source]
    position_ref[...] = total[:2] / channel_count
    own_lanes = iota((SUBS, LANES), 1) // (2 * SUBS) == iota((SUBS, LANES), 0)
    rows = []
    for source in range(devices):
        message = sums_ref[source * copies + own]
        rows.append(
            jnp.concatenate(
                [jnp.where(own_lanes, message[2 + side : 3 + side], 0.0) for side in range(2)],
                axis=1,
            )
        )
    high, low = halves(jnp.concatenate(rows, axis=0))
    both = jnp.dot(
        jnp.concatenate([high, low], axis=0), weight_ref[...], preferred_element_type=jnp.float32
    )
    count = high.shape[0]
    nodes_ref[...] = (both[:count] + both[count:]) * scale_ref[...]


def whole_channels(
    inputs, gate_values, probe_values, filter_taps, member_blocks, member_nodes, node_place
):
    devices = lax.axis_size("seq")
    copies = lax.axis_size("ch")
    channels, length = inputs.shape
    columns = node_place.shape[0] // devices
    blocks = devices * length // LANES
    local = (
        inputs,
        gate_values,
        probe_values,
        filter_taps,
        member_blocks.reshape(1, -1),
        member_nodes.reshape(1, -1),
    )
    packed = pl.pallas_call(
        functools.partial(pack_kernel, length // BLOCK),
        out_shape=jax.ShapeDtypeStruct((devices, PACK_ROWS, LANES), jnp.bfloat16),
        in_specs=[pl.BlockSpec(memory_space=pltpu.HBM)] * len(local),
        scratch_shapes=[pltpu.VMEM(part.shape, part.dtype) for part in local]
        + [pltpu.SemaphoreType.DMA((len(local),))],
        compiler_params=LEAN,
        name="pack",
    )(*(pltpu.with_memory_space_constraint(part, pltpu.HBM) for part in local))
    packed = lax.all_to_all(packed, "seq", split_axis=0, concat_axis=0, tiled=True)
    sums, weight, scale = pl.pallas_call(
        saliency_kernel,
        out_shape=(
            jax.ShapeDtypeStruct((devices * copies, 4, LANES), jnp.float32),
            jax.ShapeDtypeStruct((2 * LANES, columns), jnp.bfloat16),
            jax.ShapeDtypeStruct((1, columns), jnp.float32),
        ),
        scratch_shapes=[
            pltpu.VMEM((3, SUBS * blocks, LANES), jnp.float32),
            pltpu.VMEM((blocks * SUBS, LANES), jnp.float32),
            pltpu.VMEM((blocks * SUBS, LANES), jnp.float32),
            pltpu.VMEM((SUBS, 2, 2 * blocks, LANES), jnp.float32),
            pltpu.VMEM((SUBS, 2, PARTS, 2 * blocks, LANES), jnp.float32),
            pltpu.VMEM((SUBS * blocks, LANES), jnp.float32),
        ],
        compiler_params=LEAN,
        name="saliency",
    )(packed, node_place.reshape(-1, LANES))
    sums = lax.all_to_all(sums, ("seq", "ch"), split_axis=0, concat_axis=0, tiled=True)
    position, node_rows = pl.pallas_call(
        functools.partial(finish_kernel, channels * copies),
        out_shape=(
            jax.ShapeDtypeStruct((2, LANES), jnp.float32),
            jax.ShapeDtypeStruct((channels, columns), jnp.float32),
        ),
        compiler_params=LEAN,
        name="finish",
    )(sums, weight, scale)
    return position.reshape(length), node_rows


def phase_table(rows_count, cols_count, modulus, sine_sign, row_start, col_start):
    row_ids = lax.broadcasted_iota(jnp.int32, (rows_count, cols_count), 0) + row_start
    col_ids = lax.broadcasted_iota(jnp.int32, (rows_count, cols_count), 1) + col_start
    angles = (row_ids * col_ids % modulus).astype(jnp.float32) * (2.0 * math.pi / modulus)
    return (jnp.cos(angles), sine_sign * jnp.sin(angles))


def complex_times(first_pair, second_pair):
    first_real, first_imag = first_pair
    second_real, second_imag = second_pair
    return (
        first_real * second_real - first_imag * second_imag,
        first_real * second_imag + first_imag * second_real,
    )


def complex_product(formula, first_pair, second_pair):
    first_real, first_imag = first_pair
    second_real, second_imag = second_pair
    real_part = jnp.einsum(formula, first_real, second_real, precision=HIGHEST) - jnp.einsum(
        formula, first_imag, second_imag, precision=HIGHEST
    )
    imag_part = jnp.einsum(formula, first_real, second_imag, precision=HIGHEST) + jnp.einsum(
        formula, first_imag, second_real, precision=HIGHEST
    )
    return (real_part, imag_part)


def split_sizes(length):
    return (length // 128, 128)


def local_forward(real_part, imag_part):
    stacks, rows_count, channels, length = real_part.shape
    outer_size, inner_size = split_sizes(length)
    data_pair = (
        real_part.reshape(-1, outer_size, inner_size),
        imag_part.reshape(-1, outer_size, inner_size),
    )
    part_pair = complex_product(
        "jn,rnm->rjm", phase_table(outer_size, outer_size, outer_size, -1.0, 0, 0), data_pair
    )
    part_pair = complex_times(part_pair, phase_table(outer_size, inner_size, length, -1.0, 0, 0))
    spec_real, spec_imag = complex_product(
        "rjn,nm->rjm", part_pair, phase_table(inner_size, inner_size, inner_size, -1.0, 0, 0)
    )
    new_shape = (stacks, rows_count * channels, outer_size, inner_size)
    return (spec_real.reshape(new_shape), spec_imag.reshape(new_shape))


def local_inverse(spec_real, spec_imag):
    stacks, rows_count, outer_size, inner_size = spec_real.shape
    length = outer_size * inner_size
    data_pair = (
        spec_real.reshape(-1, outer_size, inner_size),
        spec_imag.reshape(-1, outer_size, inner_size),
    )
    part_pair = complex_product(
        "rjn,nm->rjm", data_pair, phase_table(inner_size, inner_size, inner_size, 1.0, 0, 0)
    )
    part_pair = complex_times(part_pair, phase_table(outer_size, inner_size, length, 1.0, 0, 0))
    out_real, out_imag = complex_product(
        "jn,rnm->rjm", phase_table(outer_size, outer_size, outer_size, 1.0, 0, 0), part_pair
    )
    return (
        out_real.reshape(stacks, rows_count, length),
        out_imag.reshape(stacks, rows_count, length),
    )


def spectrum_full(columns, seq_index, send):
    stacks, devices, channels, col_width = columns.shape
    modulus = 2 * devices * devices * col_width
    flattened = columns.reshape(stacks, devices, channels * col_width)
    row_cos, row_sin = phase_table(2 * devices, devices, 2 * devices, -1.0, 0, 0)
    grid_shape = (stacks, 2 * devices, channels, col_width)
    real_part = jnp.einsum("kn,snm->skm", row_cos, flattened, precision=HIGHEST).reshape(grid_shape)
    imag_part = jnp.einsum("kn,snm->skm", row_sin, flattened, precision=HIGHEST).reshape(grid_shape)
    turn_cos, turn_sin = phase_table(
        2 * devices, col_width, modulus, -1.0, 0, seq_index * col_width
    )
    real_part, imag_part = complex_times(
        (real_part, imag_part), (turn_cos[:, None, :], turn_sin[:, None, :])
    )
    real_part, imag_part = send(real_part, imag_part)
    return local_forward(real_part, imag_part)


def signal_full(spec_real, spec_imag, seq_index, devices, send):
    real_part, imag_part = local_inverse(spec_real, spec_imag)
    stacks, rows_count, length = real_part.shape
    channels = rows_count // 2
    modulus = 2 * devices * length
    real_part = real_part.reshape(stacks, 2, channels, length)
    imag_part = imag_part.reshape(stacks, 2, channels, length)
    turn_cos, turn_sin = phase_table(2, length, modulus, 1.0, 2 * seq_index, 0)
    real_part, imag_part = complex_times(
        (real_part, imag_part), (turn_cos[:, None, :], turn_sin[:, None, :])
    )
    real_part, imag_part = send(real_part, imag_part)
    col_width = length // devices
    back_cos, back_sin = phase_table(devices, 2 * devices, 2 * devices, 1.0, 0, 0)
    flat_real = real_part.reshape(stacks, 2 * devices, channels * col_width)
    flat_imag = imag_part.reshape(stacks, 2 * devices, channels * col_width)
    signal_vals = (
        jnp.einsum("ak,skm->sam", back_cos, flat_real, precision=HIGHEST)
        - jnp.einsum("ak,skm->sam", back_sin, flat_imag, precision=HIGHEST)
    ) / modulus
    return signal_vals.reshape(stacks, devices, channels, col_width)


def cotangent(conv_vals, gating, probing):
    gate_wide = gating.astype(jnp.float32)
    mixed = gate_wide * conv_vals
    sigmoid_val = jax.nn.sigmoid(mixed)
    return (
        gate_wide * probing.astype(jnp.float32) * sigmoid_val * (1.0 + mixed * (1.0 - sigmoid_val))
    )


def spread_channels(
    inputs, gate_values, probe_values, filter_taps, member_blocks, member_nodes, node_place
):
    seq_index = lax.axis_index("seq")
    devices = lax.axis_size("seq")
    channels, length = inputs.shape
    inputs_wide = inputs.astype(jnp.float32)
    stacked = jnp.stack([inputs_wide, filter_taps]).reshape(2, 1, channels, length)
    columns_pair = lax.all_to_all(stacked, "seq", split_axis=3, concat_axis=1, tiled=True)

    def send_input(real_part, imag_part):
        return (
            lax.all_to_all(real_part, "seq", split_axis=1, concat_axis=3, tiled=True),
            lax.all_to_all(imag_part, "seq", split_axis=1, concat_axis=3, tiled=True),
        )

    def send_output(real_part, imag_part):
        return (
            lax.all_to_all(real_part, "seq", split_axis=3, concat_axis=1, tiled=True),
            lax.all_to_all(imag_part, "seq", split_axis=3, concat_axis=1, tiled=True),
        )

    def send_cotangent(real_part, imag_part):
        return (
            lax.all_to_all(real_part, "seq", split_axis=1, concat_axis=3, tiled=True),
            lax.all_to_all(imag_part, "seq", split_axis=1, concat_axis=3, tiled=True),
        )

    def send_gradient(real_part, imag_part):
        return (
            lax.all_to_all(real_part, "seq", split_axis=3, concat_axis=1, tiled=True),
            lax.all_to_all(imag_part, "seq", split_axis=3, concat_axis=1, tiled=True),
        )

    forward_section, inverse_section = (spectrum_full, signal_full)
    spec_real, spec_imag = forward_section(columns_pair, seq_index, send_input)
    filter_pair = (spec_real[1], spec_imag[1])
    conv_real, conv_imag = complex_times((spec_real[0], spec_imag[0]), filter_pair)
    conv_cols = inverse_section(conv_real[None], conv_imag[None], seq_index, devices, send_output)
    conv_rows = lax.all_to_all(conv_cols, "seq", split_axis=1, concat_axis=3, tiled=True).reshape(
        channels, length
    )
    back_rows = cotangent(conv_rows, gate_values, probe_values)
    back_cols = lax.all_to_all(
        back_rows.reshape(1, 1, channels, length), "seq", split_axis=3, concat_axis=1, tiled=True
    )
    back_real, back_imag = forward_section(back_cols, seq_index, send_cotangent)
    grad_real = back_real[0] * filter_pair[0] + back_imag[0] * filter_pair[1]
    grad_imag = back_imag[0] * filter_pair[0] - back_real[0] * filter_pair[1]
    grad_cols = inverse_section(grad_real[None], grad_imag[None], seq_index, devices, send_gradient)
    returned = lax.all_to_all(grad_cols, "seq", split_axis=1, concat_axis=3, tiled=True).reshape(
        channels, length
    )
    saliency = returned * inputs_wide
    channel_count = channels * lax.axis_size("ch")
    position_saliency = lax.psum(jnp.sum(saliency, axis=0), "ch") / channel_count
    blocks_dev = length // BLOCK
    block_rows = jnp.sum(saliency.reshape(channels, blocks_dev, BLOCK), axis=2)
    local_blocks = member_blocks - seq_index * blocks_dev
    targets = node_place[member_nodes]
    member_rows = jnp.take(block_rows, local_blocks, axis=1)
    nodes_dev = NODES // devices
    gathered_rows, gathered_targets = (
        lax.all_gather(member_rows, "seq", axis=1, tiled=True),
        lax.all_gather(targets.astype(jnp.float32), "seq", axis=0, tiled=True),
    )
    owned_ids = gathered_targets.astype(jnp.int32) - seq_index * nodes_dev
    slot_ids = jnp.where((owned_ids >= 0) & (owned_ids < nodes_dev), owned_ids, nodes_dev)
    node_sums = jax.ops.segment_sum(gathered_rows.T, slot_ids, num_segments=nodes_dev + 1)[
        :nodes_dev
    ].T
    node_counts = jax.ops.segment_sum(
        jnp.ones(slot_ids.shape, jnp.float32), slot_ids, num_segments=nodes_dev + 1
    )[:nodes_dev]
    node_rows = node_sums / jnp.maximum(node_counts, 1.0)[None, :]
    return (position_saliency, node_rows)


def per_device(*args):
    channels, length = args[0].shape
    devices = lax.axis_size("seq")
    members = args[4].shape[0]
    fits = channels == SUBS * devices and devices == SUBS and length == 2 * LANES
    if fits and members == SUBS and NODES % (devices * LANES) == 0:
        return whole_channels(*args)
    return spread_channels(*args)


def solution(mesh):
    placed = (
        P("ch", "seq"),
        P("ch", "seq"),
        P("ch", "seq"),
        P("ch", "seq"),
        P("seq"),
        P("seq"),
        P(),
    )
    return jax.shard_map(
        per_device,
        mesh=mesh,
        in_specs=placed,
        out_specs=(P("seq"), P("ch", "seq")),
        check_vma=False,
    )
```

```python
import functools
import math

import jax
import jax.numpy as jnp
from jax import lax
from jax.experimental import pallas as pl
from jax.experimental.pallas import tpu as pltpu
from jax.sharding import PartitionSpec as P

BLOCK = 64
NODES = 8192
LANES = 128
SUBS = 8
HALF = LANES // 2
PART = 32
PARTS = LANES // PART
FIELD_ROWS = 16
FIELDS = 5
PACK_ROWS = FIELDS * FIELD_ROWS


HIGHEST = lax.Precision.HIGHEST
LEAN = pltpu.CompilerParams(vmem_limit_bytes=16 * 1024 * 1024)


def iota(shape, dim):
    return lax.broadcasted_iota(jnp.int32, shape, dim)


def halves(vals):
    high = vals.astype(jnp.bfloat16)
    return high, (vals - high.astype(jnp.float32)).astype(jnp.bfloat16)


def as_column(row, count):
    width = row.shape[1]
    same = iota((count, width), 0) == iota((count, width), 1)
    return jnp.sum(jnp.where(same, row, 0.0), axis=1, keepdims=True)


def member_rows(blocks_ref, nodes_ref, place_ref):
    nodes = nodes_ref[...]
    count = nodes.shape[1]
    place = place_ref[...]
    row_pick = as_column((nodes // LANES).astype(jnp.float32), count) == iota(
        (count, place.shape[0]), 1
    ).astype(jnp.float32)
    row_pick = row_pick.astype(jnp.float32).astype(jnp.bfloat16)
    high, low = (
        jnp.dot(
            row_pick,
            digit.astype(jnp.float32).astype(jnp.bfloat16),
            preferred_element_type=jnp.float32,
        )
        for digit in (place // LANES, place % LANES)
    )
    lanes = iota((count, LANES), 1)
    low_digit = as_column((nodes % LANES).astype(jnp.float32), count)
    found = jnp.where(lanes.astype(jnp.float32) == low_digit, high * LANES + low, 0.0)
    targets = jnp.sum(found, axis=1, keepdims=True)
    blocks = as_column(blocks_ref[...].astype(jnp.float32), count)
    own = lanes == iota((count, LANES), 0) + lax.axis_index("seq") * count
    return jnp.concatenate(
        [jnp.sum(jnp.where(own, vals, 0.0), axis=0, keepdims=True) for vals in (targets, blocks)],
        axis=0,
    )


def pack_kernel(*refs):
    sources, (packed_ref, members_ref), arrived, landed = refs[:7], refs[7:9], refs[9:16], refs[16]
    loads = [
        pltpu.make_async_copy(source, target, landed.at[place])
        for place, (source, target) in enumerate(zip(sources, arrived))
    ]
    for load in loads[4:] + loads[:4]:
        load.start()

    def put(pair, field, tiles):
        for side in range(2):
            rows = slice(side * SUBS, (side + 1) * SUBS)
            both = jnp.concatenate([tile[rows] for tile in tiles], axis=0)
            place = slice(field * FIELD_ROWS, (field + 1) * FIELD_ROWS)
            packed_ref[2 * pair + side, place, :] = both.astype(jnp.bfloat16)

    for load in loads[4:]:
        load.wait()
    members_ref[...] = member_rows(*arrived[4:])
    columns = [slice(0, LANES), slice(LANES, 2 * LANES)]
    for field in range(4):
        loads[field].wait()
        for pair in range(packed_ref.shape[0] // 2):
            rows = slice(pair * 2 * SUBS, (pair + 1) * 2 * SUBS)
            tiles = [arrived[field][rows, cols] for cols in columns]
            if field < 3:
                put(pair, field, [tile.astype(jnp.float32) for tile in tiles])
                continue
            split = [halves(tile) for tile in tiles]
            for term in range(2):
                put(pair, field + term, [terms[term].astype(jnp.float32) for terms in split])


def windows(row_of, blocks, first_turn, from_earlier):
    rows = []
    earlier = jnp.zeros((PART, LANES), jnp.float32)
    for block in range(blocks):
        row = jnp.broadcast_to(row_of(block), (PART, LANES))
        turned = pltpu.roll(row, first_turn, axis=1, stride=1, stride_axis=0)
        rows.append(jnp.where(from_earlier, earlier, turned))
        earlier = turned
    return rows


def turn(vals, parts):
    shift = parts * PART % LANES
    return pltpu.roll(vals, shift, axis=1) if shift else vals


def exchanged(pieces):
    lanes = iota(pieces[0].shape, 1)
    low = lanes < 2 * PART
    crossed = [None] * PARTS
    for place in range(2):
        first, second = pieces[place], pieces[place + 2]
        swapped = turn(jnp.where(low, second, first), 2)
        crossed[place] = jnp.where(low, first, swapped)
        crossed[place + 2] = jnp.where(low, swapped, second)
    even = lanes % (2 * PART) < PART
    result = []
    for first, second in (crossed[:2], crossed[2:]):
        result.append(jnp.where(even, first, turn(second, 1)))
        result.append(jnp.where(even, turn(first, -1), second))
    return result


def joined_parts(rows, single, sign):
    blocks = rows.shape[0]
    start = blocks if sign < 0 else 0
    single[start : start + blocks, :] = rows
    single[blocks - start : 2 * blocks - start, :] = jnp.zeros((blocks, LANES), jnp.float32)
    return exchanged(
        [single[start + sign * step : start + sign * step + blocks, :] for step in range(PARTS)]
    )


def spread(joined, padded, sign):
    blocks = joined[0].shape[0]
    start = blocks if sign < 0 else 0
    for part in range(PARTS):
        padded[part, start : start + blocks, :] = joined[part]
        padded[part, blocks - start : 2 * blocks - start, :] = jnp.zeros(
            (blocks, LANES), jnp.float32
        )
    columns = []
    for step in range(0, blocks, PARTS):
        offset = start + sign * step
        columns.append(
            jnp.concatenate(
                [padded[part, offset : offset + blocks, :] for part in range(PARTS)], axis=0
            )
        )
    return jnp.concatenate(columns, axis=1).astype(jnp.bfloat16)


def next_block(vals, sign):
    blocks = vals.shape[0]
    row_ids = iota((blocks, LANES), 0)
    if sign < 0:
        return jnp.where(row_ids == 0, 0.0, pltpu.roll(vals, 1, axis=0))
    return jnp.where(row_ids == blocks - 1, 0.0, pltpu.roll(vals, blocks - 1, axis=0))


def saliency_kernel(
    packed_ref,
    members_ref,
    sums_ref,
    fields,
    taps_turned,
    single,
    padded,
    products,
):
    devices = packed_ref.shape[0]
    blocks = 2 * devices
    copies = sums_ref.shape[0] // devices
    row_ids, lane_ids = iota((PART, LANES), 0), iota((PART, LANES), 1)
    lanes = iota((blocks, LANES), 1)
    terms = []
    for term in range(2):
        place = slice((3 + term) * FIELD_ROWS, (4 + term) * FIELD_ROWS)
        terms.append(
            jnp.concatenate([packed_ref[source, place, :] for source in range(devices)], axis=0)
        )
    flip = iota((LANES, LANES), 0) + iota((LANES, LANES), 1) == LANES - 1
    flip = flip.astype(jnp.float32).astype(jnp.bfloat16)
    taps_turned[...] = sum(
        jnp.dot(term, flip, preferred_element_type=jnp.float32) for term in terms
    )
    for source in range(devices):
        for field in range(FIELDS):
            place = slice(field * FIELD_ROWS, (field + 1) * FIELD_ROWS)
            both = packed_ref[source, place, :].astype(jnp.float32)
            for side in range(2):
                rows = pl.ds(2 * source + side, SUBS, stride=blocks)
                fields[field, rows, :] = both[side * SUBS : (side + 1) * SUBS]
    position_sums = jnp.zeros((blocks, LANES), jnp.float32)
    for channel in range(SUBS):
        place = slice(channel * blocks, (channel + 1) * blocks)
        signal, gating, probing, *filters = (fields[field, place, :] for field in range(FIELDS))
        left = jnp.concatenate(
            [
                spread(
                    joined_parts(filters[term], single.at[channel, term], -1),
                    padded.at[channel, term],
                    -1,
                )
                for term in range(2)
            ],
            axis=0,
        )

        def signal_row(block, first=channel * blocks):
            return fields[0, first + block : first + block + 1, :]

        right = windows(signal_row, blocks, 0, lane_ids < row_ids)
        right = jnp.concatenate([rows.astype(jnp.bfloat16) for rows in right], axis=0)
        sums = jnp.dot(left, right, preferred_element_type=jnp.float32)
        sums = sums[: PARTS * blocks] + sums[PARTS * blocks :]
        conv = sums[:blocks]
        for part in range(1, PARTS):
            own = sums[part * blocks : (part + 1) * blocks]
            wrapped = lanes >= LANES - part * PART
            conv = conv + turn(jnp.where(wrapped, next_block(own, -1), own), part)
        mixed = gating * conv
        sigmoid_val = jax.nn.sigmoid(mixed)
        back = gating * probing * sigmoid_val * (1.0 + mixed * (1.0 - sigmoid_val))
        joined = joined_parts(back, single.at[channel, 2], 1)
        high = [vals.astype(jnp.bfloat16).astype(jnp.float32) for vals in joined]
        low = [vals - term for vals, term in zip(joined, high)]
        left = jnp.concatenate(
            [
                spread(vals, padded.at[channel, 2 + term], 1)
                for term, vals in enumerate((high, low))
            ],
            axis=0,
        )

        def filter_row(block, first=channel):
            return taps_turned[block * SUBS + first : block * SUBS + first + 1, :]

        right = windows(
            filter_row, blocks, LANES + 1 - PART, lane_ids + PART - 1 - row_ids >= LANES
        )
        right = jnp.concatenate(
            [jnp.concatenate(halves(rows), axis=1) for rows in right], axis=0
        )
        sums = jnp.dot(left, right, preferred_element_type=jnp.float32)
        sums = sums[:, :LANES] + sums[:, LANES:]
        sums = sums[: PARTS * blocks] + sums[PARTS * blocks :]
        grad = sums[(PARTS - 1) * blocks :]
        for part in range(PARTS - 1):
            own = sums[part * blocks : (part + 1) * blocks]
            kept = lanes >= LANES - (part + 1) * PART
            grad = grad + turn(jnp.where(kept, own, next_block(own, 1)), part + 1)
        saliency = grad * signal
        position_sums += saliency
        products[place, :] = saliency
    pick = iota((SUBS, LANES), 1) // BLOCK == iota((SUBS, LANES), 0)
    pick = pick.astype(jnp.float32).astype(jnp.bfloat16)
    block_sums = sum(
        lax.dot_general(
            pick, term, (((1,), (1,)), ((), ())), preferred_element_type=jnp.float32
        )
        for term in halves(products[...])
    )
    own = lax.axis_index("ch")
    for copy in range(copies):
        rest = jnp.where(own == copy, block_sums[:2], members_ref[...])
        for device in range(devices):
            sums_ref[copy * devices + device, :, :] = jnp.concatenate(
                [position_sums[2 * device : 2 * device + 2], rest], axis=0
            )


def finish_kernel(members, channel_count, sums_ref, position_ref, nodes_ref):
    copies = lax.axis_size("ch")
    devices = sums_ref.shape[0] // copies
    columns = nodes_ref.shape[1]
    own = lax.axis_index("ch")
    total = sums_ref[0]
    for source in range(1, devices * copies):
        total = total + sums_ref[source]
    position_ref[...] = total[:2] / channel_count
    other = lax.rem(own + 1, copies) * devices
    listed = sums_ref[other]
    for source in range(1, devices):
        listed = listed + sums_ref[other + source]
    targets = as_column(listed[2:3], members)
    targets = targets - (lax.axis_index("seq") * columns).astype(jnp.float32)
    node_pick = iota((members, columns), 1).astype(jnp.float32) == targets
    node_pick = node_pick.astype(jnp.float32)
    scale = 1.0 / jnp.maximum(jnp.sum(node_pick, axis=0, keepdims=True), 1.0)
    slot = iota((2 * LANES, LANES), 0)
    slot_block = (slot % (2 * SUBS) * 2 + slot // LANES).astype(jnp.float32)
    block_pick = (slot_block == listed[3:4]).astype(jnp.float32).astype(jnp.bfloat16)
    own_lanes = iota((SUBS, LANES), 1) // (2 * SUBS) == iota((SUBS, LANES), 0)
    rows = []
    for source in range(devices):
        message = sums_ref[own * devices + source]
        rows.append(
            jnp.concatenate(
                [jnp.where(own_lanes, message[2 + side : 3 + side], 0.0) for side in range(2)],
                axis=1,
            )
        )
    picked = jnp.dot(
        jnp.concatenate(halves(jnp.concatenate(rows, axis=0)), axis=0),
        block_pick[:, :members],
        preferred_element_type=jnp.float32,
    )
    both = jnp.dot(
        picked.astype(jnp.bfloat16),
        node_pick.astype(jnp.bfloat16),
        preferred_element_type=jnp.float32,
    )
    count = devices * SUBS
    nodes_ref[...] = (both[:count] + both[count:]) * scale


def whole_channels(
    inputs, gate_values, probe_values, filter_taps, member_blocks, member_nodes, node_place
):
    devices = lax.axis_size("seq")
    copies = lax.axis_size("ch")
    channels, length = inputs.shape
    columns = node_place.shape[0] // devices
    blocks = devices * length // LANES
    local = (
        inputs,
        gate_values,
        probe_values,
        filter_taps,
        member_blocks.reshape(1, -1),
        member_nodes.reshape(1, -1),
        node_place.reshape(-1, LANES),
    )
    packed, members = pl.pallas_call(
        pack_kernel,
        out_shape=(
            jax.ShapeDtypeStruct((devices, PACK_ROWS, LANES), jnp.bfloat16),
            jax.ShapeDtypeStruct((2, LANES), jnp.float32),
        ),
        in_specs=[pl.BlockSpec(memory_space=pltpu.HBM)] * len(local),
        scratch_shapes=[pltpu.VMEM(part.shape, part.dtype) for part in local]
        + [pltpu.SemaphoreType.DMA((len(local),))],
        compiler_params=LEAN,
        name="pack",
    )(*(pltpu.with_memory_space_constraint(part, pltpu.HBM) for part in local))
    packed = lax.all_to_all(packed, "seq", split_axis=0, concat_axis=0, tiled=True)
    sums = pl.pallas_call(
        saliency_kernel,
        out_shape=jax.ShapeDtypeStruct((devices * copies, 4, LANES), jnp.float32),
        scratch_shapes=[
            pltpu.VMEM((FIELDS, SUBS * blocks, LANES), jnp.float32),
            pltpu.VMEM((blocks * SUBS, LANES), jnp.float32),
            pltpu.VMEM((SUBS, 3, 2 * blocks, LANES), jnp.float32),
            pltpu.VMEM((SUBS, 4, PARTS, 2 * blocks, LANES), jnp.float32),
            pltpu.VMEM((SUBS * blocks, LANES), jnp.float32),
        ],
        compiler_params=LEAN,
        name="saliency",
    )(packed, members)
    sums = lax.all_to_all(sums, ("ch", "seq"), split_axis=0, concat_axis=0, tiled=True)
    position, node_rows = pl.pallas_call(
        functools.partial(finish_kernel, devices * member_nodes.shape[0], channels * copies),
        out_shape=(
            jax.ShapeDtypeStruct((2, LANES), jnp.float32),
            jax.ShapeDtypeStruct((channels, columns), jnp.float32),
        ),
        compiler_params=LEAN,
        name="finish",
    )(sums)
    return position.reshape(length), node_rows


def phase_table(rows_count, cols_count, modulus, sine_sign, row_start, col_start):
    row_ids = lax.broadcasted_iota(jnp.int32, (rows_count, cols_count), 0) + row_start
    col_ids = lax.broadcasted_iota(jnp.int32, (rows_count, cols_count), 1) + col_start
    angles = (row_ids * col_ids % modulus).astype(jnp.float32) * (2.0 * math.pi / modulus)
    return (jnp.cos(angles), sine_sign * jnp.sin(angles))


def complex_times(first_pair, second_pair):
    first_real, first_imag = first_pair
    second_real, second_imag = second_pair
    return (
        first_real * second_real - first_imag * second_imag,
        first_real * second_imag + first_imag * second_real,
    )


def complex_product(formula, first_pair, second_pair):
    first_real, first_imag = first_pair
    second_real, second_imag = second_pair
    real_part = jnp.einsum(formula, first_real, second_real, precision=HIGHEST) - jnp.einsum(
        formula, first_imag, second_imag, precision=HIGHEST
    )
    imag_part = jnp.einsum(formula, first_real, second_imag, precision=HIGHEST) + jnp.einsum(
        formula, first_imag, second_real, precision=HIGHEST
    )
    return (real_part, imag_part)


def split_sizes(length):
    return (length // 128, 128)


def local_forward(real_part, imag_part):
    stacks, rows_count, channels, length = real_part.shape
    outer_size, inner_size = split_sizes(length)
    data_pair = (
        real_part.reshape(-1, outer_size, inner_size),
        imag_part.reshape(-1, outer_size, inner_size),
    )
    part_pair = complex_product(
        "jn,rnm->rjm", phase_table(outer_size, outer_size, outer_size, -1.0, 0, 0), data_pair
    )
    part_pair = complex_times(part_pair, phase_table(outer_size, inner_size, length, -1.0, 0, 0))
    spec_real, spec_imag = complex_product(
        "rjn,nm->rjm", part_pair, phase_table(inner_size, inner_size, inner_size, -1.0, 0, 0)
    )
    new_shape = (stacks, rows_count * channels, outer_size, inner_size)
    return (spec_real.reshape(new_shape), spec_imag.reshape(new_shape))


def local_inverse(spec_real, spec_imag):
    stacks, rows_count, outer_size, inner_size = spec_real.shape
    length = outer_size * inner_size
    data_pair = (
        spec_real.reshape(-1, outer_size, inner_size),
        spec_imag.reshape(-1, outer_size, inner_size),
    )
    part_pair = complex_product(
        "rjn,nm->rjm", data_pair, phase_table(inner_size, inner_size, inner_size, 1.0, 0, 0)
    )
    part_pair = complex_times(part_pair, phase_table(outer_size, inner_size, length, 1.0, 0, 0))
    out_real, out_imag = complex_product(
        "jn,rnm->rjm", phase_table(outer_size, outer_size, outer_size, 1.0, 0, 0), part_pair
    )
    return (
        out_real.reshape(stacks, rows_count, length),
        out_imag.reshape(stacks, rows_count, length),
    )


def spectrum_full(columns, seq_index, send):
    stacks, devices, channels, col_width = columns.shape
    modulus = 2 * devices * devices * col_width
    flattened = columns.reshape(stacks, devices, channels * col_width)
    row_cos, row_sin = phase_table(2 * devices, devices, 2 * devices, -1.0, 0, 0)
    grid_shape = (stacks, 2 * devices, channels, col_width)
    real_part = jnp.einsum("kn,snm->skm", row_cos, flattened, precision=HIGHEST).reshape(grid_shape)
    imag_part = jnp.einsum("kn,snm->skm", row_sin, flattened, precision=HIGHEST).reshape(grid_shape)
    turn_cos, turn_sin = phase_table(
        2 * devices, col_width, modulus, -1.0, 0, seq_index * col_width
    )
    real_part, imag_part = complex_times(
        (real_part, imag_part), (turn_cos[:, None, :], turn_sin[:, None, :])
    )
    real_part, imag_part = send(real_part, imag_part)
    return local_forward(real_part, imag_part)


def signal_full(spec_real, spec_imag, seq_index, devices, send):
    real_part, imag_part = local_inverse(spec_real, spec_imag)
    stacks, rows_count, length = real_part.shape
    channels = rows_count // 2
    modulus = 2 * devices * length
    real_part = real_part.reshape(stacks, 2, channels, length)
    imag_part = imag_part.reshape(stacks, 2, channels, length)
    turn_cos, turn_sin = phase_table(2, length, modulus, 1.0, 2 * seq_index, 0)
    real_part, imag_part = complex_times(
        (real_part, imag_part), (turn_cos[:, None, :], turn_sin[:, None, :])
    )
    real_part, imag_part = send(real_part, imag_part)
    col_width = length // devices
    back_cos, back_sin = phase_table(devices, 2 * devices, 2 * devices, 1.0, 0, 0)
    flat_real = real_part.reshape(stacks, 2 * devices, channels * col_width)
    flat_imag = imag_part.reshape(stacks, 2 * devices, channels * col_width)
    signal_vals = (
        jnp.einsum("ak,skm->sam", back_cos, flat_real, precision=HIGHEST)
        - jnp.einsum("ak,skm->sam", back_sin, flat_imag, precision=HIGHEST)
    ) / modulus
    return signal_vals.reshape(stacks, devices, channels, col_width)


def cotangent(conv_vals, gating, probing):
    gate_wide = gating.astype(jnp.float32)
    mixed = gate_wide * conv_vals
    sigmoid_val = jax.nn.sigmoid(mixed)
    return (
        gate_wide * probing.astype(jnp.float32) * sigmoid_val * (1.0 + mixed * (1.0 - sigmoid_val))
    )


def spread_channels(
    inputs, gate_values, probe_values, filter_taps, member_blocks, member_nodes, node_place
):
    seq_index = lax.axis_index("seq")
    devices = lax.axis_size("seq")
    channels, length = inputs.shape
    inputs_wide = inputs.astype(jnp.float32)
    stacked = jnp.stack([inputs_wide, filter_taps]).reshape(2, 1, channels, length)
    columns_pair = lax.all_to_all(stacked, "seq", split_axis=3, concat_axis=1, tiled=True)

    def send_input(real_part, imag_part):
        return (
            lax.all_to_all(real_part, "seq", split_axis=1, concat_axis=3, tiled=True),
            lax.all_to_all(imag_part, "seq", split_axis=1, concat_axis=3, tiled=True),
        )

    def send_output(real_part, imag_part):
        return (
            lax.all_to_all(real_part, "seq", split_axis=3, concat_axis=1, tiled=True),
            lax.all_to_all(imag_part, "seq", split_axis=3, concat_axis=1, tiled=True),
        )

    def send_cotangent(real_part, imag_part):
        return (
            lax.all_to_all(real_part, "seq", split_axis=1, concat_axis=3, tiled=True),
            lax.all_to_all(imag_part, "seq", split_axis=1, concat_axis=3, tiled=True),
        )

    def send_gradient(real_part, imag_part):
        return (
            lax.all_to_all(real_part, "seq", split_axis=3, concat_axis=1, tiled=True),
            lax.all_to_all(imag_part, "seq", split_axis=3, concat_axis=1, tiled=True),
        )

    forward_section, inverse_section = (spectrum_full, signal_full)
    spec_real, spec_imag = forward_section(columns_pair, seq_index, send_input)
    filter_pair = (spec_real[1], spec_imag[1])
    conv_real, conv_imag = complex_times((spec_real[0], spec_imag[0]), filter_pair)
    conv_cols = inverse_section(conv_real[None], conv_imag[None], seq_index, devices, send_output)
    conv_rows = lax.all_to_all(conv_cols, "seq", split_axis=1, concat_axis=3, tiled=True).reshape(
        channels, length
    )
    back_rows = cotangent(conv_rows, gate_values, probe_values)
    back_cols = lax.all_to_all(
        back_rows.reshape(1, 1, channels, length), "seq", split_axis=3, concat_axis=1, tiled=True
    )
    back_real, back_imag = forward_section(back_cols, seq_index, send_cotangent)
    grad_real = back_real[0] * filter_pair[0] + back_imag[0] * filter_pair[1]
    grad_imag = back_imag[0] * filter_pair[0] - back_real[0] * filter_pair[1]
    grad_cols = inverse_section(grad_real[None], grad_imag[None], seq_index, devices, send_gradient)
    returned = lax.all_to_all(grad_cols, "seq", split_axis=1, concat_axis=3, tiled=True).reshape(
        channels, length
    )
    saliency = returned * inputs_wide
    channel_count = channels * lax.axis_size("ch")
    position_saliency = lax.psum(jnp.sum(saliency, axis=0), "ch") / channel_count
    blocks_dev = length // BLOCK
    block_rows = jnp.sum(saliency.reshape(channels, blocks_dev, BLOCK), axis=2)
    local_blocks = member_blocks - seq_index * blocks_dev
    targets = node_place[member_nodes]
    member_rows = jnp.take(block_rows, local_blocks, axis=1)
    nodes_dev = NODES // devices
    gathered_rows, gathered_targets = (
        lax.all_gather(member_rows, "seq", axis=1, tiled=True),
        lax.all_gather(targets.astype(jnp.float32), "seq", axis=0, tiled=True),
    )
    owned_ids = gathered_targets.astype(jnp.int32) - seq_index * nodes_dev
    slot_ids = jnp.where((owned_ids >= 0) & (owned_ids < nodes_dev), owned_ids, nodes_dev)
    node_sums = jax.ops.segment_sum(gathered_rows.T, slot_ids, num_segments=nodes_dev + 1)[
        :nodes_dev
    ].T
    node_counts = jax.ops.segment_sum(
        jnp.ones(slot_ids.shape, jnp.float32), slot_ids, num_segments=nodes_dev + 1
    )[:nodes_dev]
    node_rows = node_sums / jnp.maximum(node_counts, 1.0)[None, :]
    return (position_saliency, node_rows)


def per_device(*args):
    channels, length = args[0].shape
    devices = lax.axis_size("seq")
    members = args[4].shape[0]
    fits = channels == SUBS * devices and devices == SUBS and length == 2 * LANES
    if fits and members == SUBS and NODES % (devices * LANES) == 0:
        return whole_channels(*args)
    return spread_channels(*args)


def solution(mesh):
    placed = (
        P("ch", "seq"),
        P("ch", "seq"),
        P("ch", "seq"),
        P("ch", "seq"),
        P("seq"),
        P("seq"),
        P(),
    )
    return jax.shard_map(
        per_device,
        mesh=mesh,
        in_specs=placed,
        out_specs=(P("seq"), P("ch", "seq")),
        check_vma=False,
    )
```

```python
import functools
import math

import jax
import jax.numpy as jnp
from jax import lax
from jax.experimental import pallas as pl
from jax.experimental.pallas import tpu as pltpu
from jax.sharding import PartitionSpec as P

BLOCK = 64
NODES = 8192
LANES = 128
SUBS = 8
HALF = LANES // 2
PART = 32
PARTS = LANES // PART
FIELD_ROWS = 16
FIELDS = 5
PACK_ROWS = FIELDS * FIELD_ROWS


HIGHEST = lax.Precision.HIGHEST
LEAN = pltpu.CompilerParams(vmem_limit_bytes=16 * 1024 * 1024)


def iota(shape, dim):
    return lax.broadcasted_iota(jnp.int32, shape, dim)


def halves(vals):
    high = vals.astype(jnp.bfloat16)
    return high, (vals - high.astype(jnp.float32)).astype(jnp.bfloat16)


def as_column(row, count):
    width = row.shape[1]
    same = iota((count, width), 0) == iota((count, width), 1)
    return jnp.sum(jnp.where(same, row, 0.0), axis=1, keepdims=True)


def member_rows(blocks_ref, nodes_ref, place_ref):
    nodes = nodes_ref[...]
    count = nodes.shape[1]
    place = place_ref[...]
    row_pick = as_column((nodes // LANES).astype(jnp.float32), count) == iota(
        (count, place.shape[0]), 1
    ).astype(jnp.float32)
    row_pick = row_pick.astype(jnp.float32).astype(jnp.bfloat16)
    high, low = (
        jnp.dot(
            row_pick,
            digit.astype(jnp.float32).astype(jnp.bfloat16),
            preferred_element_type=jnp.float32,
        )
        for digit in (place // LANES, place % LANES)
    )
    lanes = iota((count, LANES), 1)
    low_digit = as_column((nodes % LANES).astype(jnp.float32), count)
    found = jnp.where(lanes.astype(jnp.float32) == low_digit, high * LANES + low, 0.0)
    targets = jnp.sum(found, axis=1, keepdims=True)
    blocks = as_column(blocks_ref[...].astype(jnp.float32), count)
    own = lanes == iota((count, LANES), 0) + lax.axis_index("seq") * count
    return jnp.concatenate(
        [jnp.sum(jnp.where(own, vals, 0.0), axis=0, keepdims=True) for vals in (targets, blocks)],
        axis=0,
    )


def pack_kernel(*refs):
    sources, packed_ref, lists, arrived, landed = (
        refs[:7], refs[7], refs[8:11], refs[11:15], refs[15]
    )
    loads = [
        pltpu.make_async_copy(source, target, landed.at[place])
        for place, (source, target) in enumerate(zip(sources, (*arrived, *lists)))
    ]
    for load in loads:
        load.start()

    def put(pair, field, tiles):
        for side in range(2):
            rows = slice(side * SUBS, (side + 1) * SUBS)
            both = jnp.concatenate([tile[rows] for tile in tiles], axis=0)
            place = slice(field * FIELD_ROWS, (field + 1) * FIELD_ROWS)
            packed_ref[2 * pair + side, place, :] = both.astype(jnp.bfloat16)

    columns = [slice(0, LANES), slice(LANES, 2 * LANES)]
    for field in range(4):
        loads[field].wait()
        for pair in range(packed_ref.shape[0] // 2):
            rows = slice(pair * 2 * SUBS, (pair + 1) * 2 * SUBS)
            tiles = [arrived[field][rows, cols] for cols in columns]
            if field < 3:
                put(pair, field, [tile.astype(jnp.float32) for tile in tiles])
                continue
            split = [halves(tile) for tile in tiles]
            for term in range(2):
                put(pair, field + term, [terms[term].astype(jnp.float32) for terms in split])

    for load in loads[4:]:
        load.wait()


def windows(taps, first, blocks):
    later = iota((PART, LANES), 1) >= iota((PART, LANES), 0)
    rows = []
    earlier = jnp.zeros((PART, LANES), jnp.float32)
    for block in range(blocks):
        row = jnp.broadcast_to(taps[first + block : first + block + 1, :], (PART, LANES))
        turned = pltpu.roll(row, 0, axis=1, stride=1, stride_axis=0)
        rows.append(jnp.concatenate(halves(jnp.where(later, turned, earlier)), axis=1))
        earlier = turned
    return jnp.concatenate(rows, axis=0)


def turn(vals, parts):
    shift = parts * PART % LANES
    return pltpu.roll(vals, shift, axis=1) if shift else vals


def exchanged(pieces):
    lanes = iota(pieces[0].shape, 1)
    low = lanes < 2 * PART
    crossed = [None] * PARTS
    for place in range(2):
        first, second = pieces[place], pieces[place + 2]
        swapped = turn(jnp.where(low, second, first), 2)
        crossed[place] = jnp.where(low, first, swapped)
        crossed[place + 2] = jnp.where(low, swapped, second)
    even = lanes % (2 * PART) < PART
    result = []
    for first, second in (crossed[:2], crossed[2:]):
        result.append(jnp.where(even, first, turn(second, 1)))
        result.append(jnp.where(even, turn(first, -1), second))
    return result


def joined_parts(rows, single, sign):
    blocks = rows.shape[0]
    start = blocks if sign < 0 else 0
    single[start : start + blocks, :] = rows
    single[blocks - start : 2 * blocks - start, :] = jnp.zeros((blocks, LANES), jnp.float32)
    return exchanged(
        [single[start + sign * step : start + sign * step + blocks, :] for step in range(PARTS)]
    )


def spread(joined, padded, sign):
    blocks = joined[0].shape[0]
    start = blocks if sign < 0 else 0
    for part in range(PARTS):
        padded[part, start : start + blocks, :] = joined[part]
        padded[part, blocks - start : 2 * blocks - start, :] = jnp.zeros(
            (blocks, LANES), jnp.float32
        )
    columns = []
    for step in range(0, blocks, PARTS):
        offset = start + sign * step
        columns.append(
            jnp.concatenate(
                [padded[part, offset : offset + blocks, :] for part in range(PARTS)], axis=0
            )
        )
    return jnp.concatenate(columns, axis=1).astype(jnp.bfloat16)


def spread_terms(joined, padded, sign):
    high = [vals.astype(jnp.bfloat16).astype(jnp.float32) for vals in joined]
    low = [vals - term for vals, term in zip(joined, high)]
    return jnp.concatenate(
        [spread(vals, ref, sign) for vals, ref in zip((high, low), padded)], axis=0
    )


def next_block(vals, sign):
    blocks = vals.shape[0]
    row_ids = iota((blocks, LANES), 0)
    if sign < 0:
        return jnp.where(row_ids == 0, 0.0, pltpu.roll(vals, 1, axis=0))
    return jnp.where(row_ids == blocks - 1, 0.0, pltpu.roll(vals, blocks - 1, axis=0))


def overlapped(sums, sign):
    blocks = sums.shape[0] // PARTS
    lanes = iota((blocks, LANES), 1)
    result = sums[:blocks]
    for part in range(1, PARTS):
        own = sums[part * blocks : (part + 1) * blocks]
        wrapped = lanes >= LANES - part * PART
        result = result + turn(jnp.where(wrapped, next_block(own, sign), own), part)
    return result


def saliency_kernel(
    packed_ref,
    blocks_ref,
    nodes_ref,
    place_ref,
    sums_ref,
    fields,
    single,
    padded,
    products,
    held,
):
    devices = packed_ref.shape[0]
    blocks = 2 * devices
    copies = sums_ref.shape[0] // devices
    for source in range(devices):
        rows = [
            packed_ref[source, field * FIELD_ROWS : (field + 1) * FIELD_ROWS, :].astype(jnp.float32)
            for field in range(FIELDS)
        ]
        rows = [*rows[:3], rows[3] + rows[4]]
        for field in range(4):
            for side in range(2):
                place = pl.ds(2 * source + side, SUBS, stride=blocks)
                fields[field, place, :] = rows[field][side * SUBS : (side + 1) * SUBS]
    flip = iota((LANES, LANES), 0) + iota((LANES, LANES), 1) == LANES - 1
    flip = flip.astype(jnp.float32).astype(jnp.bfloat16)
    flip_both = jnp.concatenate([flip, flip], axis=0)

    def flipped(vals):
        return jnp.dot(
            jnp.concatenate(halves(vals), axis=1), flip_both, preferred_element_type=jnp.float32
        )

    fields[4] = jnp.dot(
        fields[0].astype(jnp.bfloat16), flip, preferred_element_type=jnp.float32
    )
    members = member_rows(blocks_ref, nodes_ref, place_ref)
    position_sums = jnp.zeros((blocks, LANES), jnp.float32)
    backs = []
    for channel in range(SUBS):
        place = slice(channel * blocks, (channel + 1) * blocks)
        signal, gating, probing = (fields[field, place, :] for field in range(3))
        held[channel] = windows(fields.at[3], channel * blocks, blocks)
        left = spread(
            joined_parts(signal, single.at[channel, 0], -1), padded.at[channel, 0], -1
        )
        sums = jnp.dot(left, held[channel], preferred_element_type=jnp.float32)
        conv = overlapped(sums[:, :LANES] + sums[:, LANES:], -1)
        mixed = gating * conv
        sigmoid_val = jax.nn.sigmoid(mixed)
        backs.append(gating * probing * sigmoid_val * (1.0 + mixed * (1.0 - sigmoid_val)))
    cuts = (0, SUBS // 2, 3 * SUBS // 4, SUBS)
    backs = jnp.concatenate(
        [flipped(jnp.concatenate(backs[f:l], axis=0)) for f, l in zip(cuts, cuts[1:])], axis=0
    )
    for channel in range(SUBS):
        place = slice(channel * blocks, (channel + 1) * blocks)
        left = spread_terms(
            joined_parts(backs[place], single.at[channel, 1], 1),
            [padded.at[channel, 1 + term] for term in range(2)],
            1,
        )
        sums = jnp.dot(left, held[channel], preferred_element_type=jnp.float32)
        sums = sums[:, :LANES] + sums[:, LANES:]
        grad = overlapped(sums[: PARTS * blocks] + sums[PARTS * blocks :], 1)
        saliency = grad * fields[4, place, :]
        position_sums += saliency
        products[place, :] = saliency
    position_sums = flipped(position_sums)
    pick = (LANES - 1 - iota((SUBS, LANES), 1)) // BLOCK == iota((SUBS, LANES), 0)
    pick = pick.astype(jnp.float32).astype(jnp.bfloat16)
    block_sums = sum(
        lax.dot_general(
            pick, term, (((1,), (1,)), ((), ())), preferred_element_type=jnp.float32
        )
        for term in halves(products[...])
    )
    own = lax.axis_index("ch")
    for copy in range(copies):
        rest = jnp.where(own == copy, block_sums[:2], members)
        for device in range(devices):
            sums_ref[copy * devices + device, :, :] = jnp.concatenate(
                [position_sums[2 * device : 2 * device + 2], rest], axis=0
            )


def finish_kernel(members, channel_count, sums_ref, position_ref, nodes_ref):
    copies = lax.axis_size("ch")
    devices = sums_ref.shape[0] // copies
    columns = nodes_ref.shape[1]
    own = lax.axis_index("ch")
    total = sums_ref[0]
    for source in range(1, devices * copies):
        total = total + sums_ref[source]
    position_ref[...] = total[:2] / channel_count
    other = lax.rem(own + 1, copies) * devices
    listed = sums_ref[other]
    for source in range(1, devices):
        listed = listed + sums_ref[other + source]
    targets = as_column(listed[2:3], members)
    targets = targets - (lax.axis_index("seq") * columns).astype(jnp.float32)
    node_pick = iota((members, columns), 1).astype(jnp.float32) == targets
    node_pick = node_pick.astype(jnp.float32)
    scale = 1.0 / jnp.maximum(jnp.sum(node_pick, axis=0, keepdims=True), 1.0)
    slot = iota((2 * LANES, LANES), 0)
    slot_block = (slot % (2 * SUBS) * 2 + slot // LANES).astype(jnp.float32)
    block_pick = (slot_block == listed[3:4]).astype(jnp.float32).astype(jnp.bfloat16)
    own_lanes = iota((SUBS, LANES), 1) // (2 * SUBS) == iota((SUBS, LANES), 0)
    rows = []
    for source in range(devices):
        message = sums_ref[own * devices + source]
        rows.append(
            jnp.concatenate(
                [jnp.where(own_lanes, message[2 + side : 3 + side], 0.0) for side in range(2)],
                axis=1,
            )
        )
    picked = jnp.dot(
        jnp.concatenate(halves(jnp.concatenate(rows, axis=0)), axis=0),
        block_pick[:, :members],
        preferred_element_type=jnp.float32,
    )
    both = jnp.dot(
        picked.astype(jnp.bfloat16),
        node_pick.astype(jnp.bfloat16),
        preferred_element_type=jnp.float32,
    )
    count = devices * SUBS
    nodes_ref[...] = (both[:count] + both[count:]) * scale


def whole_channels(
    inputs, gate_values, probe_values, filter_taps, member_blocks, member_nodes, node_place
):
    devices = lax.axis_size("seq")
    copies = lax.axis_size("ch")
    channels, length = inputs.shape
    columns = node_place.shape[0] // devices
    blocks = devices * length // LANES
    local = (
        inputs,
        gate_values,
        probe_values,
        filter_taps,
        member_blocks.reshape(1, -1),
        member_nodes.reshape(1, -1),
        node_place.reshape(-1, LANES),
    )
    packed, *lists = pl.pallas_call(
        pack_kernel,
        out_shape=(
            jax.ShapeDtypeStruct((devices, PACK_ROWS, LANES), jnp.bfloat16),
            *(jax.ShapeDtypeStruct(part.shape, part.dtype) for part in local[4:]),
        ),
        in_specs=[pl.BlockSpec(memory_space=pltpu.HBM)] * len(local),
        scratch_shapes=[pltpu.VMEM(part.shape, part.dtype) for part in local[:4]]
        + [pltpu.SemaphoreType.DMA((len(local),))],
        compiler_params=LEAN,
        name="pack",
    )(*(pltpu.with_memory_space_constraint(part, pltpu.HBM) for part in local))
    packed = lax.all_to_all(packed, "seq", split_axis=0, concat_axis=0, tiled=True)
    sums = pl.pallas_call(
        saliency_kernel,
        out_shape=jax.ShapeDtypeStruct((devices * copies, 4, LANES), jnp.float32),
        scratch_shapes=[
            pltpu.VMEM((FIELDS, SUBS * blocks, LANES), jnp.float32),
            pltpu.VMEM((SUBS, 2, 2 * blocks, LANES), jnp.float32),
            pltpu.VMEM((SUBS, 3, PARTS, 2 * blocks, LANES), jnp.float32),
            pltpu.VMEM((SUBS * blocks, LANES), jnp.float32),
            pltpu.VMEM((SUBS, blocks * PART, 2 * LANES), jnp.bfloat16),
        ],
        compiler_params=LEAN,
        name="saliency",
    )(packed, *lists)
    sums = lax.all_to_all(sums, ("ch", "seq"), split_axis=0, concat_axis=0, tiled=True)
    position, node_rows = pl.pallas_call(
        functools.partial(finish_kernel, devices * member_nodes.shape[0], channels * copies),
        out_shape=(
            jax.ShapeDtypeStruct((2, LANES), jnp.float32),
            jax.ShapeDtypeStruct((channels, columns), jnp.float32),
        ),
        compiler_params=LEAN,
        name="finish",
    )(sums)
    return position.reshape(length), node_rows


def phase_table(rows_count, cols_count, modulus, sine_sign, row_start, col_start):
    row_ids = lax.broadcasted_iota(jnp.int32, (rows_count, cols_count), 0) + row_start
    col_ids = lax.broadcasted_iota(jnp.int32, (rows_count, cols_count), 1) + col_start
    angles = (row_ids * col_ids % modulus).astype(jnp.float32) * (2.0 * math.pi / modulus)
    return (jnp.cos(angles), sine_sign * jnp.sin(angles))


def complex_times(first_pair, second_pair):
    first_real, first_imag = first_pair
    second_real, second_imag = second_pair
    return (
        first_real * second_real - first_imag * second_imag,
        first_real * second_imag + first_imag * second_real,
    )


def complex_product(formula, first_pair, second_pair):
    first_real, first_imag = first_pair
    second_real, second_imag = second_pair
    real_part = jnp.einsum(formula, first_real, second_real, precision=HIGHEST) - jnp.einsum(
        formula, first_imag, second_imag, precision=HIGHEST
    )
    imag_part = jnp.einsum(formula, first_real, second_imag, precision=HIGHEST) + jnp.einsum(
        formula, first_imag, second_real, precision=HIGHEST
    )
    return (real_part, imag_part)


def split_sizes(length):
    return (length // 128, 128)


def local_forward(real_part, imag_part):
    stacks, rows_count, channels, length = real_part.shape
    outer_size, inner_size = split_sizes(length)
    data_pair = (
        real_part.reshape(-1, outer_size, inner_size),
        imag_part.reshape(-1, outer_size, inner_size),
    )
    part_pair = complex_product(
        "jn,rnm->rjm", phase_table(outer_size, outer_size, outer_size, -1.0, 0, 0), data_pair
    )
    part_pair = complex_times(part_pair, phase_table(outer_size, inner_size, length, -1.0, 0, 0))
    spec_real, spec_imag = complex_product(
        "rjn,nm->rjm", part_pair, phase_table(inner_size, inner_size, inner_size, -1.0, 0, 0)
    )
    new_shape = (stacks, rows_count * channels, outer_size, inner_size)
    return (spec_real.reshape(new_shape), spec_imag.reshape(new_shape))


def local_inverse(spec_real, spec_imag):
    stacks, rows_count, outer_size, inner_size = spec_real.shape
    length = outer_size * inner_size
    data_pair = (
        spec_real.reshape(-1, outer_size, inner_size),
        spec_imag.reshape(-1, outer_size, inner_size),
    )
    part_pair = complex_product(
        "rjn,nm->rjm", data_pair, phase_table(inner_size, inner_size, inner_size, 1.0, 0, 0)
    )
    part_pair = complex_times(part_pair, phase_table(outer_size, inner_size, length, 1.0, 0, 0))
    out_real, out_imag = complex_product(
        "jn,rnm->rjm", phase_table(outer_size, outer_size, outer_size, 1.0, 0, 0), part_pair
    )
    return (
        out_real.reshape(stacks, rows_count, length),
        out_imag.reshape(stacks, rows_count, length),
    )


def spectrum_full(columns, seq_index, send):
    stacks, devices, channels, col_width = columns.shape
    modulus = 2 * devices * devices * col_width
    flattened = columns.reshape(stacks, devices, channels * col_width)
    row_cos, row_sin = phase_table(2 * devices, devices, 2 * devices, -1.0, 0, 0)
    grid_shape = (stacks, 2 * devices, channels, col_width)
    real_part = jnp.einsum("kn,snm->skm", row_cos, flattened, precision=HIGHEST).reshape(grid_shape)
    imag_part = jnp.einsum("kn,snm->skm", row_sin, flattened, precision=HIGHEST).reshape(grid_shape)
    turn_cos, turn_sin = phase_table(
        2 * devices, col_width, modulus, -1.0, 0, seq_index * col_width
    )
    real_part, imag_part = complex_times(
        (real_part, imag_part), (turn_cos[:, None, :], turn_sin[:, None, :])
    )
    real_part, imag_part = send(real_part, imag_part)
    return local_forward(real_part, imag_part)


def signal_full(spec_real, spec_imag, seq_index, devices, send):
    real_part, imag_part = local_inverse(spec_real, spec_imag)
    stacks, rows_count, length = real_part.shape
    channels = rows_count // 2
    modulus = 2 * devices * length
    real_part = real_part.reshape(stacks, 2, channels, length)
    imag_part = imag_part.reshape(stacks, 2, channels, length)
    turn_cos, turn_sin = phase_table(2, length, modulus, 1.0, 2 * seq_index, 0)
    real_part, imag_part = complex_times(
        (real_part, imag_part), (turn_cos[:, None, :], turn_sin[:, None, :])
    )
    real_part, imag_part = send(real_part, imag_part)
    col_width = length // devices
    back_cos, back_sin = phase_table(devices, 2 * devices, 2 * devices, 1.0, 0, 0)
    flat_real = real_part.reshape(stacks, 2 * devices, channels * col_width)
    flat_imag = imag_part.reshape(stacks, 2 * devices, channels * col_width)
    signal_vals = (
        jnp.einsum("ak,skm->sam", back_cos, flat_real, precision=HIGHEST)
        - jnp.einsum("ak,skm->sam", back_sin, flat_imag, precision=HIGHEST)
    ) / modulus
    return signal_vals.reshape(stacks, devices, channels, col_width)


def cotangent(conv_vals, gating, probing):
    gate_wide = gating.astype(jnp.float32)
    mixed = gate_wide * conv_vals
    sigmoid_val = jax.nn.sigmoid(mixed)
    return (
        gate_wide * probing.astype(jnp.float32) * sigmoid_val * (1.0 + mixed * (1.0 - sigmoid_val))
    )


def spread_channels(
    inputs, gate_values, probe_values, filter_taps, member_blocks, member_nodes, node_place
):
    seq_index = lax.axis_index("seq")
    devices = lax.axis_size("seq")
    channels, length = inputs.shape
    inputs_wide = inputs.astype(jnp.float32)
    stacked = jnp.stack([inputs_wide, filter_taps]).reshape(2, 1, channels, length)
    columns_pair = lax.all_to_all(stacked, "seq", split_axis=3, concat_axis=1, tiled=True)

    def send_input(real_part, imag_part):
        return (
            lax.all_to_all(real_part, "seq", split_axis=1, concat_axis=3, tiled=True),
            lax.all_to_all(imag_part, "seq", split_axis=1, concat_axis=3, tiled=True),
        )

    def send_output(real_part, imag_part):
        return (
            lax.all_to_all(real_part, "seq", split_axis=3, concat_axis=1, tiled=True),
            lax.all_to_all(imag_part, "seq", split_axis=3, concat_axis=1, tiled=True),
        )

    def send_cotangent(real_part, imag_part):
        return (
            lax.all_to_all(real_part, "seq", split_axis=1, concat_axis=3, tiled=True),
            lax.all_to_all(imag_part, "seq", split_axis=1, concat_axis=3, tiled=True),
        )

    def send_gradient(real_part, imag_part):
        return (
            lax.all_to_all(real_part, "seq", split_axis=3, concat_axis=1, tiled=True),
            lax.all_to_all(imag_part, "seq", split_axis=3, concat_axis=1, tiled=True),
        )

    forward_section, inverse_section = (spectrum_full, signal_full)
    spec_real, spec_imag = forward_section(columns_pair, seq_index, send_input)
    filter_pair = (spec_real[1], spec_imag[1])
    conv_real, conv_imag = complex_times((spec_real[0], spec_imag[0]), filter_pair)
    conv_cols = inverse_section(conv_real[None], conv_imag[None], seq_index, devices, send_output)
    conv_rows = lax.all_to_all(conv_cols, "seq", split_axis=1, concat_axis=3, tiled=True).reshape(
        channels, length
    )
    back_rows = cotangent(conv_rows, gate_values, probe_values)
    back_cols = lax.all_to_all(
        back_rows.reshape(1, 1, channels, length), "seq", split_axis=3, concat_axis=1, tiled=True
    )
    back_real, back_imag = forward_section(back_cols, seq_index, send_cotangent)
    grad_real = back_real[0] * filter_pair[0] + back_imag[0] * filter_pair[1]
    grad_imag = back_imag[0] * filter_pair[0] - back_real[0] * filter_pair[1]
    grad_cols = inverse_section(grad_real[None], grad_imag[None], seq_index, devices, send_gradient)
    returned = lax.all_to_all(grad_cols, "seq", split_axis=1, concat_axis=3, tiled=True).reshape(
        channels, length
    )
    saliency = returned * inputs_wide
    channel_count = channels * lax.axis_size("ch")
    position_saliency = lax.psum(jnp.sum(saliency, axis=0), "ch") / channel_count
    blocks_dev = length // BLOCK
    block_rows = jnp.sum(saliency.reshape(channels, blocks_dev, BLOCK), axis=2)
    local_blocks = member_blocks - seq_index * blocks_dev
    targets = node_place[member_nodes]
    member_rows = jnp.take(block_rows, local_blocks, axis=1)
    nodes_dev = NODES // devices
    gathered_rows, gathered_targets = (
        lax.all_gather(member_rows, "seq", axis=1, tiled=True),
        lax.all_gather(targets.astype(jnp.float32), "seq", axis=0, tiled=True),
    )
    owned_ids = gathered_targets.astype(jnp.int32) - seq_index * nodes_dev
    slot_ids = jnp.where((owned_ids >= 0) & (owned_ids < nodes_dev), owned_ids, nodes_dev)
    node_sums = jax.ops.segment_sum(gathered_rows.T, slot_ids, num_segments=nodes_dev + 1)[
        :nodes_dev
    ].T
    node_counts = jax.ops.segment_sum(
        jnp.ones(slot_ids.shape, jnp.float32), slot_ids, num_segments=nodes_dev + 1
    )[:nodes_dev]
    node_rows = node_sums / jnp.maximum(node_counts, 1.0)[None, :]
    return (position_saliency, node_rows)


def per_device(*args):
    channels, length = args[0].shape
    devices = lax.axis_size("seq")
    members = args[4].shape[0]
    fits = channels == SUBS * devices and devices == SUBS and length == 2 * LANES
    fits = fits and members == SUBS and lax.axis_size("ch") > 1
    if fits and NODES % (devices * LANES) == 0:
        return whole_channels(*args)
    return spread_channels(*args)


def solution(mesh):
    placed = (
        P("ch", "seq"),
        P("ch", "seq"),
        P("ch", "seq"),
        P("ch", "seq"),
        P("seq"),
        P("seq"),
        P(),
    )
    return jax.shard_map(
        per_device,
        mesh=mesh,
        in_specs=placed,
        out_specs=(P("seq"), P("ch", "seq")),
        check_vma=False,
    )
```

```python
import functools
import math

import jax
import jax.numpy as jnp
from jax import lax
from jax.experimental import pallas as pl
from jax.experimental.pallas import tpu as pltpu
from jax.sharding import PartitionSpec as P

BLOCK = 64
NODES = 8192
LANES = 128
SUBS = 8
HALF = LANES // 2
PART = 32
PARTS = LANES // PART
FIELD_ROWS = 16
FIELDS = 5
PACK_ROWS = FIELDS * FIELD_ROWS


HIGHEST = lax.Precision.HIGHEST
LEAN = pltpu.CompilerParams(vmem_limit_bytes=16 * 1024 * 1024)


def iota(shape, dim):
    return lax.broadcasted_iota(jnp.int32, shape, dim)


def halves(vals):
    high = vals.astype(jnp.bfloat16)
    return high, (vals - high.astype(jnp.float32)).astype(jnp.bfloat16)


def as_column(row, count):
    width = row.shape[1]
    same = iota((count, width), 0) == iota((count, width), 1)
    return jnp.sum(jnp.where(same, row, 0.0), axis=1, keepdims=True)


def member_rows(blocks_ref, nodes_ref, place_ref):
    nodes = nodes_ref[...]
    count = nodes.shape[1]
    place = place_ref[...]
    row_pick = as_column((nodes // LANES).astype(jnp.float32), count) == iota(
        (count, place.shape[0]), 1
    ).astype(jnp.float32)
    row_pick = row_pick.astype(jnp.float32).astype(jnp.bfloat16)
    high, low = (
        jnp.dot(
            row_pick,
            digit.astype(jnp.float32).astype(jnp.bfloat16),
            preferred_element_type=jnp.float32,
        )
        for digit in (place // LANES, place % LANES)
    )
    lanes = iota((count, LANES), 1)
    low_digit = as_column((nodes % LANES).astype(jnp.float32), count)
    found = jnp.where(lanes.astype(jnp.float32) == low_digit, high * LANES + low, 0.0)
    targets = jnp.sum(found, axis=1, keepdims=True)
    blocks = as_column(blocks_ref[...].astype(jnp.float32), count)
    own = lanes == iota((count, LANES), 0) + lax.axis_index("seq") * count
    return jnp.concatenate(
        [jnp.sum(jnp.where(own, vals, 0.0), axis=0, keepdims=True) for vals in (targets, blocks)],
        axis=0,
    )


def pack_kernel(*refs):
    sources, packed_ref, lists, arrived, landed = (
        refs[:7], refs[7], refs[8:11], refs[11:15], refs[15]
    )
    loads = [
        pltpu.make_async_copy(source, target, landed.at[place])
        for place, (source, target) in enumerate(zip(sources, (*arrived, *lists)))
    ]
    for load in loads:
        load.start()

    def put(pair, field, tiles):
        for side in range(2):
            rows = slice(side * SUBS, (side + 1) * SUBS)
            both = jnp.concatenate([tile[rows] for tile in tiles], axis=0)
            place = slice(field * FIELD_ROWS, (field + 1) * FIELD_ROWS)
            packed_ref[2 * pair + side, place, :] = both.astype(jnp.bfloat16)

    columns = [slice(0, LANES), slice(LANES, 2 * LANES)]
    for field in range(4):
        loads[field].wait()
        for pair in range(packed_ref.shape[0] // 2):
            rows = slice(pair * 2 * SUBS, (pair + 1) * 2 * SUBS)
            tiles = [arrived[field][rows, cols] for cols in columns]
            if field < 3:
                put(pair, field, [tile.astype(jnp.float32) for tile in tiles])
                continue
            split = [halves(tile) for tile in tiles]
            for term in range(2):
                put(pair, field + term, [terms[term].astype(jnp.float32) for terms in split])

    for load in loads[4:]:
        load.wait()


def windows(taps, first, blocks):
    later = iota((PART, LANES), 1) >= iota((PART, LANES), 0)
    rows = []
    earlier = jnp.zeros((PART, LANES), jnp.float32)
    for block in range(blocks):
        row = jnp.broadcast_to(taps[first + block : first + block + 1, :], (PART, LANES))
        turned = pltpu.roll(row, 0, axis=1, stride=1, stride_axis=0)
        rows.append(jnp.concatenate(halves(jnp.where(later, turned, earlier)), axis=1))
        earlier = turned
    return jnp.concatenate(rows, axis=0)


def turn(vals, parts):
    shift = parts * PART % LANES
    return pltpu.roll(vals, shift, axis=1) if shift else vals


def joined_parts(copies, single, sign):
    blocks = copies.shape[0]
    lanes = iota((blocks, LANES), 1)
    start = blocks if sign < 0 else 0
    result = []
    for part in range(PARTS):
        rows = single.at[part]
        rows[start : start + blocks, :] = copies[:, part * LANES : (part + 1) * LANES]
        rows[blocks - start : 2 * blocks - start, :] = jnp.zeros((blocks, LANES), jnp.float32)
        joined = rows[start : start + blocks, :]
        for step in range(1, PARTS):
            moved = rows[start + sign * step : start + sign * step + blocks, :]
            joined = jnp.where(lanes < step * PART, joined, moved)
        result.append(joined)
    return result


def spread(joined, padded, sign):
    blocks = joined[0].shape[0]
    start = blocks if sign < 0 else 0
    for part in range(PARTS):
        padded[part, start : start + blocks, :] = joined[part]
        padded[part, blocks - start : 2 * blocks - start, :] = jnp.zeros(
            (blocks, LANES), jnp.float32
        )
    columns = []
    for step in range(0, blocks, PARTS):
        offset = start + sign * step
        columns.append(
            jnp.concatenate(
                [padded[part, offset : offset + blocks, :] for part in range(PARTS)], axis=0
            )
        )
    return jnp.concatenate(columns, axis=1).astype(jnp.bfloat16)


def spread_terms(joined, padded, sign):
    high = [vals.astype(jnp.bfloat16).astype(jnp.float32) for vals in joined]
    low = [vals - term for vals, term in zip(joined, high)]
    return jnp.concatenate(
        [spread(vals, ref, sign) for vals, ref in zip((high, low), padded)], axis=0
    )


def next_block(vals, sign):
    blocks = vals.shape[0]
    row_ids = iota((blocks, LANES), 0)
    if sign < 0:
        return jnp.where(row_ids == 0, 0.0, pltpu.roll(vals, 1, axis=0))
    return jnp.where(row_ids == blocks - 1, 0.0, pltpu.roll(vals, blocks - 1, axis=0))


def overlapped(sums, sign):
    blocks = sums.shape[0] // PARTS
    lanes = iota((blocks, LANES), 1)
    result = sums[:blocks]
    for part in range(1, PARTS):
        own = sums[part * blocks : (part + 1) * blocks]
        wrapped = lanes >= LANES - part * PART
        result = result + turn(jnp.where(wrapped, next_block(own, sign), own), part)
    return result


def saliency_kernel(
    packed_ref,
    blocks_ref,
    nodes_ref,
    place_ref,
    sums_ref,
    fields,
    single,
    padded,
    products,
    held,
):
    devices = packed_ref.shape[0]
    blocks = 2 * devices
    copies = sums_ref.shape[0] // devices
    for source in range(devices):
        rows = [
            packed_ref[source, field * FIELD_ROWS : (field + 1) * FIELD_ROWS, :].astype(jnp.float32)
            for field in range(FIELDS)
        ]
        rows = [*rows[:3], rows[3] + rows[4]]
        for field in range(4):
            for side in range(2):
                place = pl.ds(2 * source + side, SUBS, stride=blocks)
                fields[field, place, :] = rows[field][side * SUBS : (side + 1) * SUBS]
    flip = iota((LANES, LANES), 0) + iota((LANES, LANES), 1) == LANES - 1
    flip = flip.astype(jnp.float32).astype(jnp.bfloat16)
    lane_ids, column_ids = (iota((LANES, PARTS * LANES), dim) for dim in range(2))
    origins = column_ids // LANES * PART + column_ids % PART
    repeat, flip_repeat = (
        (ids == origins).astype(jnp.float32).astype(jnp.bfloat16)
        for ids in (lane_ids, LANES - 1 - lane_ids)
    )

    def both_terms(vals, chosen):
        return jnp.dot(
            jnp.concatenate(halves(vals), axis=1),
            jnp.concatenate([chosen, chosen], axis=0),
            preferred_element_type=jnp.float32,
        )

    signals = jnp.dot(
        fields[0].astype(jnp.bfloat16), repeat, preferred_element_type=jnp.float32
    )
    fields[4] = jnp.dot(
        fields[0].astype(jnp.bfloat16), flip, preferred_element_type=jnp.float32
    )
    members = member_rows(blocks_ref, nodes_ref, place_ref)
    position_sums = jnp.zeros((blocks, LANES), jnp.float32)
    backs = []
    for channel in range(SUBS):
        place = slice(channel * blocks, (channel + 1) * blocks)
        gating, probing = fields[1, place, :], fields[2, place, :]
        held[channel] = windows(fields.at[3], channel * blocks, blocks)
        left = spread(
            joined_parts(signals[place], single.at[channel, 0], -1), padded.at[channel, 0], -1
        )
        sums = jnp.dot(left, held[channel], preferred_element_type=jnp.float32)
        conv = overlapped(sums[:, :LANES] + sums[:, LANES:], -1)
        mixed = gating * conv
        sigmoid_val = jax.nn.sigmoid(mixed)
        backs.append(gating * probing * sigmoid_val * (1.0 + mixed * (1.0 - sigmoid_val)))
    cuts = (0, SUBS // 2, 3 * SUBS // 4, SUBS)
    backs = jnp.concatenate(
        [
            both_terms(jnp.concatenate(backs[f:l], axis=0), flip_repeat)
            for f, l in zip(cuts, cuts[1:])
        ],
        axis=0,
    )
    for channel in range(SUBS):
        place = slice(channel * blocks, (channel + 1) * blocks)
        left = spread_terms(
            joined_parts(backs[place], single.at[channel, 1], 1),
            [padded.at[channel, 1 + term] for term in range(2)],
            1,
        )
        sums = jnp.dot(left, held[channel], preferred_element_type=jnp.float32)
        sums = sums[:, :LANES] + sums[:, LANES:]
        grad = overlapped(sums[: PARTS * blocks] + sums[PARTS * blocks :], 1)
        saliency = grad * fields[4, place, :]
        position_sums += saliency
        products[place, :] = saliency
    position_sums = both_terms(position_sums, flip)
    pick = (LANES - 1 - iota((SUBS, LANES), 1)) // BLOCK == iota((SUBS, LANES), 0)
    pick = pick.astype(jnp.float32).astype(jnp.bfloat16)
    block_sums = sum(
        lax.dot_general(
            pick, term, (((1,), (1,)), ((), ())), preferred_element_type=jnp.float32
        )
        for term in halves(products[...])
    )
    own = lax.axis_index("ch")
    for copy in range(copies):
        rest = jnp.where(own == copy, block_sums[:2], members)
        for device in range(devices):
            sums_ref[copy * devices + device, :, :] = jnp.concatenate(
                [position_sums[2 * device : 2 * device + 2], rest], axis=0
            )


def finish_kernel(members, channel_count, sums_ref, position_ref, nodes_ref):
    copies = lax.axis_size("ch")
    devices = sums_ref.shape[0] // copies
    columns = nodes_ref.shape[1]
    own = lax.axis_index("ch")
    total = sums_ref[0]
    for source in range(1, devices * copies):
        total = total + sums_ref[source]
    position_ref[...] = total[:2] / channel_count
    other = lax.rem(own + 1, copies) * devices
    listed = sums_ref[other]
    for source in range(1, devices):
        listed = listed + sums_ref[other + source]
    targets = as_column(listed[2:3], members)
    targets = targets - (lax.axis_index("seq") * columns).astype(jnp.float32)
    node_pick = iota((members, columns), 1).astype(jnp.float32) == targets
    node_pick = node_pick.astype(jnp.float32)
    scale = 1.0 / jnp.maximum(jnp.sum(node_pick, axis=0, keepdims=True), 1.0)
    slot = iota((2 * LANES, LANES), 0)
    slot_block = (slot % (2 * SUBS) * 2 + slot // LANES).astype(jnp.float32)
    block_pick = (slot_block == listed[3:4]).astype(jnp.float32).astype(jnp.bfloat16)
    own_lanes = iota((SUBS, LANES), 1) // (2 * SUBS) == iota((SUBS, LANES), 0)
    rows = []
    for source in range(devices):
        message = sums_ref[own * devices + source]
        rows.append(
            jnp.concatenate(
                [jnp.where(own_lanes, message[2 + side : 3 + side], 0.0) for side in range(2)],
                axis=1,
            )
        )
    picked = jnp.dot(
        jnp.concatenate(halves(jnp.concatenate(rows, axis=0)), axis=0),
        block_pick[:, :members],
        preferred_element_type=jnp.float32,
    )
    both = jnp.dot(
        picked.astype(jnp.bfloat16),
        node_pick.astype(jnp.bfloat16),
        preferred_element_type=jnp.float32,
    )
    count = devices * SUBS
    nodes_ref[...] = (both[:count] + both[count:]) * scale


def whole_channels(
    inputs, gate_values, probe_values, filter_taps, member_blocks, member_nodes, node_place
):
    devices = lax.axis_size("seq")
    copies = lax.axis_size("ch")
    channels, length = inputs.shape
    columns = node_place.shape[0] // devices
    blocks = devices * length // LANES
    local = (
        inputs,
        gate_values,
        probe_values,
        filter_taps,
        member_blocks.reshape(1, -1),
        member_nodes.reshape(1, -1),
        node_place.reshape(-1, LANES),
    )
    packed, *lists = pl.pallas_call(
        pack_kernel,
        out_shape=(
            jax.ShapeDtypeStruct((devices, PACK_ROWS, LANES), jnp.bfloat16),
            *(jax.ShapeDtypeStruct(part.shape, part.dtype) for part in local[4:]),
        ),
        in_specs=[pl.BlockSpec(memory_space=pltpu.HBM)] * len(local),
        scratch_shapes=[pltpu.VMEM(part.shape, part.dtype) for part in local[:4]]
        + [pltpu.SemaphoreType.DMA((len(local),))],
        compiler_params=LEAN,
        name="pack",
    )(*(pltpu.with_memory_space_constraint(part, pltpu.HBM) for part in local))
    packed = lax.all_to_all(packed, "seq", split_axis=0, concat_axis=0, tiled=True)
    sums = pl.pallas_call(
        saliency_kernel,
        out_shape=jax.ShapeDtypeStruct((devices * copies, 4, LANES), jnp.float32),
        scratch_shapes=[
            pltpu.VMEM((FIELDS, SUBS * blocks, LANES), jnp.float32),
            pltpu.VMEM((SUBS, 2, PARTS, 2 * blocks, LANES), jnp.float32),
            pltpu.VMEM((SUBS, 3, PARTS, 2 * blocks, LANES), jnp.float32),
            pltpu.VMEM((SUBS * blocks, LANES), jnp.float32),
            pltpu.VMEM((SUBS, blocks * PART, 2 * LANES), jnp.bfloat16),
        ],
        compiler_params=LEAN,
        name="saliency",
    )(packed, *lists)
    sums = lax.all_to_all(sums, ("ch", "seq"), split_axis=0, concat_axis=0, tiled=True)
    position, node_rows = pl.pallas_call(
        functools.partial(finish_kernel, devices * member_nodes.shape[0], channels * copies),
        out_shape=(
            jax.ShapeDtypeStruct((2, LANES), jnp.float32),
            jax.ShapeDtypeStruct((channels, columns), jnp.float32),
        ),
        compiler_params=LEAN,
        name="finish",
    )(sums)
    return position.reshape(length), node_rows


def phase_table(rows_count, cols_count, modulus, sine_sign, row_start, col_start):
    row_ids = lax.broadcasted_iota(jnp.int32, (rows_count, cols_count), 0) + row_start
    col_ids = lax.broadcasted_iota(jnp.int32, (rows_count, cols_count), 1) + col_start
    angles = (row_ids * col_ids % modulus).astype(jnp.float32) * (2.0 * math.pi / modulus)
    return (jnp.cos(angles), sine_sign * jnp.sin(angles))


def complex_times(first_pair, second_pair):
    first_real, first_imag = first_pair
    second_real, second_imag = second_pair
    return (
        first_real * second_real - first_imag * second_imag,
        first_real * second_imag + first_imag * second_real,
    )


def complex_product(formula, first_pair, second_pair):
    first_real, first_imag = first_pair
    second_real, second_imag = second_pair
    real_part = jnp.einsum(formula, first_real, second_real, precision=HIGHEST) - jnp.einsum(
        formula, first_imag, second_imag, precision=HIGHEST
    )
    imag_part = jnp.einsum(formula, first_real, second_imag, precision=HIGHEST) + jnp.einsum(
        formula, first_imag, second_real, precision=HIGHEST
    )
    return (real_part, imag_part)


def split_sizes(length):
    return (length // 128, 128)


def local_forward(real_part, imag_part):
    stacks, rows_count, channels, length = real_part.shape
    outer_size, inner_size = split_sizes(length)
    data_pair = (
        real_part.reshape(-1, outer_size, inner_size),
        imag_part.reshape(-1, outer_size, inner_size),
    )
    part_pair = complex_product(
        "jn,rnm->rjm", phase_table(outer_size, outer_size, outer_size, -1.0, 0, 0), data_pair
    )
    part_pair = complex_times(part_pair, phase_table(outer_size, inner_size, length, -1.0, 0, 0))
    spec_real, spec_imag = complex_product(
        "rjn,nm->rjm", part_pair, phase_table(inner_size, inner_size, inner_size, -1.0, 0, 0)
    )
    new_shape = (stacks, rows_count * channels, outer_size, inner_size)
    return (spec_real.reshape(new_shape), spec_imag.reshape(new_shape))


def local_inverse(spec_real, spec_imag):
    stacks, rows_count, outer_size, inner_size = spec_real.shape
    length = outer_size * inner_size
    data_pair = (
        spec_real.reshape(-1, outer_size, inner_size),
        spec_imag.reshape(-1, outer_size, inner_size),
    )
    part_pair = complex_product(
        "rjn,nm->rjm", data_pair, phase_table(inner_size, inner_size, inner_size, 1.0, 0, 0)
    )
    part_pair = complex_times(part_pair, phase_table(outer_size, inner_size, length, 1.0, 0, 0))
    out_real, out_imag = complex_product(
        "jn,rnm->rjm", phase_table(outer_size, outer_size, outer_size, 1.0, 0, 0), part_pair
    )
    return (
        out_real.reshape(stacks, rows_count, length),
        out_imag.reshape(stacks, rows_count, length),
    )


def spectrum_full(columns, seq_index, send):
    stacks, devices, channels, col_width = columns.shape
    modulus = 2 * devices * devices * col_width
    flattened = columns.reshape(stacks, devices, channels * col_width)
    row_cos, row_sin = phase_table(2 * devices, devices, 2 * devices, -1.0, 0, 0)
    grid_shape = (stacks, 2 * devices, channels, col_width)
    real_part = jnp.einsum("kn,snm->skm", row_cos, flattened, precision=HIGHEST).reshape(grid_shape)
    imag_part = jnp.einsum("kn,snm->skm", row_sin, flattened, precision=HIGHEST).reshape(grid_shape)
    turn_cos, turn_sin = phase_table(
        2 * devices, col_width, modulus, -1.0, 0, seq_index * col_width
    )
    real_part, imag_part = complex_times(
        (real_part, imag_part), (turn_cos[:, None, :], turn_sin[:, None, :])
    )
    real_part, imag_part = send(real_part, imag_part)
    return local_forward(real_part, imag_part)


def signal_full(spec_real, spec_imag, seq_index, devices, send):
    real_part, imag_part = local_inverse(spec_real, spec_imag)
    stacks, rows_count, length = real_part.shape
    channels = rows_count // 2
    modulus = 2 * devices * length
    real_part = real_part.reshape(stacks, 2, channels, length)
    imag_part = imag_part.reshape(stacks, 2, channels, length)
    turn_cos, turn_sin = phase_table(2, length, modulus, 1.0, 2 * seq_index, 0)
    real_part, imag_part = complex_times(
        (real_part, imag_part), (turn_cos[:, None, :], turn_sin[:, None, :])
    )
    real_part, imag_part = send(real_part, imag_part)
    col_width = length // devices
    back_cos, back_sin = phase_table(devices, 2 * devices, 2 * devices, 1.0, 0, 0)
    flat_real = real_part.reshape(stacks, 2 * devices, channels * col_width)
    flat_imag = imag_part.reshape(stacks, 2 * devices, channels * col_width)
    signal_vals = (
        jnp.einsum("ak,skm->sam", back_cos, flat_real, precision=HIGHEST)
        - jnp.einsum("ak,skm->sam", back_sin, flat_imag, precision=HIGHEST)
    ) / modulus
    return signal_vals.reshape(stacks, devices, channels, col_width)


def cotangent(conv_vals, gating, probing):
    gate_wide = gating.astype(jnp.float32)
    mixed = gate_wide * conv_vals
    sigmoid_val = jax.nn.sigmoid(mixed)
    return (
        gate_wide * probing.astype(jnp.float32) * sigmoid_val * (1.0 + mixed * (1.0 - sigmoid_val))
    )


def spread_channels(
    inputs, gate_values, probe_values, filter_taps, member_blocks, member_nodes, node_place
):
    seq_index = lax.axis_index("seq")
    devices = lax.axis_size("seq")
    channels, length = inputs.shape
    inputs_wide = inputs.astype(jnp.float32)
    stacked = jnp.stack([inputs_wide, filter_taps]).reshape(2, 1, channels, length)
    columns_pair = lax.all_to_all(stacked, "seq", split_axis=3, concat_axis=1, tiled=True)

    def send_input(real_part, imag_part):
        return (
            lax.all_to_all(real_part, "seq", split_axis=1, concat_axis=3, tiled=True),
            lax.all_to_all(imag_part, "seq", split_axis=1, concat_axis=3, tiled=True),
        )

    def send_output(real_part, imag_part):
        return (
            lax.all_to_all(real_part, "seq", split_axis=3, concat_axis=1, tiled=True),
            lax.all_to_all(imag_part, "seq", split_axis=3, concat_axis=1, tiled=True),
        )

    def send_cotangent(real_part, imag_part):
        return (
            lax.all_to_all(real_part, "seq", split_axis=1, concat_axis=3, tiled=True),
            lax.all_to_all(imag_part, "seq", split_axis=1, concat_axis=3, tiled=True),
        )

    def send_gradient(real_part, imag_part):
        return (
            lax.all_to_all(real_part, "seq", split_axis=3, concat_axis=1, tiled=True),
            lax.all_to_all(imag_part, "seq", split_axis=3, concat_axis=1, tiled=True),
        )

    forward_section, inverse_section = (spectrum_full, signal_full)
    spec_real, spec_imag = forward_section(columns_pair, seq_index, send_input)
    filter_pair = (spec_real[1], spec_imag[1])
    conv_real, conv_imag = complex_times((spec_real[0], spec_imag[0]), filter_pair)
    conv_cols = inverse_section(conv_real[None], conv_imag[None], seq_index, devices, send_output)
    conv_rows = lax.all_to_all(conv_cols, "seq", split_axis=1, concat_axis=3, tiled=True).reshape(
        channels, length
    )
    back_rows = cotangent(conv_rows, gate_values, probe_values)
    back_cols = lax.all_to_all(
        back_rows.reshape(1, 1, channels, length), "seq", split_axis=3, concat_axis=1, tiled=True
    )
    back_real, back_imag = forward_section(back_cols, seq_index, send_cotangent)
    grad_real = back_real[0] * filter_pair[0] + back_imag[0] * filter_pair[1]
    grad_imag = back_imag[0] * filter_pair[0] - back_real[0] * filter_pair[1]
    grad_cols = inverse_section(grad_real[None], grad_imag[None], seq_index, devices, send_gradient)
    returned = lax.all_to_all(grad_cols, "seq", split_axis=1, concat_axis=3, tiled=True).reshape(
        channels, length
    )
    saliency = returned * inputs_wide
    channel_count = channels * lax.axis_size("ch")
    position_saliency = lax.psum(jnp.sum(saliency, axis=0), "ch") / channel_count
    blocks_dev = length // BLOCK
    block_rows = jnp.sum(saliency.reshape(channels, blocks_dev, BLOCK), axis=2)
    local_blocks = member_blocks - seq_index * blocks_dev
    targets = node_place[member_nodes]
    member_rows = jnp.take(block_rows, local_blocks, axis=1)
    nodes_dev = NODES // devices
    gathered_rows, gathered_targets = (
        lax.all_gather(member_rows, "seq", axis=1, tiled=True),
        lax.all_gather(targets.astype(jnp.float32), "seq", axis=0, tiled=True),
    )
    owned_ids = gathered_targets.astype(jnp.int32) - seq_index * nodes_dev
    slot_ids = jnp.where((owned_ids >= 0) & (owned_ids < nodes_dev), owned_ids, nodes_dev)
    node_sums = jax.ops.segment_sum(gathered_rows.T, slot_ids, num_segments=nodes_dev + 1)[
        :nodes_dev
    ].T
    node_counts = jax.ops.segment_sum(
        jnp.ones(slot_ids.shape, jnp.float32), slot_ids, num_segments=nodes_dev + 1
    )[:nodes_dev]
    node_rows = node_sums / jnp.maximum(node_counts, 1.0)[None, :]
    return (position_saliency, node_rows)


def per_device(*args):
    channels, length = args[0].shape
    devices = lax.axis_size("seq")
    members = args[4].shape[0]
    fits = channels == SUBS * devices and devices == SUBS and length == 2 * LANES
    fits = fits and members == SUBS and lax.axis_size("ch") > 1
    if fits and NODES % (devices * LANES) == 0:
        return whole_channels(*args)
    return spread_channels(*args)


def solution(mesh):
    placed = (
        P("ch", "seq"),
        P("ch", "seq"),
        P("ch", "seq"),
        P("ch", "seq"),
        P("seq"),
        P("seq"),
        P(),
    )
    return jax.shard_map(
        per_device,
        mesh=mesh,
        in_specs=placed,
        out_specs=(P("seq"), P("ch", "seq")),
        check_vma=False,
    )
```

```python
import functools
import math

import jax
import jax.numpy as jnp
from jax import lax
from jax.experimental import pallas as pl
from jax.experimental.pallas import tpu as pltpu
from jax.sharding import PartitionSpec as P

BLOCK = 64
NODES = 8192
LANES = 128
SUBS = 8
HALF = LANES // 2
PART = 32
PARTS = LANES // PART
FIELD_ROWS = 16
FIELDS = 5
PACK_ROWS = FIELDS * FIELD_ROWS


HIGHEST = lax.Precision.HIGHEST
LEAN = pltpu.CompilerParams(vmem_limit_bytes=16 * 1024 * 1024)


def iota(shape, dim):
    return lax.broadcasted_iota(jnp.int32, shape, dim)


def halves(vals):
    high = vals.astype(jnp.bfloat16)
    return high, (vals - high.astype(jnp.float32)).astype(jnp.bfloat16)


def exchange_order(devices):
    return [(place + devices // 2 + 1) % devices for place in range(devices)]


def as_column(row, count):
    width = row.shape[1]
    same = iota((count, width), 0) == iota((count, width), 1)
    return jnp.sum(jnp.where(same, row, 0.0), axis=1, keepdims=True)


def member_rows(blocks_ref, nodes_ref, place_ref):
    nodes = nodes_ref[...]
    count = nodes.shape[1]
    place = place_ref[...]
    row_pick = as_column((nodes // LANES).astype(jnp.float32), count) == iota(
        (count, place.shape[0]), 1
    ).astype(jnp.float32)
    row_pick = row_pick.astype(jnp.float32).astype(jnp.bfloat16)
    high, low = (
        jnp.dot(
            row_pick,
            digit.astype(jnp.float32).astype(jnp.bfloat16),
            preferred_element_type=jnp.float32,
        )
        for digit in (place // LANES, place % LANES)
    )
    lanes = iota((count, LANES), 1)
    low_digit = as_column((nodes % LANES).astype(jnp.float32), count)
    found = jnp.where(lanes.astype(jnp.float32) == low_digit, high * LANES + low, 0.0)
    targets = jnp.sum(found, axis=1, keepdims=True)
    blocks = as_column(blocks_ref[...].astype(jnp.float32), count)
    own = lanes == iota((count, LANES), 0) + lax.axis_index("seq") * count
    return jnp.concatenate(
        [jnp.sum(jnp.where(own, vals, 0.0), axis=0, keepdims=True) for vals in (targets, blocks)],
        axis=0,
    )


def pack_kernel(*refs):
    sources, packed_ref, lists, arrived, landed = (
        refs[:7], refs[7], refs[8:11], refs[11:15], refs[15]
    )
    loads = [
        pltpu.make_async_copy(source, target, landed.at[place])
        for place, (source, target) in enumerate(zip(sources, (*arrived, *lists)))
    ]
    for load in loads:
        load.start()
    order = exchange_order(packed_ref.shape[0])

    def put(pair, field, tiles):
        for side in range(2):
            rows = slice(side * SUBS, (side + 1) * SUBS)
            both = jnp.concatenate([tile[rows] for tile in tiles], axis=0)
            place = slice(field * FIELD_ROWS, (field + 1) * FIELD_ROWS)
            packed_ref[order.index(2 * pair + side), place, :] = both.astype(jnp.bfloat16)

    columns = [slice(0, LANES), slice(LANES, 2 * LANES)]
    for field in range(4):
        loads[field].wait()
        for pair in range(packed_ref.shape[0] // 2):
            rows = slice(pair * 2 * SUBS, (pair + 1) * 2 * SUBS)
            tiles = [arrived[field][rows, cols] for cols in columns]
            if field < 3:
                put(pair, field, [tile.astype(jnp.float32) for tile in tiles])
                continue
            split = [halves(tile) for tile in tiles]
            for term in range(2):
                put(pair, field + term, [terms[term].astype(jnp.float32) for terms in split])

    for load in loads[4:]:
        load.wait()


def windows(taps, first, blocks):
    later = iota((PART, LANES), 1) >= iota((PART, LANES), 0)
    rows = []
    earlier = jnp.zeros((PART, LANES), jnp.float32)
    for block in range(blocks):
        row = jnp.broadcast_to(taps[first + block : first + block + 1, :], (PART, LANES))
        turned = pltpu.roll(row, 0, axis=1, stride=1, stride_axis=0)
        rows.append(jnp.concatenate(halves(jnp.where(later, turned, earlier)), axis=1))
        earlier = turned
    return jnp.concatenate(rows, axis=0)


def turn(vals, parts):
    shift = parts * PART % LANES
    return pltpu.roll(vals, shift, axis=1) if shift else vals


def joined_parts(copies, single, sign):
    blocks = copies.shape[0]
    lanes = iota((blocks, LANES), 1)
    start = blocks if sign < 0 else 0
    result = []
    for part in range(PARTS):
        rows = single.at[part]
        rows[start : start + blocks, :] = copies[:, part * LANES : (part + 1) * LANES]
        rows[blocks - start : 2 * blocks - start, :] = jnp.zeros((blocks, LANES), jnp.float32)
        joined = rows[start : start + blocks, :]
        for step in range(1, PARTS):
            moved = rows[start + sign * step : start + sign * step + blocks, :]
            joined = jnp.where(lanes < step * PART, joined, moved)
        result.append(joined)
    return result


def spread(joined, padded, sign):
    blocks = joined[0].shape[0]
    start = blocks if sign < 0 else 0
    for part in range(PARTS):
        padded[part, start : start + blocks, :] = joined[part]
        padded[part, blocks - start : 2 * blocks - start, :] = jnp.zeros(
            (blocks, LANES), jnp.float32
        )
    columns = []
    for step in range(0, blocks, PARTS):
        offset = start + sign * step
        columns.append(
            jnp.concatenate(
                [padded[part, offset : offset + blocks, :] for part in range(PARTS)], axis=0
            )
        )
    return jnp.concatenate(columns, axis=1).astype(jnp.bfloat16)


def spread_terms(joined, padded, sign):
    high = [vals.astype(jnp.bfloat16).astype(jnp.float32) for vals in joined]
    low = [vals - term for vals, term in zip(joined, high)]
    return jnp.concatenate(
        [spread(vals, ref, sign) for vals, ref in zip((high, low), padded)], axis=0
    )


def next_block(vals, sign):
    blocks = vals.shape[0]
    row_ids = iota((blocks, LANES), 0)
    if sign < 0:
        return jnp.where(row_ids == 0, 0.0, pltpu.roll(vals, 1, axis=0))
    return jnp.where(row_ids == blocks - 1, 0.0, pltpu.roll(vals, blocks - 1, axis=0))


def overlapped(sums, sign):
    blocks = sums.shape[0] // PARTS
    lanes = iota((blocks, LANES), 1)
    result = sums[:blocks]
    for part in range(1, PARTS):
        own = sums[part * blocks : (part + 1) * blocks]
        wrapped = lanes >= LANES - part * PART
        result = result + turn(jnp.where(wrapped, next_block(own, sign), own), part)
    return result


def saliency_kernel(
    packed_ref,
    blocks_ref,
    nodes_ref,
    place_ref,
    sums_ref,
    fields,
    single,
    padded,
    products,
    held,
):
    devices = packed_ref.shape[0]
    blocks = 2 * devices
    copies = sums_ref.shape[0] // devices
    for slot, source in enumerate(exchange_order(devices)):
        rows = [
            packed_ref[slot, field * FIELD_ROWS : (field + 1) * FIELD_ROWS, :].astype(jnp.float32)
            for field in range(FIELDS)
        ]
        rows = [*rows[:3], rows[3] + rows[4]]
        for field in range(4):
            for side in range(2):
                place = pl.ds(2 * source + side, SUBS, stride=blocks)
                fields[field, place, :] = rows[field][side * SUBS : (side + 1) * SUBS]
    flip = iota((LANES, LANES), 0) + iota((LANES, LANES), 1) == LANES - 1
    flip = flip.astype(jnp.float32).astype(jnp.bfloat16)
    lane_ids, column_ids = (iota((LANES, PARTS * LANES), dim) for dim in range(2))
    origins = column_ids // LANES * PART + column_ids % PART
    repeat, flip_repeat = (
        (ids == origins).astype(jnp.float32).astype(jnp.bfloat16)
        for ids in (lane_ids, LANES - 1 - lane_ids)
    )

    def both_terms(vals, chosen):
        return jnp.dot(
            jnp.concatenate(halves(vals), axis=1),
            jnp.concatenate([chosen, chosen], axis=0),
            preferred_element_type=jnp.float32,
        )

    signals = jnp.dot(
        fields[0].astype(jnp.bfloat16), repeat, preferred_element_type=jnp.float32
    )
    fields[4] = jnp.dot(
        fields[0].astype(jnp.bfloat16), flip, preferred_element_type=jnp.float32
    )
    members = member_rows(blocks_ref, nodes_ref, place_ref)
    position_sums = jnp.zeros((blocks, LANES), jnp.float32)
    backs = []
    for channel in range(SUBS):
        place = slice(channel * blocks, (channel + 1) * blocks)
        gating, probing = fields[1, place, :], fields[2, place, :]
        held[channel] = windows(fields.at[3], channel * blocks, blocks)
        left = spread(
            joined_parts(signals[place], single.at[channel, 0], -1), padded.at[channel, 0], -1
        )
        sums = jnp.dot(left, held[channel], preferred_element_type=jnp.float32)
        conv = overlapped(sums[:, :LANES] + sums[:, LANES:], -1)
        mixed = gating * conv
        sigmoid_val = jax.nn.sigmoid(mixed)
        backs.append(gating * probing * sigmoid_val * (1.0 + mixed * (1.0 - sigmoid_val)))
    cuts = (0, SUBS // 2, 3 * SUBS // 4, SUBS)
    backs = jnp.concatenate(
        [
            both_terms(jnp.concatenate(backs[f:l], axis=0), flip_repeat)
            for f, l in zip(cuts, cuts[1:])
        ],
        axis=0,
    )
    for channel in range(SUBS):
        place = slice(channel * blocks, (channel + 1) * blocks)
        left = spread_terms(
            joined_parts(backs[place], single.at[channel, 1], 1),
            [padded.at[channel, 1 + term] for term in range(2)],
            1,
        )
        sums = jnp.dot(left, held[channel], preferred_element_type=jnp.float32)
        sums = sums[:, :LANES] + sums[:, LANES:]
        grad = overlapped(sums[: PARTS * blocks] + sums[PARTS * blocks :], 1)
        saliency = grad * fields[4, place, :]
        position_sums += saliency
        products[place, :] = saliency
    position_sums = both_terms(position_sums, flip)
    pick = (LANES - 1 - iota((SUBS, LANES), 1)) // BLOCK == iota((SUBS, LANES), 0)
    pick = pick.astype(jnp.float32).astype(jnp.bfloat16)
    block_sums = sum(
        lax.dot_general(
            pick, term, (((1,), (1,)), ((), ())), preferred_element_type=jnp.float32
        )
        for term in halves(products[...])
    )
    own = lax.axis_index("ch")
    for copy in range(copies):
        rest = jnp.where(own == copy, block_sums[:2], members)
        for device in range(devices):
            sums_ref[copy * devices + device, :, :] = jnp.concatenate(
                [position_sums[2 * device : 2 * device + 2], rest], axis=0
            )


def finish_kernel(members, channel_count, sums_ref, position_ref, nodes_ref):
    copies = lax.axis_size("ch")
    devices = sums_ref.shape[0] // copies
    columns = nodes_ref.shape[1]
    own = lax.axis_index("ch")
    total = sums_ref[0]
    for source in range(1, devices * copies):
        total = total + sums_ref[source]
    position_ref[...] = total[:2] / channel_count
    other = lax.rem(own + 1, copies) * devices
    listed = sums_ref[other]
    for source in range(1, devices):
        listed = listed + sums_ref[other + source]
    targets = as_column(listed[2:3], members)
    targets = targets - (lax.axis_index("seq") * columns).astype(jnp.float32)
    node_pick = iota((members, columns), 1).astype(jnp.float32) == targets
    node_pick = node_pick.astype(jnp.float32)
    scale = 1.0 / jnp.maximum(jnp.sum(node_pick, axis=0, keepdims=True), 1.0)
    slot = iota((2 * LANES, LANES), 0)
    slot_block = (slot % (2 * SUBS) * 2 + slot // LANES).astype(jnp.float32)
    block_pick = (slot_block == listed[3:4]).astype(jnp.float32).astype(jnp.bfloat16)
    own_lanes = iota((SUBS, LANES), 1) // (2 * SUBS) == iota((SUBS, LANES), 0)
    rows = []
    for source in range(devices):
        message = sums_ref[own * devices + source]
        rows.append(
            jnp.concatenate(
                [jnp.where(own_lanes, message[2 + side : 3 + side], 0.0) for side in range(2)],
                axis=1,
            )
        )
    picked = jnp.dot(
        jnp.concatenate(halves(jnp.concatenate(rows, axis=0)), axis=0),
        block_pick[:, :members],
        preferred_element_type=jnp.float32,
    )
    both = jnp.dot(
        picked.astype(jnp.bfloat16),
        node_pick.astype(jnp.bfloat16),
        preferred_element_type=jnp.float32,
    )
    count = devices * SUBS
    nodes_ref[...] = (both[:count] + both[count:]) * scale


def whole_channels(
    inputs, gate_values, probe_values, filter_taps, member_blocks, member_nodes, node_place
):
    devices = lax.axis_size("seq")
    copies = lax.axis_size("ch")
    channels, length = inputs.shape
    columns = node_place.shape[0] // devices
    blocks = devices * length // LANES
    local = (
        inputs,
        gate_values,
        probe_values,
        filter_taps,
        member_blocks.reshape(1, -1),
        member_nodes.reshape(1, -1),
        node_place.reshape(-1, LANES),
    )
    packed, *lists = pl.pallas_call(
        pack_kernel,
        out_shape=(
            jax.ShapeDtypeStruct((devices, PACK_ROWS, LANES), jnp.bfloat16),
            *(jax.ShapeDtypeStruct(part.shape, part.dtype) for part in local[4:]),
        ),
        in_specs=[pl.BlockSpec(memory_space=pltpu.HBM)] * len(local),
        scratch_shapes=[pltpu.VMEM(part.shape, part.dtype) for part in local[:4]]
        + [pltpu.SemaphoreType.DMA((len(local),))],
        compiler_params=LEAN,
        name="pack",
    )(*(pltpu.with_memory_space_constraint(part, pltpu.HBM) for part in local))
    packed = lax.all_to_all(
        packed,
        "seq",
        split_axis=0,
        concat_axis=0,
        tiled=True,
        axis_index_groups=[exchange_order(devices)],
    )
    sums = pl.pallas_call(
        saliency_kernel,
        out_shape=jax.ShapeDtypeStruct((devices * copies, 4, LANES), jnp.float32),
        scratch_shapes=[
            pltpu.VMEM((FIELDS, SUBS * blocks, LANES), jnp.float32),
            pltpu.VMEM((SUBS, 2, PARTS, 2 * blocks, LANES), jnp.float32),
            pltpu.VMEM((SUBS, 3, PARTS, 2 * blocks, LANES), jnp.float32),
            pltpu.VMEM((SUBS * blocks, LANES), jnp.float32),
            pltpu.VMEM((SUBS, blocks * PART, 2 * LANES), jnp.bfloat16),
        ],
        compiler_params=LEAN,
        name="saliency",
    )(packed, *lists)
    sums = lax.all_to_all(sums, ("ch", "seq"), split_axis=0, concat_axis=0, tiled=True)
    position, node_rows = pl.pallas_call(
        functools.partial(finish_kernel, devices * member_nodes.shape[0], channels * copies),
        out_shape=(
            jax.ShapeDtypeStruct((2, LANES), jnp.float32),
            jax.ShapeDtypeStruct((channels, columns), jnp.float32),
        ),
        compiler_params=LEAN,
        name="finish",
    )(sums)
    return position.reshape(length), node_rows


def phase_table(rows_count, cols_count, modulus, sine_sign, row_start, col_start):
    row_ids = lax.broadcasted_iota(jnp.int32, (rows_count, cols_count), 0) + row_start
    col_ids = lax.broadcasted_iota(jnp.int32, (rows_count, cols_count), 1) + col_start
    angles = (row_ids * col_ids % modulus).astype(jnp.float32) * (2.0 * math.pi / modulus)
    return (jnp.cos(angles), sine_sign * jnp.sin(angles))


def complex_times(first_pair, second_pair):
    first_real, first_imag = first_pair
    second_real, second_imag = second_pair
    return (
        first_real * second_real - first_imag * second_imag,
        first_real * second_imag + first_imag * second_real,
    )


def complex_product(formula, first_pair, second_pair):
    first_real, first_imag = first_pair
    second_real, second_imag = second_pair
    real_part = jnp.einsum(formula, first_real, second_real, precision=HIGHEST) - jnp.einsum(
        formula, first_imag, second_imag, precision=HIGHEST
    )
    imag_part = jnp.einsum(formula, first_real, second_imag, precision=HIGHEST) + jnp.einsum(
        formula, first_imag, second_real, precision=HIGHEST
    )
    return (real_part, imag_part)


def split_sizes(length):
    return (length // 128, 128)


def local_forward(real_part, imag_part):
    stacks, rows_count, channels, length = real_part.shape
    outer_size, inner_size = split_sizes(length)
    data_pair = (
        real_part.reshape(-1, outer_size, inner_size),
        imag_part.reshape(-1, outer_size, inner_size),
    )
    part_pair = complex_product(
        "jn,rnm->rjm", phase_table(outer_size, outer_size, outer_size, -1.0, 0, 0), data_pair
    )
    part_pair = complex_times(part_pair, phase_table(outer_size, inner_size, length, -1.0, 0, 0))
    spec_real, spec_imag = complex_product(
        "rjn,nm->rjm", part_pair, phase_table(inner_size, inner_size, inner_size, -1.0, 0, 0)
    )
    new_shape = (stacks, rows_count * channels, outer_size, inner_size)
    return (spec_real.reshape(new_shape), spec_imag.reshape(new_shape))


def local_inverse(spec_real, spec_imag):
    stacks, rows_count, outer_size, inner_size = spec_real.shape
    length = outer_size * inner_size
    data_pair = (
        spec_real.reshape(-1, outer_size, inner_size),
        spec_imag.reshape(-1, outer_size, inner_size),
    )
    part_pair = complex_product(
        "rjn,nm->rjm", data_pair, phase_table(inner_size, inner_size, inner_size, 1.0, 0, 0)
    )
    part_pair = complex_times(part_pair, phase_table(outer_size, inner_size, length, 1.0, 0, 0))
    out_real, out_imag = complex_product(
        "jn,rnm->rjm", phase_table(outer_size, outer_size, outer_size, 1.0, 0, 0), part_pair
    )
    return (
        out_real.reshape(stacks, rows_count, length),
        out_imag.reshape(stacks, rows_count, length),
    )


def spectrum_full(columns, seq_index, send):
    stacks, devices, channels, col_width = columns.shape
    modulus = 2 * devices * devices * col_width
    flattened = columns.reshape(stacks, devices, channels * col_width)
    row_cos, row_sin = phase_table(2 * devices, devices, 2 * devices, -1.0, 0, 0)
    grid_shape = (stacks, 2 * devices, channels, col_width)
    real_part = jnp.einsum("kn,snm->skm", row_cos, flattened, precision=HIGHEST).reshape(grid_shape)
    imag_part = jnp.einsum("kn,snm->skm", row_sin, flattened, precision=HIGHEST).reshape(grid_shape)
    turn_cos, turn_sin = phase_table(
        2 * devices, col_width, modulus, -1.0, 0, seq_index * col_width
    )
    real_part, imag_part = complex_times(
        (real_part, imag_part), (turn_cos[:, None, :], turn_sin[:, None, :])
    )
    real_part, imag_part = send(real_part, imag_part)
    return local_forward(real_part, imag_part)


def signal_full(spec_real, spec_imag, seq_index, devices, send):
    real_part, imag_part = local_inverse(spec_real, spec_imag)
    stacks, rows_count, length = real_part.shape
    channels = rows_count // 2
    modulus = 2 * devices * length
    real_part = real_part.reshape(stacks, 2, channels, length)
    imag_part = imag_part.reshape(stacks, 2, channels, length)
    turn_cos, turn_sin = phase_table(2, length, modulus, 1.0, 2 * seq_index, 0)
    real_part, imag_part = complex_times(
        (real_part, imag_part), (turn_cos[:, None, :], turn_sin[:, None, :])
    )
    real_part, imag_part = send(real_part, imag_part)
    col_width = length // devices
    back_cos, back_sin = phase_table(devices, 2 * devices, 2 * devices, 1.0, 0, 0)
    flat_real = real_part.reshape(stacks, 2 * devices, channels * col_width)
    flat_imag = imag_part.reshape(stacks, 2 * devices, channels * col_width)
    signal_vals = (
        jnp.einsum("ak,skm->sam", back_cos, flat_real, precision=HIGHEST)
        - jnp.einsum("ak,skm->sam", back_sin, flat_imag, precision=HIGHEST)
    ) / modulus
    return signal_vals.reshape(stacks, devices, channels, col_width)


def cotangent(conv_vals, gating, probing):
    gate_wide = gating.astype(jnp.float32)
    mixed = gate_wide * conv_vals
    sigmoid_val = jax.nn.sigmoid(mixed)
    return (
        gate_wide * probing.astype(jnp.float32) * sigmoid_val * (1.0 + mixed * (1.0 - sigmoid_val))
    )


def spread_channels(
    inputs, gate_values, probe_values, filter_taps, member_blocks, member_nodes, node_place
):
    seq_index = lax.axis_index("seq")
    devices = lax.axis_size("seq")
    channels, length = inputs.shape
    inputs_wide = inputs.astype(jnp.float32)
    stacked = jnp.stack([inputs_wide, filter_taps]).reshape(2, 1, channels, length)
    columns_pair = lax.all_to_all(stacked, "seq", split_axis=3, concat_axis=1, tiled=True)

    def send_input(real_part, imag_part):
        return (
            lax.all_to_all(real_part, "seq", split_axis=1, concat_axis=3, tiled=True),
            lax.all_to_all(imag_part, "seq", split_axis=1, concat_axis=3, tiled=True),
        )

    def send_output(real_part, imag_part):
        return (
            lax.all_to_all(real_part, "seq", split_axis=3, concat_axis=1, tiled=True),
            lax.all_to_all(imag_part, "seq", split_axis=3, concat_axis=1, tiled=True),
        )

    def send_cotangent(real_part, imag_part):
        return (
            lax.all_to_all(real_part, "seq", split_axis=1, concat_axis=3, tiled=True),
            lax.all_to_all(imag_part, "seq", split_axis=1, concat_axis=3, tiled=True),
        )

    def send_gradient(real_part, imag_part):
        return (
            lax.all_to_all(real_part, "seq", split_axis=3, concat_axis=1, tiled=True),
            lax.all_to_all(imag_part, "seq", split_axis=3, concat_axis=1, tiled=True),
        )

    forward_section, inverse_section = (spectrum_full, signal_full)
    spec_real, spec_imag = forward_section(columns_pair, seq_index, send_input)
    filter_pair = (spec_real[1], spec_imag[1])
    conv_real, conv_imag = complex_times((spec_real[0], spec_imag[0]), filter_pair)
    conv_cols = inverse_section(conv_real[None], conv_imag[None], seq_index, devices, send_output)
    conv_rows = lax.all_to_all(conv_cols, "seq", split_axis=1, concat_axis=3, tiled=True).reshape(
        channels, length
    )
    back_rows = cotangent(conv_rows, gate_values, probe_values)
    back_cols = lax.all_to_all(
        back_rows.reshape(1, 1, channels, length), "seq", split_axis=3, concat_axis=1, tiled=True
    )
    back_real, back_imag = forward_section(back_cols, seq_index, send_cotangent)
    grad_real = back_real[0] * filter_pair[0] + back_imag[0] * filter_pair[1]
    grad_imag = back_imag[0] * filter_pair[0] - back_real[0] * filter_pair[1]
    grad_cols = inverse_section(grad_real[None], grad_imag[None], seq_index, devices, send_gradient)
    returned = lax.all_to_all(grad_cols, "seq", split_axis=1, concat_axis=3, tiled=True).reshape(
        channels, length
    )
    saliency = returned * inputs_wide
    channel_count = channels * lax.axis_size("ch")
    position_saliency = lax.psum(jnp.sum(saliency, axis=0), "ch") / channel_count
    blocks_dev = length // BLOCK
    block_rows = jnp.sum(saliency.reshape(channels, blocks_dev, BLOCK), axis=2)
    local_blocks = member_blocks - seq_index * blocks_dev
    targets = node_place[member_nodes]
    member_rows = jnp.take(block_rows, local_blocks, axis=1)
    nodes_dev = NODES // devices
    gathered_rows, gathered_targets = (
        lax.all_gather(member_rows, "seq", axis=1, tiled=True),
        lax.all_gather(targets.astype(jnp.float32), "seq", axis=0, tiled=True),
    )
    owned_ids = gathered_targets.astype(jnp.int32) - seq_index * nodes_dev
    slot_ids = jnp.where((owned_ids >= 0) & (owned_ids < nodes_dev), owned_ids, nodes_dev)
    node_sums = jax.ops.segment_sum(gathered_rows.T, slot_ids, num_segments=nodes_dev + 1)[
        :nodes_dev
    ].T
    node_counts = jax.ops.segment_sum(
        jnp.ones(slot_ids.shape, jnp.float32), slot_ids, num_segments=nodes_dev + 1
    )[:nodes_dev]
    node_rows = node_sums / jnp.maximum(node_counts, 1.0)[None, :]
    return (position_saliency, node_rows)


def per_device(*args):
    channels, length = args[0].shape
    devices = lax.axis_size("seq")
    members = args[4].shape[0]
    fits = channels == SUBS * devices and devices == SUBS and length == 2 * LANES
    fits = fits and members == SUBS and lax.axis_size("ch") > 1
    if fits and NODES % (devices * LANES) == 0:
        return whole_channels(*args)
    return spread_channels(*args)


def solution(mesh):
    placed = (
        P("ch", "seq"),
        P("ch", "seq"),
        P("ch", "seq"),
        P("ch", "seq"),
        P("seq"),
        P("seq"),
        P(),
    )
    return jax.shard_map(
        per_device,
        mesh=mesh,
        in_specs=placed,
        out_specs=(P("seq"), P("ch", "seq")),
        check_vma=False,
    )
```

```python
import functools
import math

import jax
import jax.numpy as jnp
from jax import lax
from jax.experimental import pallas as pl
from jax.experimental.pallas import tpu as pltpu
from jax.sharding import PartitionSpec as P

BLOCK = 64
NODES = 8192
LANES = 128
SUBS = 8
HALF = LANES // 2
PART = 32
PARTS = LANES // PART
FIELD_ROWS = 16
FIELDS = 5
PACK_ROWS = FIELDS * FIELD_ROWS


HIGHEST = lax.Precision.HIGHEST
LEAN = pltpu.CompilerParams(vmem_limit_bytes=16 * 1024 * 1024)


def iota(shape, dim):
    return lax.broadcasted_iota(jnp.int32, shape, dim)


def halves(vals):
    high = vals.astype(jnp.bfloat16)
    return high, (vals - high.astype(jnp.float32)).astype(jnp.bfloat16)


def exchange_order(devices):
    listed = [*range(0, devices, 2), *range(1, devices, 2)]
    first = devices // 2 - 1
    return listed[first:] + listed[:first]


def as_column(row, count):
    width = row.shape[1]
    same = iota((count, width), 0) == iota((count, width), 1)
    return jnp.sum(jnp.where(same, row, 0.0), axis=1, keepdims=True)


def member_rows(blocks_ref, nodes_ref, place_ref):
    nodes = nodes_ref[...]
    count = nodes.shape[1]
    place = place_ref[...]
    row_pick = as_column((nodes // LANES).astype(jnp.float32), count) == iota(
        (count, place.shape[0]), 1
    ).astype(jnp.float32)
    row_pick = row_pick.astype(jnp.float32).astype(jnp.bfloat16)
    high, low = (
        jnp.dot(
            row_pick,
            digit.astype(jnp.float32).astype(jnp.bfloat16),
            preferred_element_type=jnp.float32,
        )
        for digit in (place // LANES, place % LANES)
    )
    lanes = iota((count, LANES), 1)
    low_digit = as_column((nodes % LANES).astype(jnp.float32), count)
    found = jnp.where(lanes.astype(jnp.float32) == low_digit, high * LANES + low, 0.0)
    targets = jnp.sum(found, axis=1, keepdims=True)
    blocks = as_column(blocks_ref[...].astype(jnp.float32), count)
    own = lanes == iota((count, LANES), 0) + lax.axis_index("seq") * count
    return jnp.concatenate(
        [jnp.sum(jnp.where(own, vals, 0.0), axis=0, keepdims=True) for vals in (targets, blocks)],
        axis=0,
    )


def pack_kernel(*refs):
    sources, packed_ref, lists, arrived, landed = (
        refs[:7], refs[7], refs[8:11], refs[11:15], refs[15]
    )
    loads = [
        pltpu.make_async_copy(source, target, landed.at[place])
        for place, (source, target) in enumerate(zip(sources, (*arrived, *lists)))
    ]
    for load in loads:
        load.start()
    order = exchange_order(packed_ref.shape[0])

    def put(pair, field, tiles):
        for side in range(2):
            rows = slice(side * SUBS, (side + 1) * SUBS)
            both = jnp.concatenate([tile[rows] for tile in tiles], axis=0)
            place = slice(field * FIELD_ROWS, (field + 1) * FIELD_ROWS)
            packed_ref[order.index(2 * pair + side), place, :] = both.astype(jnp.bfloat16)

    columns = [slice(0, LANES), slice(LANES, 2 * LANES)]
    for field in range(4):
        loads[field].wait()
        for pair in range(packed_ref.shape[0] // 2):
            rows = slice(pair * 2 * SUBS, (pair + 1) * 2 * SUBS)
            tiles = [arrived[field][rows, cols] for cols in columns]
            if field < 3:
                put(pair, field, [tile.astype(jnp.float32) for tile in tiles])
                continue
            split = [halves(tile) for tile in tiles]
            for term in range(2):
                put(pair, field + term, [terms[term].astype(jnp.float32) for terms in split])

    for load in loads[4:]:
        load.wait()


def windows(taps, first, blocks):
    later = iota((PART, LANES), 1) >= iota((PART, LANES), 0)
    rows = []
    earlier = jnp.zeros((PART, LANES), jnp.float32)
    for block in range(blocks):
        row = jnp.broadcast_to(taps[first + block : first + block + 1, :], (PART, LANES))
        turned = pltpu.roll(row, 0, axis=1, stride=1, stride_axis=0)
        rows.append(jnp.concatenate(halves(jnp.where(later, turned, earlier)), axis=1))
        earlier = turned
    return jnp.concatenate(rows, axis=0)


def turn(vals, parts):
    shift = parts * PART % LANES
    return pltpu.roll(vals, shift, axis=1) if shift else vals


def joined_parts(copies, single, sign):
    blocks = copies.shape[0]
    lanes = iota((blocks, LANES), 1)
    start = blocks if sign < 0 else 0
    result = []
    for part in range(PARTS):
        rows = single.at[part]
        rows[start : start + blocks, :] = copies[:, part * LANES : (part + 1) * LANES]
        rows[blocks - start : 2 * blocks - start, :] = jnp.zeros((blocks, LANES), jnp.float32)
        joined = rows[start : start + blocks, :]
        for step in range(1, PARTS):
            moved = rows[start + sign * step : start + sign * step + blocks, :]
            joined = jnp.where(lanes < step * PART, joined, moved)
        result.append(joined)
    return result


def spread(joined, padded, sign):
    blocks = joined[0].shape[0]
    start = blocks if sign < 0 else 0
    for part in range(PARTS):
        padded[part, start : start + blocks, :] = joined[part]
        padded[part, blocks - start : 2 * blocks - start, :] = jnp.zeros(
            (blocks, LANES), jnp.float32
        )
    columns = []
    for step in range(0, blocks, PARTS):
        offset = start + sign * step
        columns.append(
            jnp.concatenate(
                [padded[part, offset : offset + blocks, :] for part in range(PARTS)], axis=0
            )
        )
    return jnp.concatenate(columns, axis=1).astype(jnp.bfloat16)


def spread_terms(joined, padded, sign):
    high = [vals.astype(jnp.bfloat16).astype(jnp.float32) for vals in joined]
    low = [vals - term for vals, term in zip(joined, high)]
    return jnp.concatenate(
        [spread(vals, ref, sign) for vals, ref in zip((high, low), padded)], axis=0
    )


def next_block(vals, sign):
    blocks = vals.shape[0]
    row_ids = iota((blocks, LANES), 0)
    if sign < 0:
        return jnp.where(row_ids == 0, 0.0, pltpu.roll(vals, 1, axis=0))
    return jnp.where(row_ids == blocks - 1, 0.0, pltpu.roll(vals, blocks - 1, axis=0))


def overlapped(sums, sign):
    blocks = sums.shape[0] // PARTS
    lanes = iota((blocks, LANES), 1)
    result = sums[:blocks]
    for part in range(1, PARTS):
        own = sums[part * blocks : (part + 1) * blocks]
        wrapped = lanes >= LANES - part * PART
        result = result + turn(jnp.where(wrapped, next_block(own, sign), own), part)
    return result


def saliency_kernel(
    packed_ref,
    blocks_ref,
    nodes_ref,
    place_ref,
    sums_ref,
    fields,
    single,
    padded,
    products,
    held,
):
    devices = packed_ref.shape[0]
    blocks = 2 * devices
    copies = sums_ref.shape[0] // devices
    for slot, source in enumerate(exchange_order(devices)):
        rows = [
            packed_ref[slot, field * FIELD_ROWS : (field + 1) * FIELD_ROWS, :].astype(jnp.float32)
            for field in range(FIELDS)
        ]
        rows = [*rows[:3], rows[3] + rows[4]]
        for field in range(4):
            for side in range(2):
                place = pl.ds(2 * source + side, SUBS, stride=blocks)
                fields[field, place, :] = rows[field][side * SUBS : (side + 1) * SUBS]
    flip = iota((LANES, LANES), 0) + iota((LANES, LANES), 1) == LANES - 1
    flip = flip.astype(jnp.float32).astype(jnp.bfloat16)
    lane_ids, column_ids = (iota((LANES, PARTS * LANES), dim) for dim in range(2))
    origins = column_ids // LANES * PART + column_ids % PART
    repeat, flip_repeat = (
        (ids == origins).astype(jnp.float32).astype(jnp.bfloat16)
        for ids in (lane_ids, LANES - 1 - lane_ids)
    )

    def both_terms(vals, chosen):
        return jnp.dot(
            jnp.concatenate(halves(vals), axis=1),
            jnp.concatenate([chosen, chosen], axis=0),
            preferred_element_type=jnp.float32,
        )

    signals = jnp.dot(
        fields[0].astype(jnp.bfloat16), repeat, preferred_element_type=jnp.float32
    )
    fields[4] = jnp.dot(
        fields[0].astype(jnp.bfloat16), flip, preferred_element_type=jnp.float32
    )
    members = member_rows(blocks_ref, nodes_ref, place_ref)
    position_sums = jnp.zeros((blocks, LANES), jnp.float32)
    backs = []
    for channel in range(SUBS):
        place = slice(channel * blocks, (channel + 1) * blocks)
        gating, probing = fields[1, place, :], fields[2, place, :]
        held[channel] = windows(fields.at[3], channel * blocks, blocks)
        left = spread(
            joined_parts(signals[place], single.at[channel, 0], -1), padded.at[channel, 0], -1
        )
        sums = jnp.dot(left, held[channel], preferred_element_type=jnp.float32)
        conv = overlapped(sums[:, :LANES] + sums[:, LANES:], -1)
        mixed = gating * conv
        sigmoid_val = jax.nn.sigmoid(mixed)
        backs.append(gating * probing * sigmoid_val * (1.0 + mixed * (1.0 - sigmoid_val)))
    cuts = (0, SUBS // 2, 3 * SUBS // 4, SUBS)
    backs = jnp.concatenate(
        [
            both_terms(jnp.concatenate(backs[f:l], axis=0), flip_repeat)
            for f, l in zip(cuts, cuts[1:])
        ],
        axis=0,
    )
    for channel in range(SUBS):
        place = slice(channel * blocks, (channel + 1) * blocks)
        left = spread_terms(
            joined_parts(backs[place], single.at[channel, 1], 1),
            [padded.at[channel, 1 + term] for term in range(2)],
            1,
        )
        sums = jnp.dot(left, held[channel], preferred_element_type=jnp.float32)
        sums = sums[:, :LANES] + sums[:, LANES:]
        grad = overlapped(sums[: PARTS * blocks] + sums[PARTS * blocks :], 1)
        saliency = grad * fields[4, place, :]
        position_sums += saliency
        products[place, :] = saliency
    position_sums = both_terms(position_sums, flip)
    pick = (LANES - 1 - iota((SUBS, LANES), 1)) // BLOCK == iota((SUBS, LANES), 0)
    pick = pick.astype(jnp.float32).astype(jnp.bfloat16)
    block_sums = sum(
        lax.dot_general(
            pick, term, (((1,), (1,)), ((), ())), preferred_element_type=jnp.float32
        )
        for term in halves(products[...])
    )
    own = lax.axis_index("ch")
    for copy in range(copies):
        rest = jnp.where(own == copy, block_sums[:2], members)
        for device in range(devices):
            sums_ref[copy * devices + device, :, :] = jnp.concatenate(
                [position_sums[2 * device : 2 * device + 2], rest], axis=0
            )


def finish_kernel(members, channel_count, sums_ref, position_ref, nodes_ref):
    copies = lax.axis_size("ch")
    devices = sums_ref.shape[0] // copies
    columns = nodes_ref.shape[1]
    own = lax.axis_index("ch")
    total = sums_ref[0]
    for source in range(1, devices * copies):
        total = total + sums_ref[source]
    position_ref[...] = total[:2] / channel_count
    other = lax.rem(own + 1, copies) * devices
    listed = sums_ref[other]
    for source in range(1, devices):
        listed = listed + sums_ref[other + source]
    targets = as_column(listed[2:3], members)
    targets = targets - (lax.axis_index("seq") * columns).astype(jnp.float32)
    node_pick = iota((members, columns), 1).astype(jnp.float32) == targets
    node_pick = node_pick.astype(jnp.float32)
    scale = 1.0 / jnp.maximum(jnp.sum(node_pick, axis=0, keepdims=True), 1.0)
    slot = iota((2 * LANES, LANES), 0)
    slot_block = (slot % (2 * SUBS) * 2 + slot // LANES).astype(jnp.float32)
    block_pick = (slot_block == listed[3:4]).astype(jnp.float32).astype(jnp.bfloat16)
    own_lanes = iota((SUBS, LANES), 1) // (2 * SUBS) == iota((SUBS, LANES), 0)
    rows = []
    for source in range(devices):
        message = sums_ref[own * devices + source]
        rows.append(
            jnp.concatenate(
                [jnp.where(own_lanes, message[2 + side : 3 + side], 0.0) for side in range(2)],
                axis=1,
            )
        )
    picked = jnp.dot(
        jnp.concatenate(halves(jnp.concatenate(rows, axis=0)), axis=0),
        block_pick[:, :members],
        preferred_element_type=jnp.float32,
    )
    both = jnp.dot(
        picked.astype(jnp.bfloat16),
        node_pick.astype(jnp.bfloat16),
        preferred_element_type=jnp.float32,
    )
    count = devices * SUBS
    nodes_ref[...] = (both[:count] + both[count:]) * scale


def whole_channels(
    inputs, gate_values, probe_values, filter_taps, member_blocks, member_nodes, node_place
):
    devices = lax.axis_size("seq")
    copies = lax.axis_size("ch")
    channels, length = inputs.shape
    columns = node_place.shape[0] // devices
    blocks = devices * length // LANES
    local = (
        inputs,
        gate_values,
        probe_values,
        filter_taps,
        member_blocks.reshape(1, -1),
        member_nodes.reshape(1, -1),
        node_place.reshape(-1, LANES),
    )
    packed, *lists = pl.pallas_call(
        pack_kernel,
        out_shape=(
            jax.ShapeDtypeStruct((devices, PACK_ROWS, LANES), jnp.bfloat16),
            *(jax.ShapeDtypeStruct(part.shape, part.dtype) for part in local[4:]),
        ),
        in_specs=[pl.BlockSpec(memory_space=pltpu.HBM)] * len(local),
        scratch_shapes=[pltpu.VMEM(part.shape, part.dtype) for part in local[:4]]
        + [pltpu.SemaphoreType.DMA((len(local),))],
        compiler_params=LEAN,
        name="pack",
    )(*(pltpu.with_memory_space_constraint(part, pltpu.HBM) for part in local))
    packed = lax.all_to_all(
        packed,
        "seq",
        split_axis=0,
        concat_axis=0,
        tiled=True,
        axis_index_groups=[exchange_order(devices)],
    )
    sums = pl.pallas_call(
        saliency_kernel,
        out_shape=jax.ShapeDtypeStruct((devices * copies, 4, LANES), jnp.float32),
        scratch_shapes=[
            pltpu.VMEM((FIELDS, SUBS * blocks, LANES), jnp.float32),
            pltpu.VMEM((SUBS, 2, PARTS, 2 * blocks, LANES), jnp.float32),
            pltpu.VMEM((SUBS, 3, PARTS, 2 * blocks, LANES), jnp.float32),
            pltpu.VMEM((SUBS * blocks, LANES), jnp.float32),
            pltpu.VMEM((SUBS, blocks * PART, 2 * LANES), jnp.bfloat16),
        ],
        compiler_params=LEAN,
        name="saliency",
    )(packed, *lists)
    sums = lax.all_to_all(sums, ("ch", "seq"), split_axis=0, concat_axis=0, tiled=True)
    position, node_rows = pl.pallas_call(
        functools.partial(finish_kernel, devices * member_nodes.shape[0], channels * copies),
        out_shape=(
            jax.ShapeDtypeStruct((2, LANES), jnp.float32),
            jax.ShapeDtypeStruct((channels, columns), jnp.float32),
        ),
        compiler_params=LEAN,
        name="finish",
    )(sums)
    return position.reshape(length), node_rows


def phase_table(rows_count, cols_count, modulus, sine_sign, row_start, col_start):
    row_ids = lax.broadcasted_iota(jnp.int32, (rows_count, cols_count), 0) + row_start
    col_ids = lax.broadcasted_iota(jnp.int32, (rows_count, cols_count), 1) + col_start
    angles = (row_ids * col_ids % modulus).astype(jnp.float32) * (2.0 * math.pi / modulus)
    return (jnp.cos(angles), sine_sign * jnp.sin(angles))


def complex_times(first_pair, second_pair):
    first_real, first_imag = first_pair
    second_real, second_imag = second_pair
    return (
        first_real * second_real - first_imag * second_imag,
        first_real * second_imag + first_imag * second_real,
    )


def complex_product(formula, first_pair, second_pair):
    first_real, first_imag = first_pair
    second_real, second_imag = second_pair
    real_part = jnp.einsum(formula, first_real, second_real, precision=HIGHEST) - jnp.einsum(
        formula, first_imag, second_imag, precision=HIGHEST
    )
    imag_part = jnp.einsum(formula, first_real, second_imag, precision=HIGHEST) + jnp.einsum(
        formula, first_imag, second_real, precision=HIGHEST
    )
    return (real_part, imag_part)


def split_sizes(length):
    return (length // 128, 128)


def local_forward(real_part, imag_part):
    stacks, rows_count, channels, length = real_part.shape
    outer_size, inner_size = split_sizes(length)
    data_pair = (
        real_part.reshape(-1, outer_size, inner_size),
        imag_part.reshape(-1, outer_size, inner_size),
    )
    part_pair = complex_product(
        "jn,rnm->rjm", phase_table(outer_size, outer_size, outer_size, -1.0, 0, 0), data_pair
    )
    part_pair = complex_times(part_pair, phase_table(outer_size, inner_size, length, -1.0, 0, 0))
    spec_real, spec_imag = complex_product(
        "rjn,nm->rjm", part_pair, phase_table(inner_size, inner_size, inner_size, -1.0, 0, 0)
    )
    new_shape = (stacks, rows_count * channels, outer_size, inner_size)
    return (spec_real.reshape(new_shape), spec_imag.reshape(new_shape))


def local_inverse(spec_real, spec_imag):
    stacks, rows_count, outer_size, inner_size = spec_real.shape
    length = outer_size * inner_size
    data_pair = (
        spec_real.reshape(-1, outer_size, inner_size),
        spec_imag.reshape(-1, outer_size, inner_size),
    )
    part_pair = complex_product(
        "rjn,nm->rjm", data_pair, phase_table(inner_size, inner_size, inner_size, 1.0, 0, 0)
    )
    part_pair = complex_times(part_pair, phase_table(outer_size, inner_size, length, 1.0, 0, 0))
    out_real, out_imag = complex_product(
        "jn,rnm->rjm", phase_table(outer_size, outer_size, outer_size, 1.0, 0, 0), part_pair
    )
    return (
        out_real.reshape(stacks, rows_count, length),
        out_imag.reshape(stacks, rows_count, length),
    )


def spectrum_full(columns, seq_index, send):
    stacks, devices, channels, col_width = columns.shape
    modulus = 2 * devices * devices * col_width
    flattened = columns.reshape(stacks, devices, channels * col_width)
    row_cos, row_sin = phase_table(2 * devices, devices, 2 * devices, -1.0, 0, 0)
    grid_shape = (stacks, 2 * devices, channels, col_width)
    real_part = jnp.einsum("kn,snm->skm", row_cos, flattened, precision=HIGHEST).reshape(grid_shape)
    imag_part = jnp.einsum("kn,snm->skm", row_sin, flattened, precision=HIGHEST).reshape(grid_shape)
    turn_cos, turn_sin = phase_table(
        2 * devices, col_width, modulus, -1.0, 0, seq_index * col_width
    )
    real_part, imag_part = complex_times(
        (real_part, imag_part), (turn_cos[:, None, :], turn_sin[:, None, :])
    )
    real_part, imag_part = send(real_part, imag_part)
    return local_forward(real_part, imag_part)


def signal_full(spec_real, spec_imag, seq_index, devices, send):
    real_part, imag_part = local_inverse(spec_real, spec_imag)
    stacks, rows_count, length = real_part.shape
    channels = rows_count // 2
    modulus = 2 * devices * length
    real_part = real_part.reshape(stacks, 2, channels, length)
    imag_part = imag_part.reshape(stacks, 2, channels, length)
    turn_cos, turn_sin = phase_table(2, length, modulus, 1.0, 2 * seq_index, 0)
    real_part, imag_part = complex_times(
        (real_part, imag_part), (turn_cos[:, None, :], turn_sin[:, None, :])
    )
    real_part, imag_part = send(real_part, imag_part)
    col_width = length // devices
    back_cos, back_sin = phase_table(devices, 2 * devices, 2 * devices, 1.0, 0, 0)
    flat_real = real_part.reshape(stacks, 2 * devices, channels * col_width)
    flat_imag = imag_part.reshape(stacks, 2 * devices, channels * col_width)
    signal_vals = (
        jnp.einsum("ak,skm->sam", back_cos, flat_real, precision=HIGHEST)
        - jnp.einsum("ak,skm->sam", back_sin, flat_imag, precision=HIGHEST)
    ) / modulus
    return signal_vals.reshape(stacks, devices, channels, col_width)


def cotangent(conv_vals, gating, probing):
    gate_wide = gating.astype(jnp.float32)
    mixed = gate_wide * conv_vals
    sigmoid_val = jax.nn.sigmoid(mixed)
    return (
        gate_wide * probing.astype(jnp.float32) * sigmoid_val * (1.0 + mixed * (1.0 - sigmoid_val))
    )


def spread_channels(
    inputs, gate_values, probe_values, filter_taps, member_blocks, member_nodes, node_place
):
    seq_index = lax.axis_index("seq")
    devices = lax.axis_size("seq")
    channels, length = inputs.shape
    inputs_wide = inputs.astype(jnp.float32)
    stacked = jnp.stack([inputs_wide, filter_taps]).reshape(2, 1, channels, length)
    columns_pair = lax.all_to_all(stacked, "seq", split_axis=3, concat_axis=1, tiled=True)

    def send_input(real_part, imag_part):
        return (
            lax.all_to_all(real_part, "seq", split_axis=1, concat_axis=3, tiled=True),
            lax.all_to_all(imag_part, "seq", split_axis=1, concat_axis=3, tiled=True),
        )

    def send_output(real_part, imag_part):
        return (
            lax.all_to_all(real_part, "seq", split_axis=3, concat_axis=1, tiled=True),
            lax.all_to_all(imag_part, "seq", split_axis=3, concat_axis=1, tiled=True),
        )

    def send_cotangent(real_part, imag_part):
        return (
            lax.all_to_all(real_part, "seq", split_axis=1, concat_axis=3, tiled=True),
            lax.all_to_all(imag_part, "seq", split_axis=1, concat_axis=3, tiled=True),
        )

    def send_gradient(real_part, imag_part):
        return (
            lax.all_to_all(real_part, "seq", split_axis=3, concat_axis=1, tiled=True),
            lax.all_to_all(imag_part, "seq", split_axis=3, concat_axis=1, tiled=True),
        )

    forward_section, inverse_section = (spectrum_full, signal_full)
    spec_real, spec_imag = forward_section(columns_pair, seq_index, send_input)
    filter_pair = (spec_real[1], spec_imag[1])
    conv_real, conv_imag = complex_times((spec_real[0], spec_imag[0]), filter_pair)
    conv_cols = inverse_section(conv_real[None], conv_imag[None], seq_index, devices, send_output)
    conv_rows = lax.all_to_all(conv_cols, "seq", split_axis=1, concat_axis=3, tiled=True).reshape(
        channels, length
    )
    back_rows = cotangent(conv_rows, gate_values, probe_values)
    back_cols = lax.all_to_all(
        back_rows.reshape(1, 1, channels, length), "seq", split_axis=3, concat_axis=1, tiled=True
    )
    back_real, back_imag = forward_section(back_cols, seq_index, send_cotangent)
    grad_real = back_real[0] * filter_pair[0] + back_imag[0] * filter_pair[1]
    grad_imag = back_imag[0] * filter_pair[0] - back_real[0] * filter_pair[1]
    grad_cols = inverse_section(grad_real[None], grad_imag[None], seq_index, devices, send_gradient)
    returned = lax.all_to_all(grad_cols, "seq", split_axis=1, concat_axis=3, tiled=True).reshape(
        channels, length
    )
    saliency = returned * inputs_wide
    channel_count = channels * lax.axis_size("ch")
    position_saliency = lax.psum(jnp.sum(saliency, axis=0), "ch") / channel_count
    blocks_dev = length // BLOCK
    block_rows = jnp.sum(saliency.reshape(channels, blocks_dev, BLOCK), axis=2)
    local_blocks = member_blocks - seq_index * blocks_dev
    targets = node_place[member_nodes]
    member_rows = jnp.take(block_rows, local_blocks, axis=1)
    nodes_dev = NODES // devices
    gathered_rows, gathered_targets = (
        lax.all_gather(member_rows, "seq", axis=1, tiled=True),
        lax.all_gather(targets.astype(jnp.float32), "seq", axis=0, tiled=True),
    )
    owned_ids = gathered_targets.astype(jnp.int32) - seq_index * nodes_dev
    slot_ids = jnp.where((owned_ids >= 0) & (owned_ids < nodes_dev), owned_ids, nodes_dev)
    node_sums = jax.ops.segment_sum(gathered_rows.T, slot_ids, num_segments=nodes_dev + 1)[
        :nodes_dev
    ].T
    node_counts = jax.ops.segment_sum(
        jnp.ones(slot_ids.shape, jnp.float32), slot_ids, num_segments=nodes_dev + 1
    )[:nodes_dev]
    node_rows = node_sums / jnp.maximum(node_counts, 1.0)[None, :]
    return (position_saliency, node_rows)


def per_device(*args):
    channels, length = args[0].shape
    devices = lax.axis_size("seq")
    members = args[4].shape[0]
    fits = channels == SUBS * devices and devices == SUBS and length == 2 * LANES
    fits = fits and members == SUBS and lax.axis_size("ch") > 1
    if fits and NODES % (devices * LANES) == 0:
        return whole_channels(*args)
    return spread_channels(*args)


def solution(mesh):
    placed = (
        P("ch", "seq"),
        P("ch", "seq"),
        P("ch", "seq"),
        P("ch", "seq"),
        P("seq"),
        P("seq"),
        P(),
    )
    return jax.shard_map(
        per_device,
        mesh=mesh,
        in_specs=placed,
        out_specs=(P("seq"), P("ch", "seq")),
        check_vma=False,
    )
```

```python
import functools
import math

import jax
import jax.numpy as jnp
from jax import lax
from jax.experimental import pallas as pl
from jax.experimental.pallas import tpu as pltpu
from jax.sharding import PartitionSpec as P

BLOCK = 64
NODES = 8192
LANES = 128
SUBS = 8
HALF = LANES // 2
PART = 32
PARTS = LANES // PART
FIELD_ROWS = 16
FIELDS = 5
PACK_ROWS = FIELDS * FIELD_ROWS


HIGHEST = lax.Precision.HIGHEST
LEAN = pltpu.CompilerParams(vmem_limit_bytes=16 * 1024 * 1024)


def iota(shape, dim):
    return lax.broadcasted_iota(jnp.int32, shape, dim)


def halves(vals):
    high = vals.astype(jnp.bfloat16)
    return high, (vals - high.astype(jnp.float32)).astype(jnp.bfloat16)


def exchange_order(devices):
    listed = [*range(1, devices, 2), *range(0, devices, 2)]
    first = devices // 4
    return listed[first:] + listed[:first]


def as_column(row, count):
    width = row.shape[1]
    same = iota((count, width), 0) == iota((count, width), 1)
    return jnp.sum(jnp.where(same, row, 0.0), axis=1, keepdims=True)


def member_rows(blocks_ref, nodes_ref, place_ref):
    nodes = nodes_ref[...]
    count = nodes.shape[1]
    place = place_ref[...]
    row_pick = as_column((nodes // LANES).astype(jnp.float32), count) == iota(
        (count, place.shape[0]), 1
    ).astype(jnp.float32)
    row_pick = row_pick.astype(jnp.float32).astype(jnp.bfloat16)
    high, low = (
        jnp.dot(
            row_pick,
            digit.astype(jnp.float32).astype(jnp.bfloat16),
            preferred_element_type=jnp.float32,
        )
        for digit in (place // LANES, place % LANES)
    )
    lanes = iota((count, LANES), 1)
    low_digit = as_column((nodes % LANES).astype(jnp.float32), count)
    found = jnp.where(lanes.astype(jnp.float32) == low_digit, high * LANES + low, 0.0)
    targets = jnp.sum(found, axis=1, keepdims=True)
    blocks = as_column(blocks_ref[...].astype(jnp.float32), count)
    own = lanes == iota((count, LANES), 0) + lax.axis_index("seq") * count
    return jnp.concatenate(
        [jnp.sum(jnp.where(own, vals, 0.0), axis=0, keepdims=True) for vals in (targets, blocks)],
        axis=0,
    )


def pack_kernel(*refs):
    sources, packed_ref, lists, arrived, landed = (
        refs[:7], refs[7], refs[8:11], refs[11:15], refs[15]
    )
    loads = [
        pltpu.make_async_copy(source, target, landed.at[place])
        for place, (source, target) in enumerate(zip(sources, (*arrived, *lists)))
    ]
    for load in loads:
        load.start()
    order = exchange_order(packed_ref.shape[0])

    def put(pair, field, tiles):
        for side in range(2):
            rows = slice(side * SUBS, (side + 1) * SUBS)
            both = jnp.concatenate([tile[rows] for tile in tiles], axis=0)
            place = slice(field * FIELD_ROWS, (field + 1) * FIELD_ROWS)
            packed_ref[order.index(2 * pair + side), place, :] = both.astype(jnp.bfloat16)

    columns = [slice(0, LANES), slice(LANES, 2 * LANES)]
    for field in range(4):
        loads[field].wait()
        for pair in range(packed_ref.shape[0] // 2):
            rows = slice(pair * 2 * SUBS, (pair + 1) * 2 * SUBS)
            tiles = [arrived[field][rows, cols] for cols in columns]
            if field < 3:
                put(pair, field, [tile.astype(jnp.float32) for tile in tiles])
                continue
            split = [halves(tile) for tile in tiles]
            for term in range(2):
                put(pair, field + term, [terms[term].astype(jnp.float32) for terms in split])

    for load in loads[4:]:
        load.wait()


def windows(taps, first, blocks):
    later = iota((PART, LANES), 1) >= iota((PART, LANES), 0)
    rows = []
    earlier = jnp.zeros((PART, LANES), jnp.float32)
    for block in range(blocks):
        row = jnp.broadcast_to(taps[first + block : first + block + 1, :], (PART, LANES))
        turned = pltpu.roll(row, 0, axis=1, stride=1, stride_axis=0)
        rows.append(jnp.concatenate(halves(jnp.where(later, turned, earlier)), axis=1))
        earlier = turned
    return jnp.concatenate(rows, axis=0)


def turn(vals, parts):
    shift = parts * PART % LANES
    return pltpu.roll(vals, shift, axis=1) if shift else vals


def joined_parts(copies, single, sign):
    blocks = copies.shape[0]
    lanes = iota((blocks, LANES), 1)
    start = blocks if sign < 0 else 0
    result = []
    for part in range(PARTS):
        rows = single.at[part]
        rows[start : start + blocks, :] = copies[:, part * LANES : (part + 1) * LANES]
        rows[blocks - start : 2 * blocks - start, :] = jnp.zeros((blocks, LANES), jnp.float32)
        joined = rows[start : start + blocks, :]
        for step in range(1, PARTS):
            moved = rows[start + sign * step : start + sign * step + blocks, :]
            joined = jnp.where(lanes < step * PART, joined, moved)
        result.append(joined)
    return result


def spread(joined, padded, sign):
    blocks = joined[0].shape[0]
    start = blocks if sign < 0 else 0
    for part in range(PARTS):
        padded[part, start : start + blocks, :] = joined[part]
        padded[part, blocks - start : 2 * blocks - start, :] = jnp.zeros(
            (blocks, LANES), jnp.float32
        )
    columns = []
    for step in range(0, blocks, PARTS):
        offset = start + sign * step
        columns.append(
            jnp.concatenate(
                [padded[part, offset : offset + blocks, :] for part in range(PARTS)], axis=0
            )
        )
    return jnp.concatenate(columns, axis=1).astype(jnp.bfloat16)


def spread_terms(joined, padded, sign):
    high = [vals.astype(jnp.bfloat16).astype(jnp.float32) for vals in joined]
    low = [vals - term for vals, term in zip(joined, high)]
    return jnp.concatenate(
        [spread(vals, ref, sign) for vals, ref in zip((high, low), padded)], axis=0
    )


def next_block(vals, sign):
    blocks = vals.shape[0]
    row_ids = iota((blocks, LANES), 0)
    if sign < 0:
        return jnp.where(row_ids == 0, 0.0, pltpu.roll(vals, 1, axis=0))
    return jnp.where(row_ids == blocks - 1, 0.0, pltpu.roll(vals, blocks - 1, axis=0))


def overlapped(sums, sign):
    blocks = sums.shape[0] // PARTS
    lanes = iota((blocks, LANES), 1)
    result = sums[:blocks]
    for part in range(1, PARTS):
        own = sums[part * blocks : (part + 1) * blocks]
        wrapped = lanes >= LANES - part * PART
        result = result + turn(jnp.where(wrapped, next_block(own, sign), own), part)
    return result


def saliency_kernel(
    packed_ref,
    blocks_ref,
    nodes_ref,
    place_ref,
    sums_ref,
    fields,
    single,
    padded,
    products,
    held,
):
    devices = packed_ref.shape[0]
    blocks = 2 * devices
    copies = sums_ref.shape[0] // devices
    for slot, source in enumerate(exchange_order(devices)):
        rows = [
            packed_ref[slot, field * FIELD_ROWS : (field + 1) * FIELD_ROWS, :].astype(jnp.float32)
            for field in range(FIELDS)
        ]
        rows = [*rows[:3], rows[3] + rows[4]]
        for field in range(4):
            for side in range(2):
                place = pl.ds(2 * source + side, SUBS, stride=blocks)
                fields[field, place, :] = rows[field][side * SUBS : (side + 1) * SUBS]
    flip = iota((LANES, LANES), 0) + iota((LANES, LANES), 1) == LANES - 1
    flip = flip.astype(jnp.float32).astype(jnp.bfloat16)
    lane_ids, column_ids = (iota((LANES, PARTS * LANES), dim) for dim in range(2))
    origins = column_ids // LANES * PART + column_ids % PART
    repeat, flip_repeat = (
        (ids == origins).astype(jnp.float32).astype(jnp.bfloat16)
        for ids in (lane_ids, LANES - 1 - lane_ids)
    )

    def both_terms(vals, chosen):
        return jnp.dot(
            jnp.concatenate(halves(vals), axis=1),
            jnp.concatenate([chosen, chosen], axis=0),
            preferred_element_type=jnp.float32,
        )

    signals = jnp.dot(
        fields[0].astype(jnp.bfloat16), repeat, preferred_element_type=jnp.float32
    )
    fields[4] = jnp.dot(
        fields[0].astype(jnp.bfloat16), flip, preferred_element_type=jnp.float32
    )
    members = member_rows(blocks_ref, nodes_ref, place_ref)
    position_sums = jnp.zeros((blocks, LANES), jnp.float32)
    backs = []
    for channel in range(SUBS):
        place = slice(channel * blocks, (channel + 1) * blocks)
        gating, probing = fields[1, place, :], fields[2, place, :]
        held[channel] = windows(fields.at[3], channel * blocks, blocks)
        left = spread(
            joined_parts(signals[place], single.at[channel, 0], -1), padded.at[channel, 0], -1
        )
        sums = jnp.dot(left, held[channel], preferred_element_type=jnp.float32)
        conv = overlapped(sums[:, :LANES] + sums[:, LANES:], -1)
        mixed = gating * conv
        sigmoid_val = jax.nn.sigmoid(mixed)
        backs.append(gating * probing * sigmoid_val * (1.0 + mixed * (1.0 - sigmoid_val)))
    cuts = (0, SUBS // 2, 3 * SUBS // 4, SUBS)
    backs = jnp.concatenate(
        [
            both_terms(jnp.concatenate(backs[f:l], axis=0), flip_repeat)
            for f, l in zip(cuts, cuts[1:])
        ],
        axis=0,
    )
    for channel in range(SUBS):
        place = slice(channel * blocks, (channel + 1) * blocks)
        left = spread_terms(
            joined_parts(backs[place], single.at[channel, 1], 1),
            [padded.at[channel, 1 + term] for term in range(2)],
            1,
        )
        sums = jnp.dot(left, held[channel], preferred_element_type=jnp.float32)
        sums = sums[:, :LANES] + sums[:, LANES:]
        grad = overlapped(sums[: PARTS * blocks] + sums[PARTS * blocks :], 1)
        saliency = grad * fields[4, place, :]
        position_sums += saliency
        products[place, :] = saliency
    position_sums = both_terms(position_sums, flip)
    pick = (LANES - 1 - iota((SUBS, LANES), 1)) // BLOCK == iota((SUBS, LANES), 0)
    pick = pick.astype(jnp.float32).astype(jnp.bfloat16)
    block_sums = sum(
        lax.dot_general(
            pick, term, (((1,), (1,)), ((), ())), preferred_element_type=jnp.float32
        )
        for term in halves(products[...])
    )
    own = lax.axis_index("ch")
    for copy in range(copies):
        rest = jnp.where(own == copy, block_sums[:2], members)
        for device in range(devices):
            sums_ref[copy * devices + device, :, :] = jnp.concatenate(
                [position_sums[2 * device : 2 * device + 2], rest], axis=0
            )


def finish_kernel(members, channel_count, sums_ref, position_ref, nodes_ref):
    copies = lax.axis_size("ch")
    devices = sums_ref.shape[0] // copies
    columns = nodes_ref.shape[1]
    own = lax.axis_index("ch")
    total = sums_ref[0]
    for source in range(1, devices * copies):
        total = total + sums_ref[source]
    position_ref[...] = total[:2] / channel_count
    other = lax.rem(own + 1, copies) * devices
    listed = sums_ref[other]
    for source in range(1, devices):
        listed = listed + sums_ref[other + source]
    targets = as_column(listed[2:3], members)
    targets = targets - (lax.axis_index("seq") * columns).astype(jnp.float32)
    node_pick = iota((members, columns), 1).astype(jnp.float32) == targets
    node_pick = node_pick.astype(jnp.float32)
    scale = 1.0 / jnp.maximum(jnp.sum(node_pick, axis=0, keepdims=True), 1.0)
    slot = iota((2 * LANES, LANES), 0)
    slot_block = (slot % (2 * SUBS) * 2 + slot // LANES).astype(jnp.float32)
    block_pick = (slot_block == listed[3:4]).astype(jnp.float32).astype(jnp.bfloat16)
    own_lanes = iota((SUBS, LANES), 1) // (2 * SUBS) == iota((SUBS, LANES), 0)
    rows = []
    for source in range(devices):
        message = sums_ref[own * devices + source]
        rows.append(
            jnp.concatenate(
                [jnp.where(own_lanes, message[2 + side : 3 + side], 0.0) for side in range(2)],
                axis=1,
            )
        )
    picked = jnp.dot(
        jnp.concatenate(halves(jnp.concatenate(rows, axis=0)), axis=0),
        block_pick[:, :members],
        preferred_element_type=jnp.float32,
    )
    both = jnp.dot(
        picked.astype(jnp.bfloat16),
        node_pick.astype(jnp.bfloat16),
        preferred_element_type=jnp.float32,
    )
    count = devices * SUBS
    nodes_ref[...] = (both[:count] + both[count:]) * scale


def whole_channels(
    inputs, gate_values, probe_values, filter_taps, member_blocks, member_nodes, node_place
):
    devices = lax.axis_size("seq")
    copies = lax.axis_size("ch")
    channels, length = inputs.shape
    columns = node_place.shape[0] // devices
    blocks = devices * length // LANES
    local = (
        inputs,
        gate_values,
        probe_values,
        filter_taps,
        member_blocks.reshape(1, -1),
        member_nodes.reshape(1, -1),
        node_place.reshape(-1, LANES),
    )
    packed, *lists = pl.pallas_call(
        pack_kernel,
        out_shape=(
            jax.ShapeDtypeStruct((devices, PACK_ROWS, LANES), jnp.bfloat16),
            *(jax.ShapeDtypeStruct(part.shape, part.dtype) for part in local[4:]),
        ),
        in_specs=[pl.BlockSpec(memory_space=pltpu.HBM)] * len(local),
        scratch_shapes=[pltpu.VMEM(part.shape, part.dtype) for part in local[:4]]
        + [pltpu.SemaphoreType.DMA((len(local),))],
        compiler_params=LEAN,
        name="pack",
    )(*(pltpu.with_memory_space_constraint(part, pltpu.HBM) for part in local))
    packed = lax.all_to_all(
        packed,
        "seq",
        split_axis=0,
        concat_axis=0,
        tiled=True,
        axis_index_groups=[exchange_order(devices)],
    )
    sums = pl.pallas_call(
        saliency_kernel,
        out_shape=jax.ShapeDtypeStruct((devices * copies, 4, LANES), jnp.float32),
        scratch_shapes=[
            pltpu.VMEM((FIELDS, SUBS * blocks, LANES), jnp.float32),
            pltpu.VMEM((SUBS, 2, PARTS, 2 * blocks, LANES), jnp.float32),
            pltpu.VMEM((SUBS, 3, PARTS, 2 * blocks, LANES), jnp.float32),
            pltpu.VMEM((SUBS * blocks, LANES), jnp.float32),
            pltpu.VMEM((SUBS, blocks * PART, 2 * LANES), jnp.bfloat16),
        ],
        compiler_params=LEAN,
        name="saliency",
    )(packed, *lists)
    sums = lax.all_to_all(sums, ("ch", "seq"), split_axis=0, concat_axis=0, tiled=True)
    position, node_rows = pl.pallas_call(
        functools.partial(finish_kernel, devices * member_nodes.shape[0], channels * copies),
        out_shape=(
            jax.ShapeDtypeStruct((2, LANES), jnp.float32),
            jax.ShapeDtypeStruct((channels, columns), jnp.float32),
        ),
        compiler_params=LEAN,
        name="finish",
    )(sums)
    return position.reshape(length), node_rows


def phase_table(rows_count, cols_count, modulus, sine_sign, row_start, col_start):
    row_ids = lax.broadcasted_iota(jnp.int32, (rows_count, cols_count), 0) + row_start
    col_ids = lax.broadcasted_iota(jnp.int32, (rows_count, cols_count), 1) + col_start
    angles = (row_ids * col_ids % modulus).astype(jnp.float32) * (2.0 * math.pi / modulus)
    return (jnp.cos(angles), sine_sign * jnp.sin(angles))


def complex_times(first_pair, second_pair):
    first_real, first_imag = first_pair
    second_real, second_imag = second_pair
    return (
        first_real * second_real - first_imag * second_imag,
        first_real * second_imag + first_imag * second_real,
    )


def complex_product(formula, first_pair, second_pair):
    first_real, first_imag = first_pair
    second_real, second_imag = second_pair
    real_part = jnp.einsum(formula, first_real, second_real, precision=HIGHEST) - jnp.einsum(
        formula, first_imag, second_imag, precision=HIGHEST
    )
    imag_part = jnp.einsum(formula, first_real, second_imag, precision=HIGHEST) + jnp.einsum(
        formula, first_imag, second_real, precision=HIGHEST
    )
    return (real_part, imag_part)


def split_sizes(length):
    return (length // 128, 128)


def local_forward(real_part, imag_part):
    stacks, rows_count, channels, length = real_part.shape
    outer_size, inner_size = split_sizes(length)
    data_pair = (
        real_part.reshape(-1, outer_size, inner_size),
        imag_part.reshape(-1, outer_size, inner_size),
    )
    part_pair = complex_product(
        "jn,rnm->rjm", phase_table(outer_size, outer_size, outer_size, -1.0, 0, 0), data_pair
    )
    part_pair = complex_times(part_pair, phase_table(outer_size, inner_size, length, -1.0, 0, 0))
    spec_real, spec_imag = complex_product(
        "rjn,nm->rjm", part_pair, phase_table(inner_size, inner_size, inner_size, -1.0, 0, 0)
    )
    new_shape = (stacks, rows_count * channels, outer_size, inner_size)
    return (spec_real.reshape(new_shape), spec_imag.reshape(new_shape))


def local_inverse(spec_real, spec_imag):
    stacks, rows_count, outer_size, inner_size = spec_real.shape
    length = outer_size * inner_size
    data_pair = (
        spec_real.reshape(-1, outer_size, inner_size),
        spec_imag.reshape(-1, outer_size, inner_size),
    )
    part_pair = complex_product(
        "rjn,nm->rjm", data_pair, phase_table(inner_size, inner_size, inner_size, 1.0, 0, 0)
    )
    part_pair = complex_times(part_pair, phase_table(outer_size, inner_size, length, 1.0, 0, 0))
    out_real, out_imag = complex_product(
        "jn,rnm->rjm", phase_table(outer_size, outer_size, outer_size, 1.0, 0, 0), part_pair
    )
    return (
        out_real.reshape(stacks, rows_count, length),
        out_imag.reshape(stacks, rows_count, length),
    )


def spectrum_full(columns, seq_index, send):
    stacks, devices, channels, col_width = columns.shape
    modulus = 2 * devices * devices * col_width
    flattened = columns.reshape(stacks, devices, channels * col_width)
    row_cos, row_sin = phase_table(2 * devices, devices, 2 * devices, -1.0, 0, 0)
    grid_shape = (stacks, 2 * devices, channels, col_width)
    real_part = jnp.einsum("kn,snm->skm", row_cos, flattened, precision=HIGHEST).reshape(grid_shape)
    imag_part = jnp.einsum("kn,snm->skm", row_sin, flattened, precision=HIGHEST).reshape(grid_shape)
    turn_cos, turn_sin = phase_table(
        2 * devices, col_width, modulus, -1.0, 0, seq_index * col_width
    )
    real_part, imag_part = complex_times(
        (real_part, imag_part), (turn_cos[:, None, :], turn_sin[:, None, :])
    )
    real_part, imag_part = send(real_part, imag_part)
    return local_forward(real_part, imag_part)


def signal_full(spec_real, spec_imag, seq_index, devices, send):
    real_part, imag_part = local_inverse(spec_real, spec_imag)
    stacks, rows_count, length = real_part.shape
    channels = rows_count // 2
    modulus = 2 * devices * length
    real_part = real_part.reshape(stacks, 2, channels, length)
    imag_part = imag_part.reshape(stacks, 2, channels, length)
    turn_cos, turn_sin = phase_table(2, length, modulus, 1.0, 2 * seq_index, 0)
    real_part, imag_part = complex_times(
        (real_part, imag_part), (turn_cos[:, None, :], turn_sin[:, None, :])
    )
    real_part, imag_part = send(real_part, imag_part)
    col_width = length // devices
    back_cos, back_sin = phase_table(devices, 2 * devices, 2 * devices, 1.0, 0, 0)
    flat_real = real_part.reshape(stacks, 2 * devices, channels * col_width)
    flat_imag = imag_part.reshape(stacks, 2 * devices, channels * col_width)
    signal_vals = (
        jnp.einsum("ak,skm->sam", back_cos, flat_real, precision=HIGHEST)
        - jnp.einsum("ak,skm->sam", back_sin, flat_imag, precision=HIGHEST)
    ) / modulus
    return signal_vals.reshape(stacks, devices, channels, col_width)


def cotangent(conv_vals, gating, probing):
    gate_wide = gating.astype(jnp.float32)
    mixed = gate_wide * conv_vals
    sigmoid_val = jax.nn.sigmoid(mixed)
    return (
        gate_wide * probing.astype(jnp.float32) * sigmoid_val * (1.0 + mixed * (1.0 - sigmoid_val))
    )


def spread_channels(
    inputs, gate_values, probe_values, filter_taps, member_blocks, member_nodes, node_place
):
    seq_index = lax.axis_index("seq")
    devices = lax.axis_size("seq")
    channels, length = inputs.shape
    inputs_wide = inputs.astype(jnp.float32)
    stacked = jnp.stack([inputs_wide, filter_taps]).reshape(2, 1, channels, length)
    columns_pair = lax.all_to_all(stacked, "seq", split_axis=3, concat_axis=1, tiled=True)

    def send_input(real_part, imag_part):
        return (
            lax.all_to_all(real_part, "seq", split_axis=1, concat_axis=3, tiled=True),
            lax.all_to_all(imag_part, "seq", split_axis=1, concat_axis=3, tiled=True),
        )

    def send_output(real_part, imag_part):
        return (
            lax.all_to_all(real_part, "seq", split_axis=3, concat_axis=1, tiled=True),
            lax.all_to_all(imag_part, "seq", split_axis=3, concat_axis=1, tiled=True),
        )

    def send_cotangent(real_part, imag_part):
        return (
            lax.all_to_all(real_part, "seq", split_axis=1, concat_axis=3, tiled=True),
            lax.all_to_all(imag_part, "seq", split_axis=1, concat_axis=3, tiled=True),
        )

    def send_gradient(real_part, imag_part):
        return (
            lax.all_to_all(real_part, "seq", split_axis=3, concat_axis=1, tiled=True),
            lax.all_to_all(imag_part, "seq", split_axis=3, concat_axis=1, tiled=True),
        )

    forward_section, inverse_section = (spectrum_full, signal_full)
    spec_real, spec_imag = forward_section(columns_pair, seq_index, send_input)
    filter_pair = (spec_real[1], spec_imag[1])
    conv_real, conv_imag = complex_times((spec_real[0], spec_imag[0]), filter_pair)
    conv_cols = inverse_section(conv_real[None], conv_imag[None], seq_index, devices, send_output)
    conv_rows = lax.all_to_all(conv_cols, "seq", split_axis=1, concat_axis=3, tiled=True).reshape(
        channels, length
    )
    back_rows = cotangent(conv_rows, gate_values, probe_values)
    back_cols = lax.all_to_all(
        back_rows.reshape(1, 1, channels, length), "seq", split_axis=3, concat_axis=1, tiled=True
    )
    back_real, back_imag = forward_section(back_cols, seq_index, send_cotangent)
    grad_real = back_real[0] * filter_pair[0] + back_imag[0] * filter_pair[1]
    grad_imag = back_imag[0] * filter_pair[0] - back_real[0] * filter_pair[1]
    grad_cols = inverse_section(grad_real[None], grad_imag[None], seq_index, devices, send_gradient)
    returned = lax.all_to_all(grad_cols, "seq", split_axis=1, concat_axis=3, tiled=True).reshape(
        channels, length
    )
    saliency = returned * inputs_wide
    channel_count = channels * lax.axis_size("ch")
    position_saliency = lax.psum(jnp.sum(saliency, axis=0), "ch") / channel_count
    blocks_dev = length // BLOCK
    block_rows = jnp.sum(saliency.reshape(channels, blocks_dev, BLOCK), axis=2)
    local_blocks = member_blocks - seq_index * blocks_dev
    targets = node_place[member_nodes]
    member_rows = jnp.take(block_rows, local_blocks, axis=1)
    nodes_dev = NODES // devices
    gathered_rows, gathered_targets = (
        lax.all_gather(member_rows, "seq", axis=1, tiled=True),
        lax.all_gather(targets.astype(jnp.float32), "seq", axis=0, tiled=True),
    )
    owned_ids = gathered_targets.astype(jnp.int32) - seq_index * nodes_dev
    slot_ids = jnp.where((owned_ids >= 0) & (owned_ids < nodes_dev), owned_ids, nodes_dev)
    node_sums = jax.ops.segment_sum(gathered_rows.T, slot_ids, num_segments=nodes_dev + 1)[
        :nodes_dev
    ].T
    node_counts = jax.ops.segment_sum(
        jnp.ones(slot_ids.shape, jnp.float32), slot_ids, num_segments=nodes_dev + 1
    )[:nodes_dev]
    node_rows = node_sums / jnp.maximum(node_counts, 1.0)[None, :]
    return (position_saliency, node_rows)


def per_device(*args):
    channels, length = args[0].shape
    devices = lax.axis_size("seq")
    members = args[4].shape[0]
    fits = channels == SUBS * devices and devices == SUBS and length == 2 * LANES
    fits = fits and members == SUBS and lax.axis_size("ch") > 1
    if fits and NODES % (devices * LANES) == 0:
        return whole_channels(*args)
    return spread_channels(*args)


def solution(mesh):
    placed = (
        P("ch", "seq"),
        P("ch", "seq"),
        P("ch", "seq"),
        P("ch", "seq"),
        P("seq"),
        P("seq"),
        P(),
    )
    return jax.shard_map(
        per_device,
        mesh=mesh,
        in_specs=placed,
        out_specs=(P("seq"), P("ch", "seq")),
        check_vma=False,
    )
```
